256 devices in a mesh: ctx: 32 (over x, y, z_lo), exp: 8 (over z_hi, core).
Axes of the slice: x: 4, y: 4, z: 8 (z_hi: 4, z_lo: 2; z = z_hi * 2 + z_lo), core: 2. Of those that a mesh axis runs over, the one named last changes fastest.
Arguments:
- queries: bfloat16 [4, 8192, 2048], P(None, 'ctx', 'exp'), may hold values from -12 to 12
- rotated_key_heads: bfloat16 [4, 8192, 256], P(None, 'ctx'), may hold values from -12 to 12
- value_head_rows: bfloat16 [4, 8192, 256], P(None, 'ctx'), may hold values from -6 to 6
- out_proj: bfloat16 [2048, 2048], P('exp'), may hold values from -0.59765625 to 0.59765625
- norm_gain: float32 [2048], replicated, may hold values from 0.5 to 1.5
- expert_ids: int32 [32768, 1], P(('ctx', 'exp')), may hold values from 0 to 7; in each aligned block of 128 rows (0 to 127, 128 to 255, ...) at most 32 rows name the same one
- gate_weights: float32 [32768, 1], P(('ctx', 'exp')), may hold values from 0.25 to 1
- expert_gate: bfloat16 [8, 2048, 768], P('exp'), may hold values from -0.125 to 0.125
- expert_up: bfloat16 [8, 2048, 768], P('exp'), may hold values from -0.125 to 0.125
- expert_down: bfloat16 [8, 768, 2048], P('exp'), may hold values from -0.21875 to 0.21875
- grad_out: bfloat16 [32768, 2048], P(('ctx', 'exp')), may hold values from -2.5 to 2.5
Outputs:
- layer_out: bfloat16 [32768, 2048], P(('ctx', 'exp'))
- grad_hidden: bfloat16 [32768, 2048], P(('ctx', 'exp'))
- grad_gate: float32 [8, 2048, 768], P('exp', 'ctx')
- grad_up: float32 [8, 2048, 768], P('exp', 'ctx')
- grad_down: float32 [8, 768, 2048], P('exp', None, 'ctx')
The draws below stay inside these ranges and needn't reach their ends.
Inputs may be any that keep to these rules, and one draw needn't show every extreme that they name: `expert_ids`: in the rows of one device no expert is named more than 32 times, and the experts named in one row differ from each other.
All inputs are finite; a program needn't handle non-finite values.
Results may differ from the reference program's by a relative error of at most 0.035.
Values may be sent and summed in bfloat16 or wider, within the bound.
A program may use at most 128 MiB of HBM per device.

```python
import math
import jax
import jax.numpy as jnp
import numpy as np
from jax import lax

D = 2048
LOCAL_QUERY_HEADS = 16
LOCAL_KEY_HEADS = 2
HEAD_SIZE = 128
FF = 768
TOPK = 1
SEQUENCE_COUNT = 4
BLK = 256
SEQUENCE_LENGTH = 8192
TOKENS = 32768
TOK_DEV = 128
EXPERTS = 8
CAP = 32
N_CTX = 32
N_EXP = 8


def draw_queries(key, part):
    key = jax.random.fold_in(key, 3)
    value_entries = jnp.clip(jax.random.normal(key, (SEQUENCE_COUNT, SEQUENCE_LENGTH, LOCAL_QUERY_HEADS * HEAD_SIZE), jnp.float32), -6.0, 6.0)
    return value_entries.astype(jnp.bfloat16)


def draw_rotated_key_heads(key, part):
    key = jax.random.fold_in(key, 5)
    value_entries = jnp.clip(jax.random.normal(key, (SEQUENCE_COUNT, SEQUENCE_LENGTH, LOCAL_KEY_HEADS * HEAD_SIZE), jnp.float32), -6.0, 6.0)
    return value_entries.astype(jnp.bfloat16)


def strengthened(entries, key, source, target, parts, factor):
    owner, partner = [(jnp.arange(entries.shape[axis_at]) // (entries.shape[axis_at] // parts)).reshape([-1 if axis == axis_at else 1 for axis in range(entries.ndim)]) for axis_at in (source, target)]
    chosen = jax.random.permutation(key, parts)[partner]
    strong = (owner == chosen) | (owner == (partner + parts // 2) % parts)
    return jnp.where(strong, factor * entries, entries)


def block_levels(own_key, dims, pieces, low, top_value):
    factor_of, own = 1.0, jax.random.fold_in(own_key, 6)
    for axis_at, parts in pieces:
        heights = jnp.exp(jax.random.uniform(jax.random.fold_in(own, axis_at), (parts,), jnp.float32, low / len(pieces), top_value / len(pieces)))
        factor_of = factor_of * jnp.repeat(heights, dims[axis_at] // parts).reshape([-1 if axis == axis_at else 1 for axis in range(len(dims))])
    return factor_of


def assign_block(rng, own, number, rows, count, top, bound, slope):
    sequence = jax.random.permutation(rng, count)
    heavy_load, ordinary = portions_of(count, rows * top, bound, slope, True), portions_of(count, rows * top, bound, slope, False)
    places = jnp.arange(count)

    def named(tallies, offset_by):
        used = int((tallies > 0).sum())
        fixed = max(1, used // 4)
        moved = fixed + (places - fixed + offset_by * (used - fixed)) % max(1, count - fixed)
        return jnp.zeros((count,), jnp.int32).at[sequence[jnp.where(places < fixed, places, moved)]].set(jnp.asarray(tallies, jnp.int32))

    tallies = jnp.where(number % 4 == 0, named(heavy_load, number // 4), named(ordinary, number - number // 4 - 1))
    mixed = jax.random.permutation(jax.random.fold_in(own, 3), count)
    giver, sink = mixed[0:count // 2 * 2:2], mixed[1:count // 2 * 2:2]
    margin = jnp.minimum(tallies[giver] - 1, bound - tallies[sink]) // 2
    margin = jnp.where((giver == sequence[0]) | (sink == sequence[0]) | (tallies[sink] == 0), 0, jnp.maximum(margin, 0))
    moved = jax.random.randint(jax.random.fold_in(own, 4), (count // 2,), 0, 1 << 20) % (margin + 1)
    tallies = tallies.at[giver].add(-moved).at[sink].add(moved)
    items = jnp.searchsorted(jnp.cumsum(tallies), jnp.arange(rows * top), side="right").astype(jnp.int32)
    table = items.reshape(top, rows).T
    table = table[jax.random.permutation(jax.random.fold_in(own, 1), rows)]
    offset_by = jax.random.randint(jax.random.fold_in(own, 2), (rows, 1), 0, top)
    return jnp.take_along_axis(table, (jnp.arange(top)[None, :] + offset_by) % top, axis=1)


def portions_of(count, total, most, slope, full):
    weights = [(1 << 20) // math.isqrt(rank ** slope) + 1 for rank in range(1, count + 1)]
    largest = most if full else min(most, max(-(-total // count), total * weights[0] // sum(weights)))
    least = 1 if total - largest >= count - 1 else 0
    counts, spare = [largest] + [least] * (count - 1), total - largest - least * (count - 1)
    while spare > 0:
        movable = [i for i in range(1, count) if counts[i] < largest] or [i for i in range(1, count) if counts[i] < most]
        pool, remaining = sum([weights[i] for i in movable]), spare
        for i in movable:
            addition = min(most - counts[i], max(1, remaining * weights[i] // pool), spare)
            counts[i] = counts[i] + addition
            spare = spare - addition
    return np.array(counts)


def gaussian(own_key, dims, width, bound, cuts=(), held_as=jnp.bfloat16):
    level = block_levels(own_key, dims, cuts, -0.22, 0.18) if cuts else 1.0
    values = jax.random.normal(own_key, dims, jnp.float32) * width * level
    return jnp.minimum(jnp.maximum(values, -bound), bound).astype(held_as)


def bell_draw_with(key, dims, width, limit, shards, heavy, kind=jnp.bfloat16):
    drawn = width * jax.random.normal(key, dims, jnp.float32)
    if shards:
        drawn = drawn * block_levels(key, dims, shards, -0.22, 0.18)
    return jnp.clip(strengthened(drawn, jax.random.fold_in(key, 3), *heavy), -limit, limit).astype(kind)


def setup_inputs(seed: int = 0) -> dict:
    splits = jax.random.split(jax.random.key(seed), 12)
    queries = draw_queries(jax.random.fold_in(splits[11], 71), 0)
    rotated_key_heads = draw_rotated_key_heads(jax.random.fold_in(splits[11], 71), 0)
    value_head_rows = gaussian(splits[2], (SEQUENCE_COUNT, SEQUENCE_LENGTH, LOCAL_KEY_HEADS * HEAD_SIZE), 1.0, 6.0, ((1, 32),))
    out_proj = gaussian(splits[3], (LOCAL_QUERY_HEADS * HEAD_SIZE, D), 0.1, 0.59765625, ((0, 8),))
    norm_gain = jnp.clip(1.0 + 0.1 * jax.random.normal(splits[4], (D,), jnp.float32), 0.5, 1.5)
    expert_ids_keys = jax.random.split(jax.random.fold_in(splits[5], 1), TOKENS // TOK_DEV)
    expert_ids_turns = jax.random.permutation(jax.random.fold_in(splits[5], 3), TOKENS // TOK_DEV)
    expert_ids = jax.vmap(lambda own, number: assign_block(jax.random.fold_in(splits[5], 2), own, number, TOK_DEV, EXPERTS, TOPK, CAP, 2))(expert_ids_keys, expert_ids_turns).reshape((TOKENS, TOPK))
    gate_weights = jnp.clip(0.25 + 0.75 * jax.random.uniform(splits[6], (TOKENS, TOPK), jnp.float32) ** block_levels(splits[6], (TOKENS, TOPK), ((0, 256),), -0.2, 0.2), 0.25, 1.0)
    expert_gate = gaussian(splits[7], (EXPERTS, D, FF), D ** -0.5, 0.125, ((0, 8),))
    expert_up = gaussian(splits[8], (EXPERTS, D, FF), D ** -0.5, 0.125, ((0, 8),))
    expert_down = gaussian(splits[9], (EXPERTS, FF, D), FF ** -0.5, 0.21875, ((0, 8),))
    grad_out = bell_draw_with(splits[10], (TOKENS, D), 0.1, 2.5, ((0, 256),), (0, 1, 256, 6.0))
    return {"queries": queries, "rotated_key_heads": rotated_key_heads, "value_head_rows": value_head_rows, "out_proj": out_proj, "norm_gain": norm_gain, "expert_ids": expert_ids, "gate_weights": gate_weights, "expert_gate": expert_gate, "expert_up": expert_up, "expert_down": expert_down, "grad_out": grad_out}


epsilon = 1e-06
masked_score = -1e+30

def attend_head(trio):
    query_rows, key_rows, value_rows = trio
    positions = jnp.arange(query_rows.shape[0], dtype=jnp.int32)
    allowed = positions[None, :] <= positions[:, None]
    scores = jnp.dot(query_rows, key_rows.T, preferred_element_type=jnp.float32) * (1.0 / math.sqrt(HEAD_SIZE))
    scores = jnp.where(allowed, scores, masked_score)
    row_best = lax.optimization_barrier(jnp.max(scores, axis=1, keepdims=True))
    weights = jnp.where(allowed, jnp.exp(scores - row_best), 0.0)
    totals = lax.optimization_barrier(jnp.sum(weights, axis=1, keepdims=True))
    blended = jnp.dot(weights.astype(jnp.bfloat16), value_rows, preferred_element_type=jnp.float32)
    return (blended / totals).astype(jnp.bfloat16)

def block_tables(block_ids, block_gates):
    flat_ids = block_ids.reshape(-1).astype(jnp.int32)
    chosen = (flat_ids[:, None] == jnp.arange(EXPERTS, dtype=jnp.int32)[None, :]).astype(jnp.int32)
    earlier = jnp.cumsum(chosen, axis=0) - chosen
    target = flat_ids * CAP + lax.optimization_barrier(jnp.sum(earlier * chosen, axis=1))
    placed = (jnp.arange(EXPERTS * CAP, dtype=jnp.int32)[:, None] == target[None, :]).reshape(EXPERTS * CAP, TOK_DEV, TOPK)
    selector = jnp.any(placed, axis=2).astype(jnp.bfloat16)
    weighting = lax.optimization_barrier(jnp.sum(jnp.where(placed, block_gates[None, :, :], 0.0), axis=2))
    return (selector, weighting)

def round_sum(partials):
    rounded = lax.optimization_barrier(partials.astype(jnp.bfloat16))
    return lax.optimization_barrier(jnp.sum(rounded.astype(jnp.float32), axis=0))

def expert_pass(item):
    arrived, cotangent, gate_mat, up_mat, down_mat = item
    arrived_f = arrived.astype(jnp.float32)
    gate_f = gate_mat.astype(jnp.float32)
    up_f = up_mat.astype(jnp.float32)
    down_f = down_mat.astype(jnp.float32)
    gate_act = jnp.einsum('csd,df->csf', arrived_f, gate_f)
    up_act = jnp.einsum('csd,df->csf', arrived_f, up_f)
    sigma = jax.nn.sigmoid(gate_act)
    gated = gate_act * sigma
    hidden_units = (gated * up_act).astype(jnp.bfloat16)
    result = jnp.einsum('csf,fd->csd', hidden_units.astype(jnp.float32), down_f).astype(jnp.bfloat16)
    cotangent_f = cotangent.astype(jnp.float32)
    back_units = jnp.einsum('csd,fd->csf', cotangent_f, down_f)
    back_gate = (back_units * up_act * sigma * (1.0 + gate_act * (1.0 - sigma))).astype(jnp.bfloat16)
    back_up = (back_units * gated).astype(jnp.bfloat16)
    back_in = (jnp.einsum('csf,df->csd', back_gate.astype(jnp.float32), gate_f) + jnp.einsum('csf,df->csd', back_up.astype(jnp.float32), up_f)).astype(jnp.bfloat16)
    grad_gate_part = round_sum(jnp.einsum('csd,csf->cdf', arrived_f, back_gate.astype(jnp.float32)))
    grad_up_part = round_sum(jnp.einsum('csd,csf->cdf', arrived_f, back_up.astype(jnp.float32)))
    grad_down_part = round_sum(jnp.einsum('csf,csd->cfd', hidden_units.astype(jnp.float32), cotangent_f))
    return (result, back_in, grad_gate_part, grad_up_part, grad_down_part)

def reference(queries, rotated_key_heads, value_head_rows, out_proj, norm_gain, expert_ids, gate_weights, expert_gate, expert_up, expert_down, grad_out):
    query_group_width = LOCAL_QUERY_HEADS // LOCAL_KEY_HEADS
    query_all = queries.reshape(SEQUENCE_COUNT, SEQUENCE_LENGTH, LOCAL_QUERY_HEADS, HEAD_SIZE).transpose(0, 2, 1, 3).reshape(SEQUENCE_COUNT * LOCAL_QUERY_HEADS, SEQUENCE_LENGTH, HEAD_SIZE)
    gathered_keys = jnp.repeat(rotated_key_heads.reshape(SEQUENCE_COUNT, SEQUENCE_LENGTH, LOCAL_KEY_HEADS, HEAD_SIZE).transpose(0, 2, 1, 3), query_group_width, axis=1).reshape(SEQUENCE_COUNT * LOCAL_QUERY_HEADS, SEQUENCE_LENGTH, HEAD_SIZE)
    gathered_values = jnp.repeat(value_head_rows.reshape(SEQUENCE_COUNT, SEQUENCE_LENGTH, LOCAL_KEY_HEADS, HEAD_SIZE).transpose(0, 2, 1, 3), query_group_width, axis=1).reshape(SEQUENCE_COUNT * LOCAL_QUERY_HEADS, SEQUENCE_LENGTH, HEAD_SIZE)
    attended = lax.map(attend_head, (query_all, gathered_keys, gathered_values))
    attended = attended.reshape(SEQUENCE_COUNT, LOCAL_QUERY_HEADS, SEQUENCE_LENGTH, HEAD_SIZE).transpose(0, 2, 1, 3).reshape(SEQUENCE_COUNT * SEQUENCE_LENGTH, LOCAL_QUERY_HEADS * HEAD_SIZE)
    group_cols = LOCAL_QUERY_HEADS // N_EXP * HEAD_SIZE
    hidden_sum = jnp.zeros((SEQUENCE_COUNT * SEQUENCE_LENGTH, D), jnp.float32)
    for group_index in range(N_EXP):
        part_term = jnp.dot(attended[:, group_index * group_cols:(group_index + 1) * group_cols], out_proj[group_index * group_cols:(group_index + 1) * group_cols], preferred_element_type=jnp.float32)
        rounded = lax.optimization_barrier(part_term.astype(jnp.bfloat16))
        hidden_sum = hidden_sum + rounded.astype(jnp.float32)
    hidden = hidden_sum.astype(jnp.bfloat16).reshape(SEQUENCE_COUNT, N_CTX, BLK, D).transpose(1, 0, 2, 3).reshape(TOKENS, D)
    hidden_f = hidden.astype(jnp.float32)
    inv_rms = lax.rsqrt(lax.optimization_barrier(jnp.mean(hidden_f * hidden_f, axis=1, keepdims=True)) + epsilon)
    unit = hidden_f * inv_rms
    normed = (unit * norm_gain).astype(jnp.bfloat16)
    block_count = TOKENS // TOK_DEV
    selector, weighting = jax.vmap(block_tables)(expert_ids.reshape(block_count, TOK_DEV, TOPK), gate_weights.reshape(block_count, TOK_DEV, TOPK))
    send_rows = jnp.einsum('bst,btd->bsd', selector.astype(jnp.float32), normed.reshape(block_count, TOK_DEV, D).astype(jnp.float32)).astype(jnp.bfloat16)
    send_grads = jnp.einsum('bst,btd->bsd', weighting, grad_out.reshape(block_count, TOK_DEV, D).astype(jnp.float32), precision=lax.Precision.HIGHEST).astype(jnp.bfloat16)
    per_expert_rows = send_rows.reshape(N_CTX, N_EXP, EXPERTS, CAP, D).transpose(2, 0, 1, 3, 4).reshape(EXPERTS, N_CTX, N_EXP * CAP, D)
    per_expert_grads = send_grads.reshape(N_CTX, N_EXP, EXPERTS, CAP, D).transpose(2, 0, 1, 3, 4).reshape(EXPERTS, N_CTX, N_EXP * CAP, D)
    result, back_in, grad_gate, grad_up, grad_down = lax.map(expert_pass, (per_expert_rows, per_expert_grads, expert_gate, expert_up, expert_down))
    result = result.reshape(EXPERTS, N_CTX, N_EXP, CAP, D).transpose(1, 2, 0, 3, 4).reshape(block_count, EXPERTS * CAP, D)
    back_in = back_in.reshape(EXPERTS, N_CTX, N_EXP, CAP, D).transpose(1, 2, 0, 3, 4).reshape(block_count, EXPERTS * CAP, D)
    expert_sum = jnp.einsum('bst,bsd->btd', weighting, result.astype(jnp.float32), precision=lax.Precision.HIGHEST).reshape(TOKENS, D)
    layer_out = (hidden_f + expert_sum).astype(jnp.bfloat16)
    back_normed = jnp.einsum('bst,bsd->btd', selector.astype(jnp.float32), back_in.astype(jnp.float32)).reshape(TOKENS, D)
    scaled_back = back_normed * norm_gain
    grad_hidden = (grad_out.astype(jnp.float32) + inv_rms * (scaled_back - unit * lax.optimization_barrier(jnp.mean(scaled_back * unit, axis=1, keepdims=True)))).astype(jnp.bfloat16)
    return (layer_out, grad_hidden, grad_gate, grad_up, grad_down)
```

```python
import math

import jax
import jax.numpy as jnp
from jax import lax
from jax.experimental import pallas as pl
from jax.experimental.pallas import tpu as pltpu
from jax.sharding import PartitionSpec as P

MESH = pl.DeviceIdType.MESH
LOCAL_QUERY_HEADS = 16
LOCAL_KEY_HEADS = 2
HEAD_SIZE = 128


epsilon = 1e-06
masked_score = -1e30


def block_fold(query_heads, query_pos):
    score_scale = 1.0 / math.sqrt(query_heads.shape[4])
    last_query = jnp.max(query_pos)

    def fold_step(running, pieces, first_row):
        key_piece, value_piece = pieces
        seq_count = key_piece.shape[0]
        kv_count = query_heads.shape[2]
        sub_rows = math.gcd(key_piece.shape[1], 512)
        sub_steps = key_piece.shape[1] // sub_rows

        def visit_block(carried, sub_index):
            key_first = sub_index * sub_rows

            def compute(current):
                old_best, weight_total, weighted = current
                key_sub = lax.dynamic_slice_in_dim(
                    key_piece, sub_index * sub_rows, sub_rows, 1
                ).reshape(seq_count, sub_rows, kv_count, -1)
                value_sub = lax.dynamic_slice_in_dim(
                    value_piece, sub_index * sub_rows, sub_rows, 1
                ).reshape(seq_count, sub_rows, kv_count, -1)
                scores = (
                    jnp.einsum(
                        "sqgrd,skgd->sgrqk",
                        query_heads,
                        key_sub,
                        preferred_element_type=jnp.float32,
                    )
                    * score_scale
                )
                allowed = (key_first + jnp.arange(sub_rows))[None, :] <= query_pos[:, None]
                scores = jnp.where(allowed, scores, masked_score)
                new_best = jnp.maximum(old_best, jnp.max(scores, axis=-1))
                weights = jnp.where(allowed, jnp.exp(scores - new_best[..., None]), 0.0)
                factor = jnp.exp(old_best - new_best)
                new_total = weight_total * factor + jnp.sum(weights, axis=-1)
                blended = jnp.einsum(
                    "sgrqk,skgd->sgrqd",
                    weights.astype(jnp.bfloat16),
                    value_sub,
                    preferred_element_type=jnp.float32,
                )
                return (new_best, new_total, weighted * factor[..., None] + blended)

            def unchanged(current):
                return current

            return (lax.cond(key_first <= last_query, compute, unchanged, carried), None)

        running, _ = lax.scan(visit_block, running, jnp.arange(sub_steps))
        return running

    return fold_step


def grouped_fold(query_heads, pos_groups, running, pieces, first_row):
    folders = [block_fold(query_heads, pos_groups[0])]
    return tuple(
        (folder(state_one, pieces, first_row) for folder, state_one in zip(folders, running))
    )


def start_state(seq_count, kv_count, repeats, block_len, head_dim):
    best_start = jnp.full((seq_count, kv_count, repeats, block_len), masked_score, jnp.float32)
    total_start = jnp.zeros((seq_count, kv_count, repeats, block_len), jnp.float32)
    weighted_start = jnp.zeros((seq_count, kv_count, repeats, block_len, head_dim), jnp.float32)
    return (best_start, total_start, weighted_start)


def grouped_start(seq_count, kv_count, repeats, block_len, group_count):
    return tuple(
        (
            start_state(seq_count, kv_count, repeats, block_len // group_count, HEAD_SIZE)
            for index in range(group_count)
        )
    )


def finish_heads(running):
    best_score, weight_total, weighted = running
    scaled = weighted / weight_total[..., None]
    seq_count, kv_count, repeats, block_len, head_dim = scaled.shape
    return (
        scaled.transpose(0, 3, 1, 2, 4)
        .reshape(seq_count, block_len, kv_count * repeats * head_dim)
        .astype(jnp.bfloat16)
    )


def grouped_finish(running):
    return jnp.concatenate([finish_heads(state_one) for state_one in running], axis=1)


def own_heads(
    queries,
    rotated_key_heads,
    value_head_rows,
    owner_index,
    pos_groups,
    heads_dev,
    query_group_width,
):
    seq_count, block_len, _ = queries.shape
    kv_count = max(1, heads_dev // query_group_width)
    repeats = heads_dev // kv_count
    kv_first = owner_index * heads_dev // query_group_width
    key_mine = lax.dynamic_slice_in_dim(
        rotated_key_heads, kv_first * HEAD_SIZE, kv_count * HEAD_SIZE, 2
    )
    value_mine = lax.dynamic_slice_in_dim(
        value_head_rows, kv_first * HEAD_SIZE, kv_count * HEAD_SIZE, 2
    )
    query_heads = queries.reshape(seq_count, block_len, kv_count, repeats, HEAD_SIZE)
    running = grouped_fold(
        query_heads,
        pos_groups,
        grouped_start(seq_count, kv_count, repeats, block_len, len(pos_groups)),
        (
            lax.all_gather(key_mine, "ctx", axis=1, tiled=True),
            lax.all_gather(value_mine, "ctx", axis=1, tiled=True),
        ),
        jnp.int32(0),
    )
    return grouped_finish(running)


F = 768
DM = 2048
CAP = 32
HALF = 1152


def mesh_place():
    ctx = lax.axis_index("ctx")
    e = lax.axis_index("exp")
    x = ctx // 8
    y = lax.rem(ctx // 2, 4)
    z = lax.rem(ctx, 2)
    return ctx, e, x, y, z


def ctx_of(x, y, z):
    return x * 8 + y * 2 + z


def wrap4(i):
    return lax.rem(i + 4, 4)


def greet(partners):
    barrier = pltpu.get_barrier_semaphore()
    for place in partners:
        pl.semaphore_signal(barrier, inc=1, device_id=place, device_id_type=MESH)
    pl.semaphore_wait(barrier, len(partners))


def all_partners(ctx, e, x, y, z):
    found = [{"exp": lax.rem(e + d, 8)} for d in range(1, 8)]
    found += [{"ctx": ctx_of(wrap4(x + d), y, z)} for d in (1, -1)]
    found += [{"ctx": ctx_of(x, wrap4(y + d), z)} for d in (1, -1)]
    found += [{"ctx": ctx_of(x, y, 1 - z)}]
    return found


def remote(src, dst, send, recv, place):
    return pltpu.make_async_remote_copy(
        src_ref=src, dst_ref=dst, send_sem=send, recv_sem=recv,
        device_id=place, device_id_type=MESH,
    )


class RingSum:
    def __init__(self, index, right, left, part, slots, send, recv, base, add):
        self.i, self.part, self.slots, self.add = index, part, slots, add
        i = index
        plan = [
            (part(wrap4(i + 2), 0), right),
            (part(wrap4(i + 2), 1), left),
            (part(wrap4(i + 1), 1), right),
            (part(wrap4(i - 1), 0), left),
            (part(wrap4(i + 1), 0), right),
            (part(wrap4(i - 1), 1), left),
        ]
        self.copies = [
            remote(src, slots.at[n], send.at[base + n], recv.at[base + n], place)
            for n, (src, place) in enumerate(plan)
        ]

    def start(self):
        for n in range(4):
            self.copies[n].start()

    def middle(self):
        i = self.i
        self.copies[0].wait_recv()
        self.add(self.part(wrap4(i + 1), 0), [self.slots.at[0]])
        self.copies[4].start()
        self.copies[1].wait_recv()
        self.add(self.part(wrap4(i - 1), 1), [self.slots.at[1]])
        self.copies[5].start()

    def finish(self):
        i = self.i
        self.copies[3].wait_recv()
        self.copies[4].wait_recv()
        self.add(self.part(i, 0), [self.slots.at[3], self.slots.at[4]])
        self.copies[2].wait_recv()
        self.copies[5].wait_recv()
        self.add(self.part(i, 1), [self.slots.at[2], self.slots.at[5]])

    def drain(self):
        for copy in self.copies:
            copy.wait_send()


def add_rows(target, others):
    total = target[...].astype(jnp.float32)
    for other in others:
        total = total + other[...].astype(jnp.float32)
    target[...] = total.astype(jnp.bfloat16)


def add_blocks(target, others):
    def one(k, _):
        a, b = k // 2, lax.rem(k, 2)
        add_rows(target.at[a, b], [o.at[a, b] for o in others])
        return 0

    lax.fori_loop(0, 4, one, 0)


def expert_kernel(
    rows_in, grads_in, gate_in, up_in, down_in,
    res_out, back_out, gg_out, gu_out, gd_out,
    xr, cr, wg, wu, wd, act_g, act_u, act, xt, ct, grad,
    res, back, slots1a, slots1b, slots2a, slots2b, slot3,
    wsem, lsem, a2a_send, a2a_recv, rs_send, rs_recv,
):
    ctx, e, x, y, z = mesh_place()
    f32 = jnp.float32
    weight_copies = [
        pltpu.make_async_copy(src, dst, wsem.at[n])
        for n, (src, dst) in enumerate(((gate_in, wg), (up_in, wu), (down_in, wd)))
    ]
    for copy in weight_copies:
        copy.start()
    greet(all_partners(ctx, e, x, y, z))

    def exchange(src, dst, first):
        own = pltpu.make_async_copy(src.at[e], dst.at[e], lsem.at[first])
        out = []
        for d in range(1, 8):
            to = lax.rem(e + d, 8)
            out.append(remote(
                src.at[to], dst.at[e],
                a2a_send.at[first, d], a2a_recv.at[first, d], {"exp": to},
            ))
        return own, out

    def begin(pair):
        own, out = pair
        own.start()
        for copy in out:
            copy.start()

    def arrive(pair):
        own, out = pair
        own.wait()
        for copy in out:
            copy.wait_recv()

    rows_x = exchange(rows_in, xr, 0)
    grads_x = exchange(grads_in, cr, 1)
    res_x = exchange(res, res_out, 2)
    back_x = exchange(back, back_out, 3)
    begin(rows_x)
    begin(grads_x)
    for copy in weight_copies:
        copy.wait()
    arrive(rows_x)

    rows = xr[...].reshape(8 * CAP, DM)
    for n in range(3):
        cols = slice(n * 256, (n + 1) * 256)
        act_g[:, cols] = jnp.dot(rows, wg[:, cols], preferred_element_type=f32)
        act_u[:, cols] = jnp.dot(rows, wu[:, cols], preferred_element_type=f32)
    xt[...] = rows.T
    arrive(grads_x)
    cot = cr[...].reshape(8 * CAP, DM)
    ct[...] = cot.T
    over_last = (((1,), (1,)), ((), ()))
    for n in range(3):
        cols = slice(n * 256, (n + 1) * 256)
        back_units = lax.dot_general(cot, wd[cols, :], over_last, preferred_element_type=f32)
        gate_act, up_act = act_g[:, cols], act_u[:, cols]
        sigma = jax.nn.sigmoid(gate_act)
        gated = gate_act * sigma
        act[:, 1536 + n * 256:1536 + (n + 1) * 256] = (gated * up_act).astype(jnp.bfloat16)
        act[:, cols] = (
            back_units * up_act * sigma * (1.0 + gate_act * (1.0 - sigma))
        ).astype(jnp.bfloat16)
        act[:, 768 + n * 256:768 + (n + 1) * 256] = (back_units * gated).astype(jnp.bfloat16)

    for n in range(8):
        cols = slice(n * 256, (n + 1) * 256)
        res[:, :, cols] = jnp.dot(
            act[:, 1536:], wd[:, cols], preferred_element_type=f32
        ).astype(jnp.bfloat16).reshape(8, CAP, 256)
    begin(res_x)

    for px in range(4):
        for py in range(2):
            left = xt[px * 512 + py * 256:px * 512 + (py + 1) * 256, :]
            left_c = ct[px * 512 + py * 256:px * 512 + (py + 1) * 256, :]
            grad[px, 2 * py:2 * py + 2, :, :, 0:1536] = jnp.dot(
                left, act[:, :1536], preferred_element_type=f32
            ).astype(jnp.bfloat16).reshape(2, 2, 64, 1536)
            grad[px, 2 * py:2 * py + 2, :, :, 1536:2304] = jnp.dot(
                left_c, act[:, 1536:], preferred_element_type=f32
            ).astype(jnp.bfloat16).reshape(2, 2, 64, 768)

    in_a, in_b = pl.ds(0, HALF), pl.ds(HALF, HALF)
    x_right, x_left = {"ctx": ctx_of(wrap4(x + 1), y, z)}, {"ctx": ctx_of(wrap4(x - 1), y, z)}
    y_right, y_left = {"ctx": ctx_of(x, wrap4(y + 1), z)}, {"ctx": ctx_of(x, wrap4(y - 1), z)}
    first_a = RingSum(
        x, x_right, x_left, lambda i, h: grad.at[i, pl.ds(2 * h, 2), :, :, in_a],
        slots1a, rs_send, rs_recv, 0, add_blocks)
    first_b = RingSum(
        y, y_right, y_left, lambda i, h: grad.at[pl.ds(2 * h, 2), i, :, :, in_b],
        slots1b, rs_send, rs_recv, 6, add_blocks)
    second_a = RingSum(
        y, y_right, y_left, lambda i, h: grad.at[x, i, h, :, in_a],
        slots2a, rs_send, rs_recv, 12, add_rows)
    second_b = RingSum(
        x, x_right, x_left, lambda i, h: grad.at[i, y, h, :, in_b],
        slots2b, rs_send, rs_recv, 18, add_rows)
    first_a.start()
    first_b.start()

    for n in range(8):
        cols = slice(n * 256, (n + 1) * 256)
        back[:, :, cols] = (
            lax.dot_general(act[:, 0:768], wg[cols, :], over_last, preferred_element_type=f32)
            + lax.dot_general(act[:, 768:1536], wu[cols, :], over_last, preferred_element_type=f32)
        ).astype(jnp.bfloat16).reshape(8, CAP, 256)
    begin(back_x)

    first_a.middle()
    first_b.middle()
    first_a.finish()
    second_a.start()
    first_b.finish()
    second_b.start()
    second_a.middle()
    second_b.middle()
    second_a.finish()
    second_b.finish()
    last = remote(
        grad.at[x, y, 1 - z], slot3, rs_send.at[24], rs_recv.at[24],
        {"ctx": ctx_of(x, y, 1 - z)},
    )
    last.start()
    last.wait_recv()
    total = grad[x, y, z].astype(f32) + slot3[...].astype(f32)
    gg_out[...] = total[:, 0:768]
    gu_out[...] = total[:, 768:1536]
    gd_out[...] = total[:, 1536:2304]
    last.wait_send()
    for ring in (first_a, first_b, second_a, second_b):
        ring.drain()
    arrive(res_x)
    arrive(back_x)
    for pair in (rows_x, grads_x, res_x, back_x):
        for copy in pair[1]:
            copy.wait_send()


def expert_call(send_rows, send_grads, gate, up, down):
    bf, f32 = jnp.bfloat16, jnp.float32
    anywhere = pl.BlockSpec(memory_space=pl.ANY)
    vmem = pl.BlockSpec(memory_space=pltpu.VMEM)
    blocks = jax.ShapeDtypeStruct((8, CAP, DM), bf)
    shard = jax.ShapeDtypeStruct((64, F), f32)
    return pl.pallas_call(
        expert_kernel,
        out_shape=(blocks, blocks, shard, shard, shard),
        in_specs=[anywhere] * 5,
        out_specs=(anywhere, anywhere, vmem, vmem, vmem),
        scratch_shapes=[
            pltpu.VMEM((8, CAP, DM), bf),
            pltpu.VMEM((8, CAP, DM), bf),
            pltpu.VMEM((DM, F), bf),
            pltpu.VMEM((DM, F), bf),
            pltpu.VMEM((F, DM), bf),
            pltpu.VMEM((8 * CAP, F), f32),
            pltpu.VMEM((8 * CAP, F), f32),
            pltpu.VMEM((8 * CAP, 3 * F), bf),
            pltpu.VMEM((DM, 8 * CAP), bf),
            pltpu.VMEM((DM, 8 * CAP), bf),
            pltpu.VMEM((4, 4, 2, 64, 3 * F), bf),
            pltpu.VMEM((8, CAP, DM), bf),
            pltpu.VMEM((8, CAP, DM), bf),
            pltpu.VMEM((6, 2, 2, 64, HALF), bf),
            pltpu.VMEM((6, 2, 2, 64, HALF), bf),
            pltpu.VMEM((6, 64, HALF), bf),
            pltpu.VMEM((6, 64, HALF), bf),
            pltpu.VMEM((64, 3 * F), bf),
            pltpu.SemaphoreType.DMA((3,)),
            pltpu.SemaphoreType.DMA((4,)),
            pltpu.SemaphoreType.DMA((4, 8)),
            pltpu.SemaphoreType.DMA((4, 8)),
            pltpu.SemaphoreType.DMA((25,)),
            pltpu.SemaphoreType.DMA((25,)),
        ],
        compiler_params=pltpu.CompilerParams(
            collective_id=1, has_side_effects=True, vmem_limit_bytes=56 * 1024 * 1024
        ),
        name="expert_layer",
    )(send_rows, send_grads, gate, up, down)


def on_device(
    queries,
    rotated_key_heads,
    value_head_rows,
    out_proj,
    norm_gain,
    expert_ids,
    gate_weights,
    expert_gate,
    expert_up,
    expert_down,
    grad_out,
):
    seq_count, block_len, width = queries.shape
    heads_dev = width // HEAD_SIZE
    query_group_width = LOCAL_QUERY_HEADS // LOCAL_KEY_HEADS
    exp_count = lax.axis_size("exp")
    owner_index = lax.axis_index("exp")
    ctx_index = lax.axis_index("ctx")
    pos_groups = [ctx_index * block_len + jnp.arange(block_len)]
    attended = own_heads(
        queries,
        rotated_key_heads,
        value_head_rows,
        owner_index,
        pos_groups,
        heads_dev,
        query_group_width,
    )
    flat_heads = attended.reshape(seq_count * block_len, heads_dev * HEAD_SIZE)
    hidden = lax.psum_scatter(
        jnp.dot(flat_heads, out_proj, preferred_element_type=jnp.float32).astype(jnp.bfloat16),
        "exp",
        scatter_dimension=0,
        tiled=True,
    )
    hidden_f = hidden.astype(jnp.float32)
    inv_rms = lax.rsqrt(jnp.mean(hidden_f * hidden_f, axis=1, keepdims=True) + epsilon)
    unit = hidden_f * inv_rms
    normed = (unit * norm_gain).astype(jnp.bfloat16)
    dmodel = normed.shape[1]
    tok_rows, top_count = expert_ids.shape
    local_experts = expert_gate.shape[0]
    experts = local_experts * exp_count
    capacity = min(tok_rows, 2 * tok_rows * top_count // experts)
    flat_ids = expert_ids.reshape(-1)
    chosen = (flat_ids[:, None] == jnp.arange(experts)[None, :]).astype(jnp.int32)
    earlier = jnp.cumsum(chosen, axis=0) - chosen
    target = flat_ids * capacity + jnp.sum(earlier * chosen, axis=1)
    placed = (jnp.arange(experts * capacity)[:, None] == target[None, :]).reshape(
        experts * capacity, tok_rows, top_count
    )
    selector = jnp.any(placed, axis=2).astype(jnp.bfloat16)
    weighting = jnp.sum(jnp.where(placed, gate_weights[None, :, :], 0.0), axis=2)
    send_rows = jnp.dot(selector, normed, preferred_element_type=jnp.float32).astype(jnp.bfloat16)
    send_grads = jnp.dot(
        weighting, grad_out.astype(jnp.float32), precision=lax.Precision.HIGHEST
    ).astype(jnp.bfloat16)
    back_result, back_rows, grad_gate, grad_up, grad_down = expert_call(
        send_rows.reshape(experts, capacity, dmodel),
        send_grads.reshape(experts, capacity, dmodel),
        expert_gate[0],
        expert_up[0],
        expert_down[0],
    )
    expert_sum = jnp.dot(
        weighting.T,
        back_result.reshape(experts * capacity, dmodel).astype(jnp.float32),
        precision=lax.Precision.HIGHEST,
    )
    layer_out = (hidden_f + expert_sum).astype(jnp.bfloat16)
    back_normed = jnp.dot(
        selector.T,
        back_rows.reshape(experts * capacity, dmodel),
        preferred_element_type=jnp.float32,
    )
    scaled_back = back_normed * norm_gain
    grad_hidden = (
        grad_out.astype(jnp.float32)
        + inv_rms * (scaled_back - unit * jnp.mean(scaled_back * unit, axis=1, keepdims=True))
    ).astype(jnp.bfloat16)
    return (layer_out, grad_hidden, grad_gate[None], grad_up[None], grad_down.T[None])


def solution(mesh):
    in_specs = (
        P(None, "ctx", "exp"),
        P(None, "ctx", None),
        P(None, "ctx", None),
        P("exp", None),
        P(),
        P(("ctx", "exp"), None),
        P(("ctx", "exp"), None),
        P("exp", None, None),
        P("exp", None, None),
        P("exp", None, None),
        P(("ctx", "exp"), None),
    )
    out_specs = (
        P(("ctx", "exp"), None),
        P(("ctx", "exp"), None),
        P("exp", "ctx", None),
        P("exp", "ctx", None),
        P("exp", None, "ctx"),
    )
    return jax.shard_map(
        on_device, mesh=mesh, in_specs=in_specs, out_specs=out_specs, check_vma=False
    )
```

```python
import math

import jax
import jax.numpy as jnp
from jax import lax
from jax.experimental import pallas as pl
from jax.experimental.pallas import tpu as pltpu
from jax.sharding import PartitionSpec as P

MESH = pl.DeviceIdType.MESH
LOCAL_QUERY_HEADS = 16
LOCAL_KEY_HEADS = 2
HEAD_SIZE = 128


epsilon = 1e-06
masked_score = -1e30


F = 768
DM = 2048
CAP = 32
HALF = 1152


def mesh_place():
    ctx = lax.axis_index("ctx")
    e = lax.axis_index("exp")
    x = ctx // 8
    y = lax.rem(ctx // 2, 4)
    z = lax.rem(ctx, 2)
    return ctx, e, x, y, z


def ctx_of(x, y, z):
    return x * 8 + y * 2 + z


def wrap4(i):
    return lax.rem(i + 4, 4)


def greet(partners):
    barrier = pltpu.get_barrier_semaphore()
    for place in partners:
        pl.semaphore_signal(barrier, inc=1, device_id=place, device_id_type=MESH)
    pl.semaphore_wait(barrier, len(partners))


def all_partners(ctx, e, x, y, z):
    found = [{"exp": lax.rem(e + d, 8)} for d in range(1, 8)]
    found += [{"ctx": ctx_of(wrap4(x + d), y, z)} for d in (1, -1)]
    found += [{"ctx": ctx_of(x, wrap4(y + d), z)} for d in (1, -1)]
    found += [{"ctx": ctx_of(x, y, 1 - z)}]
    return found


def remote(src, dst, send, recv, place):
    return pltpu.make_async_remote_copy(
        src_ref=src, dst_ref=dst, send_sem=send, recv_sem=recv,
        device_id=place, device_id_type=MESH,
    )


class RingSum:
    def __init__(self, index, right, left, part, slots, send, recv, base, add):
        self.i, self.part, self.slots, self.add = index, part, slots, add
        i = index
        plan = [
            (part(wrap4(i + 2), 0), right),
            (part(wrap4(i + 2), 1), left),
            (part(wrap4(i + 1), 1), right),
            (part(wrap4(i - 1), 0), left),
            (part(wrap4(i + 1), 0), right),
            (part(wrap4(i - 1), 1), left),
        ]
        self.copies = [
            remote(src, slots.at[n], send.at[base + n], recv.at[base + n], place)
            for n, (src, place) in enumerate(plan)
        ]

    def start(self):
        for n in range(4):
            self.copies[n].start()

    def middle(self):
        i = self.i
        self.copies[0].wait_recv()
        self.add(self.part(wrap4(i + 1), 0), [self.slots.at[0]])
        self.copies[4].start()
        self.copies[1].wait_recv()
        self.add(self.part(wrap4(i - 1), 1), [self.slots.at[1]])
        self.copies[5].start()

    def finish(self):
        i = self.i
        self.copies[3].wait_recv()
        self.copies[4].wait_recv()
        self.add(self.part(i, 0), [self.slots.at[3], self.slots.at[4]])
        self.copies[2].wait_recv()
        self.copies[5].wait_recv()
        self.add(self.part(i, 1), [self.slots.at[2], self.slots.at[5]])

    def drain(self):
        for copy in self.copies:
            copy.wait_send()


def add_rows(target, others):
    total = target[...].astype(jnp.float32)
    for other in others:
        total = total + other[...].astype(jnp.float32)
    target[...] = total.astype(jnp.bfloat16)


def add_blocks(target, others):
    def one(k, _):
        a, b = k // 2, lax.rem(k, 2)
        add_rows(target.at[a, b], [o.at[a, b] for o in others])
        return 0

    lax.fori_loop(0, 4, one, 0)


def expert_kernel(
    rows_in, grads_in, gate_in, up_in, down_in,
    res_out, back_out, gg_out, gu_out, gd_out,
    xr, cr, wg, wu, wd, act_g, act_u, act, xt, ct, grad,
    res, back, slots1a, slots1b, slots2a, slots2b, slot3,
    wsem, lsem, a2a_send, a2a_recv, rs_send, rs_recv,
):
    ctx, e, x, y, z = mesh_place()
    f32 = jnp.float32
    weight_copies = [
        pltpu.make_async_copy(src, dst, wsem.at[n])
        for n, (src, dst) in enumerate(((gate_in, wg), (up_in, wu), (down_in, wd)))
    ]
    for copy in weight_copies:
        copy.start()
    greet(all_partners(ctx, e, x, y, z))

    def exchange(src, dst, first):
        own = pltpu.make_async_copy(src.at[e], dst.at[e], lsem.at[first])
        out = []
        for d in range(1, 8):
            to = lax.rem(e + d, 8)
            out.append(remote(
                src.at[to], dst.at[e],
                a2a_send.at[first, d], a2a_recv.at[first, d], {"exp": to},
            ))
        return own, out

    def begin(pair):
        own, out = pair
        own.start()
        for copy in out:
            copy.start()

    def arrive(pair):
        own, out = pair
        own.wait()
        for copy in out:
            copy.wait_recv()

    rows_x = exchange(rows_in, xr, 0)
    grads_x = exchange(grads_in, cr, 1)
    res_x = exchange(res, res_out, 2)
    back_x = exchange(back, back_out, 3)
    begin(rows_x)
    begin(grads_x)
    for copy in weight_copies:
        copy.wait()
    arrive(rows_x)

    rows = xr[...].reshape(8 * CAP, DM)
    for n in range(3):
        cols = slice(n * 256, (n + 1) * 256)
        act_g[:, cols] = jnp.dot(rows, wg[:, cols], preferred_element_type=f32)
        act_u[:, cols] = jnp.dot(rows, wu[:, cols], preferred_element_type=f32)
    xt[...] = rows.T
    arrive(grads_x)
    cot = cr[...].reshape(8 * CAP, DM)
    ct[...] = cot.T
    over_last = (((1,), (1,)), ((), ()))
    for n in range(3):
        cols = slice(n * 256, (n + 1) * 256)
        back_units = lax.dot_general(cot, wd[cols, :], over_last, preferred_element_type=f32)
        gate_act, up_act = act_g[:, cols], act_u[:, cols]
        sigma = jax.nn.sigmoid(gate_act)
        gated = gate_act * sigma
        act[:, 1536 + n * 256:1536 + (n + 1) * 256] = (gated * up_act).astype(jnp.bfloat16)
        act[:, cols] = (
            back_units * up_act * sigma * (1.0 + gate_act * (1.0 - sigma))
        ).astype(jnp.bfloat16)
        act[:, 768 + n * 256:768 + (n + 1) * 256] = (back_units * gated).astype(jnp.bfloat16)

    for n in range(8):
        cols = slice(n * 256, (n + 1) * 256)
        res[:, :, cols] = jnp.dot(
            act[:, 1536:], wd[:, cols], preferred_element_type=f32
        ).astype(jnp.bfloat16).reshape(8, CAP, 256)
    begin(res_x)

    for px in range(4):
        for py in range(2):
            left = xt[px * 512 + py * 256:px * 512 + (py + 1) * 256, :]
            left_c = ct[px * 512 + py * 256:px * 512 + (py + 1) * 256, :]
            grad[px, 2 * py:2 * py + 2, :, :, 0:1536] = jnp.dot(
                left, act[:, :1536], preferred_element_type=f32
            ).astype(jnp.bfloat16).reshape(2, 2, 64, 1536)
            grad[px, 2 * py:2 * py + 2, :, :, 1536:2304] = jnp.dot(
                left_c, act[:, 1536:], preferred_element_type=f32
            ).astype(jnp.bfloat16).reshape(2, 2, 64, 768)

    in_a, in_b = pl.ds(0, HALF), pl.ds(HALF, HALF)
    x_right, x_left = {"ctx": ctx_of(wrap4(x + 1), y, z)}, {"ctx": ctx_of(wrap4(x - 1), y, z)}
    y_right, y_left = {"ctx": ctx_of(x, wrap4(y + 1), z)}, {"ctx": ctx_of(x, wrap4(y - 1), z)}
    first_a = RingSum(
        x, x_right, x_left, lambda i, h: grad.at[i, pl.ds(2 * h, 2), :, :, in_a],
        slots1a, rs_send, rs_recv, 0, add_blocks)
    first_b = RingSum(
        y, y_right, y_left, lambda i, h: grad.at[pl.ds(2 * h, 2), i, :, :, in_b],
        slots1b, rs_send, rs_recv, 6, add_blocks)
    second_a = RingSum(
        y, y_right, y_left, lambda i, h: grad.at[x, i, h, :, in_a],
        slots2a, rs_send, rs_recv, 12, add_rows)
    second_b = RingSum(
        x, x_right, x_left, lambda i, h: grad.at[i, y, h, :, in_b],
        slots2b, rs_send, rs_recv, 18, add_rows)
    first_a.start()
    first_b.start()

    for n in range(8):
        cols = slice(n * 256, (n + 1) * 256)
        back[:, :, cols] = (
            lax.dot_general(act[:, 0:768], wg[cols, :], over_last, preferred_element_type=f32)
            + lax.dot_general(act[:, 768:1536], wu[cols, :], over_last, preferred_element_type=f32)
        ).astype(jnp.bfloat16).reshape(8, CAP, 256)
    begin(back_x)

    first_a.middle()
    first_b.middle()
    first_a.finish()
    second_a.start()
    first_b.finish()
    second_b.start()
    second_a.middle()
    second_b.middle()
    second_a.finish()
    second_b.finish()
    last = remote(
        grad.at[x, y, 1 - z], slot3, rs_send.at[24], rs_recv.at[24],
        {"ctx": ctx_of(x, y, 1 - z)},
    )
    last.start()
    last.wait_recv()
    total = grad[x, y, z].astype(f32) + slot3[...].astype(f32)
    gg_out[...] = total[:, 0:768]
    gu_out[...] = total[:, 768:1536]
    gd_out[...] = total[:, 1536:2304]
    last.wait_send()
    for ring in (first_a, first_b, second_a, second_b):
        ring.drain()
    arrive(res_x)
    arrive(back_x)
    for pair in (rows_x, grads_x, res_x, back_x):
        for copy in pair[1]:
            copy.wait_send()


def expert_call(send_rows, send_grads, gate, up, down):
    bf, f32 = jnp.bfloat16, jnp.float32
    anywhere = pl.BlockSpec(memory_space=pl.ANY)
    vmem = pl.BlockSpec(memory_space=pltpu.VMEM)
    blocks = jax.ShapeDtypeStruct((8, CAP, DM), bf)
    shard = jax.ShapeDtypeStruct((64, F), f32)
    return pl.pallas_call(
        expert_kernel,
        out_shape=(blocks, blocks, shard, shard, shard),
        in_specs=[anywhere] * 5,
        out_specs=(anywhere, anywhere, vmem, vmem, vmem),
        scratch_shapes=[
            pltpu.VMEM((8, CAP, DM), bf),
            pltpu.VMEM((8, CAP, DM), bf),
            pltpu.VMEM((DM, F), bf),
            pltpu.VMEM((DM, F), bf),
            pltpu.VMEM((F, DM), bf),
            pltpu.VMEM((8 * CAP, F), f32),
            pltpu.VMEM((8 * CAP, F), f32),
            pltpu.VMEM((8 * CAP, 3 * F), bf),
            pltpu.VMEM((DM, 8 * CAP), bf),
            pltpu.VMEM((DM, 8 * CAP), bf),
            pltpu.VMEM((4, 4, 2, 64, 3 * F), bf),
            pltpu.VMEM((8, CAP, DM), bf),
            pltpu.VMEM((8, CAP, DM), bf),
            pltpu.VMEM((6, 2, 2, 64, HALF), bf),
            pltpu.VMEM((6, 2, 2, 64, HALF), bf),
            pltpu.VMEM((6, 64, HALF), bf),
            pltpu.VMEM((6, 64, HALF), bf),
            pltpu.VMEM((64, 3 * F), bf),
            pltpu.SemaphoreType.DMA((3,)),
            pltpu.SemaphoreType.DMA((4,)),
            pltpu.SemaphoreType.DMA((4, 8)),
            pltpu.SemaphoreType.DMA((4, 8)),
            pltpu.SemaphoreType.DMA((25,)),
            pltpu.SemaphoreType.DMA((25,)),
        ],
        compiler_params=pltpu.CompilerParams(
            collective_id=1, has_side_effects=True, vmem_limit_bytes=56 * 1024 * 1024
        ),
        name="expert_layer",
    )(send_rows, send_grads, gate, up, down)


class RingGather:
    def __init__(self, index, right, left, part, send, recv, base):
        i = index
        plan = [
            (part(i, None), right),
            (part(i, None), left),
            (part(wrap4(i - 1), 0), right),
            (part(wrap4(i + 1), 1), left),
        ]
        self.copies = [
            remote(src, src, send.at[base + n], recv.at[base + n], place)
            for n, (src, place) in enumerate(plan)
        ]

    def start(self):
        self.copies[0].start()
        self.copies[1].start()

    def middle(self):
        self.copies[0].wait_recv()
        self.copies[2].start()
        self.copies[1].wait_recv()
        self.copies[3].start()

    def finish(self):
        self.copies[2].wait_recv()
        self.copies[3].wait_recv()

    def drain(self):
        for copy in self.copies:
            copy.wait_send()


def attention_kernel(
    q_in, k_in, v_in, o_in, hid_out,
    qs, kv, w, best, tot, acc, att, part_f, part_b, got,
    lsem, q_send, q_recv, w_send, w_recv, z_send, z_recv, g_send, g_recv, s_send, s_recv,
):
    ctx, e, x, y, z = mesh_place()
    f32, bf = jnp.float32, jnp.bfloat16
    seq, core = e // 2, lax.rem(e, 2)
    group, slot = e // 4, lax.rem(e, 4)
    head_cols = pl.ds(pl.multiple_of(core * HEAD_SIZE, HEAD_SIZE), HEAD_SIZE)
    own_k = pltpu.make_async_copy(k_in.at[seq, :, head_cols], kv.at[x, y, z, 0], lsem.at[0])
    own_v = pltpu.make_async_copy(v_in.at[seq, :, head_cols], kv.at[x, y, z, 1], lsem.at[1])
    own_k.start()
    own_v.start()
    greet(all_partners(ctx, e, x, y, z))

    x_right, x_left = {"ctx": ctx_of(wrap4(x + 1), y, z)}, {"ctx": ctx_of(wrap4(x - 1), y, z)}
    y_right, y_left = {"ctx": ctx_of(x, wrap4(y + 1), z)}, {"ctx": ctx_of(x, wrap4(y - 1), z)}

    def ring_x(base, part):
        return RingGather(x, x_right, x_left, part, g_send, g_recv, base)

    def ring_y(base, part):
        return RingGather(y, y_right, y_left, part, g_send, g_recv, base)

    def two(h):
        return slice(None) if h is None else pl.ds(2 * h, 2)

    kv_a1 = ring_x(0, lambda i, h: kv.at[i, y, 0] if h is None else kv.at[i, y, 0, h])
    kv_b1 = ring_y(4, lambda i, h: kv.at[x, i, 1] if h is None else kv.at[x, i, 1, h])
    kv_a2 = ring_y(8, lambda i, h: kv.at[two(h), i, 0])
    kv_b2 = ring_x(12, lambda i, h: kv.at[i, two(h), 1])
    w_a1 = ring_x(16, lambda i, h: w.at[pl.ds(0, 2), i, y] if h is None else w.at[h, i, y])
    w_b1 = ring_y(20, lambda i, h: w.at[pl.ds(2, 2), x, i] if h is None else w.at[2 + h, x, i])
    w_a2 = ring_y(24, lambda i, h: w.at[pl.ds(0, 2), :, i] if h is None else w.at[h, :, i])
    w_b2 = ring_x(28, lambda i, h: w.at[pl.ds(2, 2), i] if h is None else w.at[2 + h, i])
    z_copy = remote(
        kv.at[x, y, z], kv.at[x, y, z], z_send, z_recv, {"ctx": ctx_of(x, y, 1 - z)}
    )

    own_k.wait()
    own_v.wait()
    z_copy.start()

    @pl.when(z == 0)
    def _():
        kv_a1.start()

    @pl.when(z == 1)
    def _():
        kv_b1.start()

    piece = pl.ds(pl.multiple_of((x * 4 + y) * 16, 16), 16)
    scatters = []
    for d in range(4):
        s = lax.rem(seq + d, 4)
        to = {"exp": 2 * s + group}
        scatters.append((
            remote(q_in.at[s], qs.at[slot], q_send.at[d], q_recv.at[slot], to),
            remote(o_in.at[piece, :], w.at[slot, x, y], w_send.at[d], w_recv.at[slot], to),
        ))
    mine = core == group
    own_q = pltpu.make_async_copy(q_in.at[seq], qs.at[slot], q_recv.at[slot])
    own_w = pltpu.make_async_copy(o_in.at[piece, :], w.at[slot, x, y], w_recv.at[slot])
    for n, own in ((0, own_q), (1, own_w)):
        @pl.when(mine)
        def _():
            own.start()

        @pl.when(jnp.logical_not(mine))
        def _():
            scatters[0][n].start()

        for d in range(1, 4):
            scatters[d][n].start()

    z_copy.wait_recv()

    @pl.when(z == 0)
    def _():
        kv_b1.start()

    @pl.when(z == 1)
    def _():
        kv_a1.start()

    for j in range(4):
        pltpu.make_async_copy(qs.at[j], qs.at[j], q_recv.at[j]).wait()
    kv_a1.middle()
    kv_b1.middle()

    scale = math.log2(math.e) / math.sqrt(HEAD_SIZE)
    over_last = (((1,), (1,)), ((), ()))

    def head_scores(j, t, key):
        query = qs[j, :, t * HEAD_SIZE:(t + 1) * HEAD_SIZE]
        return lax.dot_general(query, key, over_last, preferred_element_type=f32) * scale

    def own_block(j, _):
        key, value = kv[x, y, z, 0], kv[x, y, z, 1]
        rows_at = lax.broadcasted_iota(jnp.int32, (256, 256), 0)
        cols_at = lax.broadcasted_iota(jnp.int32, (256, 256), 1)
        for t in range(2):
            scores = jnp.where(cols_at <= rows_at, head_scores(j, t, key), masked_score)
            top = jnp.max(scores, axis=1, keepdims=True)
            weights = jnp.exp2(scores - top)
            best[j, t] = jnp.broadcast_to(top, (256, HEAD_SIZE))
            tot[j, t] = weights[:, :HEAD_SIZE] + weights[:, HEAD_SIZE:]
            acc[j, t] = jnp.dot(weights.astype(bf), value, preferred_element_type=f32)
        return 0

    def fold(bx, by, bz):
        def heads(jj, _):
            key, value = kv[bx, by, bz, 0], kv[bx, by, bz, 1]
            for t4 in range(4):
                j, t = jj * 2 + t4 // 2, t4 % 2
                scores = head_scores(j, t, key)
                old = best[j, t]
                new = jnp.maximum(old, jnp.max(scores, axis=1, keepdims=True))
                weights = jnp.exp2(scores - jnp.concatenate([new, new], axis=1))
                factor = jnp.exp2(old - new)
                best[j, t] = new
                tot[j, t] = tot[j, t] * factor + weights[:, :HEAD_SIZE] + weights[:, HEAD_SIZE:]
                acc[j, t] = acc[j, t] * factor + jnp.dot(
                    weights.astype(bf), value, preferred_element_type=f32
                )
            return 0

        lax.fori_loop(0, 2, heads, 0)

    def visit(count, place):
        def one(i, _):
            bx, by, bz = place(i)

            @pl.when(ctx_of(bx, by, bz) < ctx)
            def _():
                fold(bx, by, bz)

            return 0

        lax.fori_loop(0, count, one, 0)

    lax.fori_loop(0, 4, own_block, 0)
    kv_a1.finish()
    kv_a2.start()
    kv_b1.finish()
    kv_b2.start()
    for j in range(4):
        pltpu.make_async_copy(w.at[j, x, y], w.at[j, x, y], w_recv.at[j]).wait()
    w_a1.start()
    w_b1.start()

    def first_places(i):
        in_a = i < 3
        bx = jnp.where(in_a, wrap4(x + 1 + i), x)
        by = jnp.where(in_a, y, wrap4(y + i - 2))
        last = i == 6
        return bx, jnp.where(last, y, by), jnp.where(in_a | last, 0, 1)

    def first_place(i):
        bx, by, bz = first_places(i)
        return jnp.where(i == 6, x, bx), by, bz

    visit(jnp.where(z == 1, 7, 6), first_place)
    kv_a2.middle()
    kv_b2.middle()
    w_a1.middle()
    w_b1.middle()

    def near_place(i):
        in_a = i < 8
        k = lax.rem(i, 8)
        step = 1 - 2 * lax.rem(k, 2)
        bx = jnp.where(in_a, k // 2, wrap4(x + step))
        by = jnp.where(in_a, wrap4(y + step), k // 2)
        return bx, by, jnp.where(in_a, 0, 1)

    visit(6, near_place)
    w_a1.finish()
    w_a2.start()
    w_b1.finish()
    w_b2.start()
    visit(10, lambda i: near_place(i + 6))
    kv_a2.finish()
    kv_b2.finish()
    w_a2.middle()
    w_b2.middle()

    def far_place(i):
        in_a = i < 4
        k = lax.rem(i, 4)
        bx = jnp.where(in_a, k, wrap4(x + 2))
        by = jnp.where(in_a, wrap4(y + 2), k)
        return bx, by, jnp.where(in_a, 0, 1)

    visit(8, far_place)

    for j in range(4):
        for t in range(2):
            total = jnp.sum(tot[j, t], axis=1, keepdims=True)
            h = j * 2 + t
            att[:, :, h * HEAD_SIZE:(h + 1) * HEAD_SIZE] = (
                (acc[j, t] / total).astype(bf).reshape(2, 128, HEAD_SIZE)
            )
    w_a2.finish()
    w_b2.finish()

    sibling = {"exp": e + 1 - 2 * core}
    half = remote(part_b, got, s_send, s_recv, sibling)

    def project(rows, n):
        cols = pl.ds(pl.multiple_of(n * 256, 256), 256)
        return cols, jnp.dot(
            rows, w[:, :, :, :, cols].reshape(1024, 256), preferred_element_type=f32
        )

    def theirs(n, _):
        cols, value = project(att[1 - core], n)
        part_b[:, cols] = value.astype(bf)
        return 0

    def ours(n, _):
        cols, value = project(att[core], n)
        part_f[:, cols] = value
        return 0

    lax.fori_loop(0, 8, theirs, 0)
    half.start()
    lax.fori_loop(0, 8, ours, 0)
    half.wait_recv()
    hid_out[...] = (part_f[...] + got[...].astype(f32)).astype(bf)

    half.wait_send()
    z_copy.wait_send()
    for ring in (kv_a1, kv_b1, kv_a2, kv_b2, w_a1, w_b1, w_a2, w_b2):
        ring.drain()
    for n in range(2):
        @pl.when(jnp.logical_not(mine))
        def _():
            scatters[0][n].wait_send()

        for d in range(1, 4):
            scatters[d][n].wait_send()


def attention_call(queries, keys, values, out_proj):
    bf, f32 = jnp.bfloat16, jnp.float32
    anywhere = pl.BlockSpec(memory_space=pl.ANY)
    dma = pltpu.SemaphoreType.DMA
    return pl.pallas_call(
        attention_kernel,
        out_shape=jax.ShapeDtypeStruct((128, DM), bf),
        in_specs=[anywhere] * 4,
        out_specs=pl.BlockSpec(memory_space=pltpu.VMEM),
        scratch_shapes=[
            pltpu.VMEM((4, 256, 256), bf),
            pltpu.VMEM((4, 4, 2, 2, 256, HEAD_SIZE), bf),
            pltpu.VMEM((4, 4, 4, 16, DM), bf),
            pltpu.VMEM((4, 2, 256, HEAD_SIZE), f32),
            pltpu.VMEM((4, 2, 256, HEAD_SIZE), f32),
            pltpu.VMEM((4, 2, 256, HEAD_SIZE), f32),
            pltpu.VMEM((2, 128, 1024), bf),
            pltpu.VMEM((128, DM), f32),
            pltpu.VMEM((128, DM), bf),
            pltpu.VMEM((128, DM), bf),
            dma((2,)), dma((4,)), dma((4,)), dma((4,)), dma((4,)),
            dma(()), dma(()), dma((32,)), dma((32,)), dma(()), dma(()),
        ],
        compiler_params=pltpu.CompilerParams(
            collective_id=2, has_side_effects=True, vmem_limit_bytes=48 * 1024 * 1024
        ),
        name="attention",
    )(queries, keys, values, out_proj)


def on_device(
    queries,
    rotated_key_heads,
    value_head_rows,
    out_proj,
    norm_gain,
    expert_ids,
    gate_weights,
    expert_gate,
    expert_up,
    expert_down,
    grad_out,
):
    exp_count = lax.axis_size("exp")
    hidden = attention_call(queries, rotated_key_heads, value_head_rows, out_proj)
    hidden_f = hidden.astype(jnp.float32)
    inv_rms = lax.rsqrt(jnp.mean(hidden_f * hidden_f, axis=1, keepdims=True) + epsilon)
    unit = hidden_f * inv_rms
    normed = (unit * norm_gain).astype(jnp.bfloat16)
    dmodel = normed.shape[1]
    tok_rows, top_count = expert_ids.shape
    local_experts = expert_gate.shape[0]
    experts = local_experts * exp_count
    capacity = min(tok_rows, 2 * tok_rows * top_count // experts)
    flat_ids = expert_ids.reshape(-1)
    chosen = (flat_ids[:, None] == jnp.arange(experts)[None, :]).astype(jnp.int32)
    earlier = jnp.cumsum(chosen, axis=0) - chosen
    target = flat_ids * capacity + jnp.sum(earlier * chosen, axis=1)
    placed = (jnp.arange(experts * capacity)[:, None] == target[None, :]).reshape(
        experts * capacity, tok_rows, top_count
    )
    selector = jnp.any(placed, axis=2).astype(jnp.bfloat16)
    weighting = jnp.sum(jnp.where(placed, gate_weights[None, :, :], 0.0), axis=2)
    send_rows = jnp.dot(selector, normed, preferred_element_type=jnp.float32).astype(jnp.bfloat16)
    send_grads = jnp.dot(
        weighting, grad_out.astype(jnp.float32), precision=lax.Precision.HIGHEST
    ).astype(jnp.bfloat16)
    back_result, back_rows, grad_gate, grad_up, grad_down = expert_call(
        send_rows.reshape(experts, capacity, dmodel),
        send_grads.reshape(experts, capacity, dmodel),
        expert_gate[0],
        expert_up[0],
        expert_down[0],
    )
    expert_sum = jnp.dot(
        weighting.T,
        back_result.reshape(experts * capacity, dmodel).astype(jnp.float32),
        precision=lax.Precision.HIGHEST,
    )
    layer_out = (hidden_f + expert_sum).astype(jnp.bfloat16)
    back_normed = jnp.dot(
        selector.T,
        back_rows.reshape(experts * capacity, dmodel),
        preferred_element_type=jnp.float32,
    )
    scaled_back = back_normed * norm_gain
    grad_hidden = (
        grad_out.astype(jnp.float32)
        + inv_rms * (scaled_back - unit * jnp.mean(scaled_back * unit, axis=1, keepdims=True))
    ).astype(jnp.bfloat16)
    return (layer_out, grad_hidden, grad_gate[None], grad_up[None], grad_down.T[None])


def solution(mesh):
    in_specs = (
        P(None, "ctx", "exp"),
        P(None, "ctx", None),
        P(None, "ctx", None),
        P("exp", None),
        P(),
        P(("ctx", "exp"), None),
        P(("ctx", "exp"), None),
        P("exp", None, None),
        P("exp", None, None),
        P("exp", None, None),
        P(("ctx", "exp"), None),
    )
    out_specs = (
        P(("ctx", "exp"), None),
        P(("ctx", "exp"), None),
        P("exp", "ctx", None),
        P("exp", "ctx", None),
        P("exp", None, "ctx"),
    )
    return jax.shard_map(
        on_device, mesh=mesh, in_specs=in_specs, out_specs=out_specs, check_vma=False
    )
```

```python
import math

import jax
import jax.numpy as jnp
from jax import lax
from jax.experimental import pallas as pl
from jax.experimental.pallas import tpu as pltpu
from jax.sharding import PartitionSpec as P

MESH = pl.DeviceIdType.MESH
HEAD_SIZE = 128
F = 768
DM = 2048
CAP = 32
SLOTS = 8 * CAP
TOK = 128
CHAINS = ((0, 640), (1152, 640), (640, 512), (1792, 512))

epsilon = 1e-06
masked_score = -1e30


def mesh_place():
    ctx = lax.axis_index("ctx")
    e = lax.axis_index("exp")
    x = ctx // 8
    y = lax.rem(ctx // 2, 4)
    z = lax.rem(ctx, 2)
    return ctx, e, x, y, z


def ctx_of(x, y, z):
    return x * 8 + y * 2 + z


def wrap4(i):
    return lax.rem(i + 4, 4)


def greet(partners):
    barrier = pltpu.get_barrier_semaphore()
    for place in partners:
        pl.semaphore_signal(barrier, inc=1, device_id=place, device_id_type=MESH)
    pl.semaphore_wait(barrier, len(partners))


def all_partners(ctx, e, x, y, z):
    found = [{"exp": lax.rem(e + d, 8)} for d in range(1, 8)]
    found += [{"ctx": ctx_of(wrap4(x + d), y, z)} for d in (1, -1)]
    found += [{"ctx": ctx_of(x, wrap4(y + d), z)} for d in (1, -1)]
    found += [{"ctx": ctx_of(x, y, 1 - z)}]
    return found


def remote(src, dst, send, recv, place):
    return pltpu.make_async_remote_copy(
        src_ref=src, dst_ref=dst, send_sem=send, recv_sem=recv,
        device_id=place, device_id_type=MESH,
    )


class RingSum:
    def __init__(self, index, right, left, part, slots, send, recv, base, add):
        self.i, self.part, self.slots, self.add = index, part, slots, add
        i = index
        plan = [
            (part(wrap4(i + 2), 0), right),
            (part(wrap4(i + 2), 1), left),
            (part(wrap4(i + 1), 1), right),
            (part(wrap4(i - 1), 0), left),
            (part(wrap4(i + 1), 0), right),
            (part(wrap4(i - 1), 1), left),
        ]
        self.copies = [
            remote(src, slots.at[n], send.at[base + n], recv.at[base + n], place)
            for n, (src, place) in enumerate(plan)
        ]

    def start(self, *chosen):
        for n in chosen or range(4):
            self.copies[n].start()

    def middle(self):
        i = self.i
        self.copies[0].wait_recv()
        self.add(self.part(wrap4(i + 1), 0), [self.slots.at[0]])
        self.copies[4].start()
        self.copies[1].wait_recv()
        self.add(self.part(wrap4(i - 1), 1), [self.slots.at[1]])
        self.copies[5].start()

    def finish(self):
        i = self.i
        self.copies[3].wait_recv()
        self.copies[4].wait_recv()
        self.add(self.part(i, 0), [self.slots.at[3], self.slots.at[4]])
        self.copies[2].wait_recv()
        self.copies[5].wait_recv()
        self.add(self.part(i, 1), [self.slots.at[2], self.slots.at[5]])

    def drain(self):
        for copy in self.copies:
            copy.wait_send()


def add_rows(target, others):
    total = target[...].astype(jnp.float32)
    for other in others:
        total = total + other[...].astype(jnp.float32)
    target[...] = total.astype(jnp.bfloat16)


def add_blocks(target, others):
    def one(k, _):
        a, b = k // 2, lax.rem(k, 2)
        add_rows(target.at[a, b], [o.at[a, b] for o in others])
        return 0

    lax.fori_loop(0, 4, one, 0)


class RingGather:
    def __init__(self, index, right, left, part, send, recv, base):
        i = index
        plan = [
            (part(i, None), right),
            (part(i, None), left),
            (part(wrap4(i - 1), 0), right),
            (part(wrap4(i + 1), 1), left),
        ]
        self.copies = [
            remote(src, src, send.at[base + n], recv.at[base + n], place)
            for n, (src, place) in enumerate(plan)
        ]

    def start(self):
        self.copies[0].start()
        self.copies[1].start()

    def middle(self):
        self.copies[0].wait_recv()
        self.copies[2].start()
        self.copies[1].wait_recv()
        self.copies[3].start()

    def finish(self):
        self.copies[2].wait_recv()
        self.copies[3].wait_recv()

    def drain(self):
        for copy in self.copies:
            copy.wait_send()


def layer_kernel(
    q_in, k_in, v_in, o_in, gain_in, ids_in, weights_in, gate_in, up_in, down_in, grad_in,
    layer_out, hidden_grad_out, gg_out, gu_out, gd_out,
    qs, kv, w, best, tot, acc, att, part_f, part_b, got,
    sel, sel_t, hidden_s, rows_s, grads_s, xr, cr, wg, wu, wd,
    act_g, act_u, act_b, act, xt, ct, grad, res, back, res_r, back_r,
    slots1_wide, slots1_slim, slots2_wide, slots2_slim, slot3_wide, slot3_slim,
    lsem, q_send, q_recv, w_send, w_recv, z_send, z_recv, g_send, g_recv, s_send, s_recv,
    a2a_local, a2a_send, a2a_recv, rs_send, rs_recv,
):
    ctx, e, x, y, z = mesh_place()
    f32, bf = jnp.float32, jnp.bfloat16
    seq, core = e // 2, lax.rem(e, 2)
    group, slot = e // 4, lax.rem(e, 4)
    head_cols = pl.ds(pl.multiple_of(core * HEAD_SIZE, HEAD_SIZE), HEAD_SIZE)
    own_k = pltpu.make_async_copy(k_in.at[seq, :, head_cols], kv.at[x, y, z, 0], lsem.at[0])
    own_v = pltpu.make_async_copy(v_in.at[seq, :, head_cols], kv.at[x, y, z, 1], lsem.at[1])
    own_k.start()
    own_v.start()
    weight_copies = [
        pltpu.make_async_copy(src, dst, lsem.at[2 + n])
        for n, (src, dst) in enumerate(((gate_in, wg), (up_in, wu), (down_in, wd)))
    ]
    greet(all_partners(ctx, e, x, y, z))

    x_right, x_left = {"ctx": ctx_of(wrap4(x + 1), y, z)}, {"ctx": ctx_of(wrap4(x - 1), y, z)}
    y_right, y_left = {"ctx": ctx_of(x, wrap4(y + 1), z)}, {"ctx": ctx_of(x, wrap4(y - 1), z)}

    def ring_x(base, part):
        return RingGather(x, x_right, x_left, part, g_send, g_recv, base)

    def ring_y(base, part):
        return RingGather(y, y_right, y_left, part, g_send, g_recv, base)

    def two(h):
        return slice(None) if h is None else pl.ds(2 * h, 2)

    kv_a1 = ring_x(0, lambda i, h: kv.at[i, y, 0] if h is None else kv.at[i, y, 0, h])
    kv_b1 = ring_y(4, lambda i, h: kv.at[x, i, 1] if h is None else kv.at[x, i, 1, h])
    kv_a2 = ring_y(8, lambda i, h: kv.at[two(h), i, 0])
    kv_b2 = ring_x(12, lambda i, h: kv.at[i, two(h), 1])
    w_a1 = ring_x(16, lambda i, h: w.at[pl.ds(0, 2), i, y] if h is None else w.at[h, i, y])
    w_b1 = ring_y(20, lambda i, h: w.at[pl.ds(2, 2), x, i] if h is None else w.at[2 + h, x, i])
    w_a2 = ring_y(24, lambda i, h: w.at[pl.ds(0, 2), :, i] if h is None else w.at[h, :, i])
    w_b2 = ring_x(28, lambda i, h: w.at[pl.ds(2, 2), i] if h is None else w.at[2 + h, i])
    z_partner = {"ctx": ctx_of(x, y, 1 - z)}
    z_copy = remote(kv.at[x, y, z], kv.at[x, y, z], z_send, z_recv, z_partner)

    own_k.wait()
    own_v.wait()
    z_copy.start()

    @pl.when(z == 0)
    def _():
        kv_a1.start()

    @pl.when(z == 1)
    def _():
        kv_b1.start()

    piece = pl.ds(pl.multiple_of((x * 4 + y) * 16, 16), 16)
    scatters = []
    for d in range(4):
        to = {"exp": 2 * lax.rem(seq + d, 4) + group}
        scatters.append((
            remote(
                q_in.at[lax.rem(seq + d, 4)], qs.at[slot], q_send.at[d], q_recv.at[slot], to
            ),
            remote(o_in.at[piece, :], w.at[slot, x, y], w_send.at[d], w_recv.at[slot], to),
        ))
    mine = core == group
    own_q = pltpu.make_async_copy(q_in.at[seq], qs.at[slot], q_recv.at[slot])
    own_w = pltpu.make_async_copy(o_in.at[piece, :], w.at[slot, x, y], w_recv.at[slot])
    for n, own in ((0, own_q), (1, own_w)):
        @pl.when(mine)
        def _():
            own.start()

        @pl.when(jnp.logical_not(mine))
        def _():
            scatters[0][n].start()

        for d in range(1, 4):
            scatters[d][n].start()
    for copy in weight_copies:
        copy.start()

    z_copy.wait_recv()

    @pl.when(z == 0)
    def _():
        kv_b1.start()

    @pl.when(z == 1)
    def _():
        kv_a1.start()

    def exchange(src, dst, number):
        own = pltpu.make_async_copy(src.at[e], dst.at[e], a2a_local.at[number])
        out = []
        for d in range(1, 8):
            to = lax.rem(e + d, 8)
            out.append(remote(
                src.at[to], dst.at[e],
                a2a_send.at[number, d], a2a_recv.at[number, d], {"exp": to},
            ))
        return own, out

    def begin(pair):
        own, out = pair
        for copy in out:
            copy.start()
        own.start()

    def arrive(pair):
        own, out = pair
        own.wait()
        for copy in out:
            copy.wait_recv()

    rows_x = exchange(rows_s, xr, 0)
    grads_x = exchange(grads_s, cr, 1)
    res_x = exchange(res, res_r, 2)
    back_x = exchange(back, back_r, 3)

    ids = ids_in[...]
    lanes = lax.broadcasted_iota(jnp.int32, (TOK, TOK), 1)
    chosen = (lanes == ids).astype(f32)
    before = (lanes < lax.broadcasted_iota(jnp.int32, (TOK, TOK), 0)).astype(bf)
    earlier = jnp.dot(before, chosen.astype(bf), preferred_element_type=f32)
    place = ids.astype(f32) * CAP + jnp.sum(earlier * chosen, axis=1, keepdims=True)
    slot_at = lax.broadcasted_iota(jnp.int32, (TOK, SLOTS), 1).astype(f32)
    taken = (slot_at == place).astype(f32)
    sel_t[...] = taken.astype(bf)
    sel[...] = taken.T.astype(bf)
    gates = weights_in[...]

    def dispatch(dst, value, n):
        cols = slice(n * 256, (n + 1) * 256)
        dst[:, :, cols] = jnp.dot(
            sel[...], value, preferred_element_type=f32
        ).astype(bf).reshape(8, CAP, 256)

    for n in range(8):
        cols = slice(n * 256, (n + 1) * 256)
        dispatch(grads_s, (grad_in[:, cols].astype(f32) * gates).astype(bf), n)
    begin(grads_x)

    kv_a1.middle()
    kv_b1.middle()
    kv_a1.finish()
    kv_a2.start()
    kv_b1.finish()
    kv_b2.start()
    for j in range(4):
        pltpu.make_async_copy(qs.at[j], qs.at[j], q_recv.at[j]).wait()

    scale = math.log2(math.e) / math.sqrt(HEAD_SIZE)
    over_last = (((1,), (1,)), ((), ()))

    def head_scores(h, key):
        t = h % 2
        query = qs[h // 2, :, t * HEAD_SIZE:(t + 1) * HEAD_SIZE]
        return lax.dot_general(query, key, over_last, preferred_element_type=f32) * scale

    def with_ones(value):
        return jnp.concatenate([value, jnp.ones(value.shape, bf)], axis=1)

    key, value = kv[x, y, z, 0], with_ones(kv[x, y, z, 1])
    below = lax.broadcasted_iota(jnp.int32, (256, 256), 1) <= lax.broadcasted_iota(
        jnp.int32, (256, 256), 0
    )
    for h in range(8):
        scores = jnp.where(below, head_scores(h, key), masked_score)
        top = jnp.max(scores, axis=1, keepdims=True)
        blended = jnp.dot(jnp.exp2(scores - top).astype(bf), value, preferred_element_type=f32)
        best[h] = jnp.broadcast_to(top, (256, HEAD_SIZE))
        acc[h] = blended[:, :HEAD_SIZE]
        tot[h] = blended[:, HEAD_SIZE:]

    def fold(places):
        key = jnp.concatenate([kv[bx, by, bz, 0] for bx, by, bz in places], axis=0)
        value = with_ones(jnp.concatenate([kv[bx, by, bz, 1] for bx, by, bz in places], axis=0))
        for h in range(8):
            scores = head_scores(h, key)
            old = best[h]
            new = jnp.maximum(old, jnp.max(scores, axis=1, keepdims=True))
            weights = jnp.exp2(scores - jnp.concatenate([new] * (2 * len(places)), axis=1))
            factor = jnp.exp2(old - new)
            blended = jnp.dot(weights.astype(bf), value, preferred_element_type=f32)
            best[h] = new
            acc[h] = acc[h] * factor + blended[:, :HEAD_SIZE]
            tot[h] = tot[h] * factor + blended[:, HEAD_SIZE:]

    def four(g):
        even = lax.rem(g, 2) == 0
        k = g // 2
        off = jnp.where(k == 2, -1, jnp.where(k == 3, 2, k))
        line = jnp.where(even, wrap4(y + off), wrap4(x + off))

        def at(i):
            return jnp.where(even, i, line), jnp.where(even, line, i), jnp.where(even, 0, 1)

        whole = ctx_of(*at(3)) < ctx

        @pl.when(whole)
        def _():
            fold([at(i) for i in range(4)])

        @pl.when(jnp.logical_not(whole))
        def _():
            def one(i, _):
                bx, by, bz = at(i)

                @pl.when(ctx_of(bx, by, bz) < ctx)
                def _():
                    fold([(bx, by, bz)])

                return 0

            lax.fori_loop(0, 4, one, 0)

    def line(g, _):
        @pl.when(g == 0)
        def _():
            for j in range(4):
                pltpu.make_async_copy(w.at[j, x, y], w.at[j, x, y], w_recv.at[j]).wait()
            w_a1.start()
            w_b1.start()

        @pl.when(g == 2)
        def _():
            kv_a2.middle()
            kv_b2.middle()
            w_a1.middle()
            w_b1.middle()

        @pl.when(g == 4)
        def _():
            w_a1.finish()
            w_a2.start()
            w_b1.finish()
            w_b2.start()

        @pl.when(g == 6)
        def _():
            kv_a2.finish()
            kv_b2.finish()

        @pl.when(g == 7)
        def _():
            w_a2.middle()
            w_b2.middle()

        four(g)
        return 0

    lax.fori_loop(0, 8, line, 0)

    for h in range(8):
        att[:, :, h * HEAD_SIZE:(h + 1) * HEAD_SIZE] = (
            (acc[h] / tot[h]).astype(bf).reshape(2, 128, HEAD_SIZE)
        )
    w_a2.finish()
    w_b2.finish()

    half = remote(part_b, got, s_send, s_recv, {"exp": e + 1 - 2 * core})

    def project(rows, n):
        cols = pl.ds(pl.multiple_of(n * 256, 256), 256)
        return cols, jnp.dot(
            rows, w[:, :, :, :, cols].reshape(1024, 256), preferred_element_type=f32
        )

    def theirs(n, _):
        cols, value = project(att[1 - core], n)
        part_b[:, cols] = value.astype(bf)
        return 0

    def ours(n, _):
        cols, value = project(att[core], n)
        part_f[:, cols] = value
        return 0

    lax.fori_loop(0, 8, theirs, 0)
    half.start()
    lax.fori_loop(0, 8, ours, 0)
    half.wait_recv()
    hidden_s[...] = (part_f[...] + got[...].astype(f32)).astype(bf)

    hidden_f = hidden_s[...].astype(f32)
    inv_rms = lax.rsqrt(jnp.mean(hidden_f * hidden_f, axis=1, keepdims=True) + epsilon)
    for n in range(8):
        cols = slice(n * 256, (n + 1) * 256)
        unit = hidden_s[:, cols].astype(f32) * inv_rms
        dispatch(rows_s, (unit * gain_in[:, cols]).astype(bf), n)
    begin(rows_x)

    for copy in weight_copies:
        copy.wait()
    arrive(grads_x)
    cot = cr[...].reshape(SLOTS, DM)
    ct[...] = cot.T
    for n in range(3):
        cols = slice(n * 256, (n + 1) * 256)
        act_b[:, cols] = lax.dot_general(cot, wd[cols, :], over_last, preferred_element_type=f32)

    arrive(rows_x)
    rows = xr[...].reshape(SLOTS, DM)
    for n in range(3):
        cols = slice(n * 256, (n + 1) * 256)
        act_g[:, cols] = jnp.dot(rows, wg[:, cols], preferred_element_type=f32)
        act_u[:, cols] = jnp.dot(rows, wu[:, cols], preferred_element_type=f32)
    xt[...] = rows.T
    for n in range(3):
        cols = slice(n * 256, (n + 1) * 256)
        gate_act, up_act, back_units = act_g[:, cols], act_u[:, cols], act_b[:, cols]
        sigma = jax.nn.sigmoid(gate_act)
        gated = gate_act * sigma
        act[:, 1536 + n * 256:1536 + (n + 1) * 256] = (gated * up_act).astype(bf)
        act[:, cols] = (
            back_units * up_act * sigma * (1.0 + gate_act * (1.0 - sigma))
        ).astype(bf)
        act[:, 768 + n * 256:768 + (n + 1) * 256] = (back_units * gated).astype(bf)

    chains = []
    for c, (first, width) in enumerate(CHAINS):
        cols = pl.ds(first, width)
        wide = c < 2
        slots1 = (slots1_wide if wide else slots1_slim).at[c % 2]
        slots2 = (slots2_wide if wide else slots2_slim).at[c % 2]
        slot3 = (slot3_wide if wide else slot3_slim).at[c % 2]
        base = 13 * c
        if c % 2 == 0:
            one = RingSum(
                x, x_right, x_left, lambda i, h, cols=cols: grad.at[i, pl.ds(2 * h, 2), :, :, cols],
                slots1, rs_send, rs_recv, base, add_blocks)
            second = RingSum(
                y, y_right, y_left, lambda i, h, cols=cols: grad.at[x, i, h, :, cols],
                slots2, rs_send, rs_recv, base + 6, add_rows)
        else:
            one = RingSum(
                y, y_right, y_left, lambda i, h, cols=cols: grad.at[pl.ds(2 * h, 2), i, :, :, cols],
                slots1, rs_send, rs_recv, base, add_blocks)
            second = RingSum(
                x, x_right, x_left, lambda i, h, cols=cols: grad.at[i, y, h, :, cols],
                slots2, rs_send, rs_recv, base + 6, add_rows)
        last = remote(
            grad.at[x, y, 1 - z, :, cols], slot3,
            rs_send.at[base + 12], rs_recv.at[base + 12], z_partner,
        )
        chains.append((one, second, last, slot3))

    def weight_grads(step):
        px, py = wrap4(x + step), wrap4(y + step)
        for k in range(2):
            some = pl.ds(pl.multiple_of(px * 512 + k * 256, 256), 256)
            grad[px, 2 * k:2 * k + 2, :, :, 0:1152] = jnp.dot(
                xt[some, :], act[:, 0:1152], preferred_element_type=f32
            ).astype(bf).reshape(2, 2, 64, 1152)
        for k in range(4):
            some = pl.ds(pl.multiple_of(k * 512 + py * 128, 128), 128)
            grad[k, py, :, :, 1152:1536] = jnp.dot(
                xt[some, :], act[:, 1152:1536], preferred_element_type=f32
            ).astype(bf).reshape(2, 64, 384)
            grad[k, py, :, :, 1536:2304] = jnp.dot(
                ct[some, :], act[:, 1536:2304], preferred_element_type=f32
            ).astype(bf).reshape(2, 64, 768)

    def launch(*chosen):
        for chain in chains:
            chain[0].start(*chosen)

    weight_grads(2)
    launch(0, 1)
    for n in range(8):
        cols = slice(n * 256, (n + 1) * 256)
        res[:, :, cols] = jnp.dot(
            act[:, 1536:], wd[:, cols], preferred_element_type=f32
        ).astype(bf).reshape(8, CAP, 256)
    begin(res_x)
    weight_grads(1)
    launch(2)
    weight_grads(-1)
    launch(3)
    weight_grads(0)
    for n in range(8):
        cols = slice(n * 256, (n + 1) * 256)
        back[:, :, cols] = (
            lax.dot_general(act[:, 0:768], wg[cols, :], over_last, preferred_element_type=f32)
            + lax.dot_general(act[:, 768:1536], wu[cols, :], over_last, preferred_element_type=f32)
        ).astype(bf).reshape(8, CAP, 256)
    begin(back_x)

    for chain in chains:
        chain[0].middle()
    for chain in chains:
        chain[0].finish()
        chain[1].start()

    arrive(res_x)
    returned = res_r[...].reshape(SLOTS, DM)
    for n in range(8):
        cols = slice(n * 256, (n + 1) * 256)
        expert_sum = gates * jnp.dot(sel_t[...], returned[:, cols], preferred_element_type=f32)
        layer_out[:, cols] = (hidden_s[:, cols].astype(f32) + expert_sum).astype(bf)

    for chain in chains:
        chain[1].middle()
    for chain in chains:
        chain[1].finish()
        chain[2].start()

    arrive(back_x)
    returned = back_r[...].reshape(SLOTS, DM)
    shared = jnp.zeros((TOK, 1), f32)
    for n in range(8):
        cols = slice(n * 256, (n + 1) * 256)
        scaled = gain_in[:, cols] * jnp.dot(
            sel_t[...], returned[:, cols], preferred_element_type=f32
        )
        part_f[:, cols] = scaled
        unit = hidden_s[:, cols].astype(f32) * inv_rms
        shared = shared + jnp.sum(scaled * unit, axis=1, keepdims=True)
    shared = shared * (1.0 / DM)
    for n in range(8):
        cols = slice(n * 256, (n + 1) * 256)
        unit = hidden_s[:, cols].astype(f32) * inv_rms
        hidden_grad_out[:, cols] = (
            grad_in[:, cols].astype(f32) + inv_rms * (part_f[:, cols] - unit * shared)
        ).astype(bf)

    for (first, width), (_, _, last, slot3) in zip(CHAINS, chains):
        cols = slice(first, first + width)
        last.wait_recv()
        part_f[0:64, cols.start % 1152:cols.start % 1152 + width] = (
            grad[x, y, z, :, cols].astype(f32) + slot3[...].astype(f32)
        )
        if first == 0:
            gg_out[:, 0:640] = part_f[0:64, 0:640]
        elif first == 640:
            gg_out[:, 640:768] = part_f[0:64, 640:768]
            gu_out[:, 0:384] = part_f[0:64, 768:1152]
        elif first == 1152:
            gu_out[:, 384:768] = part_f[0:64, 0:384]
            gd_out[:, 0:256] = part_f[0:64, 384:640]
        else:
            gd_out[:, 256:768] = part_f[0:64, 640:1152]

    half.wait_send()
    z_copy.wait_send()
    for ring in (kv_a1, kv_b1, kv_a2, kv_b2, w_a1, w_b1, w_a2, w_b2):
        ring.drain()
    for n in range(2):
        @pl.when(jnp.logical_not(mine))
        def _():
            scatters[0][n].wait_send()

        for d in range(1, 4):
            scatters[d][n].wait_send()
    for one, second, last, _ in chains:
        one.drain()
        second.drain()
        last.wait_send()
    for pair in (rows_x, grads_x, res_x, back_x):
        for copy in pair[1]:
            copy.wait_send()


def on_device(
    queries, rotated_key_heads, value_head_rows, out_proj, norm_gain, expert_ids,
    gate_weights, expert_gate, expert_up, expert_down, grad_out,
):
    bf, f32 = jnp.bfloat16, jnp.float32
    anywhere = pl.BlockSpec(memory_space=pl.ANY)
    vmem = pl.BlockSpec(memory_space=pltpu.VMEM)
    dma = pltpu.SemaphoreType.DMA
    rows = jax.ShapeDtypeStruct((TOK, DM), bf)
    shard = jax.ShapeDtypeStruct((64, F), f32)
    swapped = pltpu.VMEM((8, CAP, DM), bf)
    units = pltpu.VMEM((SLOTS, F), f32)
    state = pltpu.VMEM((8, 256, HEAD_SIZE), f32)
    layer, hidden_grad, gg, gu, gd = pl.pallas_call(
        layer_kernel,
        out_shape=(rows, rows, shard, shard, shard),
        in_specs=[anywhere] * 4 + [vmem] * 3 + [anywhere] * 3 + [vmem],
        out_specs=(vmem,) * 5,
        scratch_shapes=[
            pltpu.VMEM((4, 256, 256), bf),
            pltpu.VMEM((4, 4, 2, 2, 256, HEAD_SIZE), bf),
            pltpu.VMEM((4, 4, 4, 16, DM), bf),
            state, state, state,
            pltpu.VMEM((2, 128, 1024), bf),
            pltpu.VMEM((TOK, DM), f32),
            pltpu.VMEM((TOK, DM), bf),
            pltpu.VMEM((TOK, DM), bf),
            pltpu.VMEM((SLOTS, TOK), bf),
            pltpu.VMEM((TOK, SLOTS), bf),
            pltpu.VMEM((TOK, DM), bf),
            swapped, swapped, swapped, swapped,
            pltpu.VMEM((DM, F), bf),
            pltpu.VMEM((DM, F), bf),
            pltpu.VMEM((F, DM), bf),
            units, units, units,
            pltpu.VMEM((SLOTS, 3 * F), bf),
            pltpu.VMEM((DM, SLOTS), bf),
            pltpu.VMEM((DM, SLOTS), bf),
            pltpu.VMEM((4, 4, 2, 64, 3 * F), bf),
            swapped, swapped, swapped, swapped,
            pltpu.VMEM((2, 6, 2, 2, 64, 640), bf),
            pltpu.VMEM((2, 6, 2, 2, 64, 512), bf),
            pltpu.VMEM((2, 6, 64, 640), bf),
            pltpu.VMEM((2, 6, 64, 512), bf),
            pltpu.VMEM((2, 64, 640), bf),
            pltpu.VMEM((2, 64, 512), bf),
            dma((5,)), dma((4,)), dma((4,)), dma((4,)), dma((4,)),
            dma(()), dma(()), dma((32,)), dma((32,)), dma(()), dma(()),
            dma((4,)), dma((4, 8)), dma((4, 8)), dma((52,)), dma((52,)),
        ],
        compiler_params=pltpu.CompilerParams(
            collective_id=1, has_side_effects=True, vmem_limit_bytes=62 * 1024 * 1024
        ),
        name="layer",
    )(
        queries, rotated_key_heads, value_head_rows, out_proj, norm_gain[None], expert_ids,
        gate_weights, expert_gate[0], expert_up[0], expert_down[0], grad_out,
    )
    return (layer, hidden_grad, gg[None], gu[None], gd.T[None])


def solution(mesh):
    in_specs = (
        P(None, "ctx", "exp"),
        P(None, "ctx", None),
        P(None, "ctx", None),
        P("exp", None),
        P(),
        P(("ctx", "exp"), None),
        P(("ctx", "exp"), None),
        P("exp", None, None),
        P("exp", None, None),
        P("exp", None, None),
        P(("ctx", "exp"), None),
    )
    out_specs = (
        P(("ctx", "exp"), None),
        P(("ctx", "exp"), None),
        P("exp", "ctx", None),
        P("exp", "ctx", None),
        P("exp", None, "ctx"),
    )
    return jax.shard_map(
        on_device, mesh=mesh, in_specs=in_specs, out_specs=out_specs, check_vma=False
    )
```

```python
import math

import jax
import jax.numpy as jnp
from jax import lax
from jax.experimental import pallas as pl
from jax.experimental.pallas import tpu as pltpu
from jax.sharding import PartitionSpec as P

MESH = pl.DeviceIdType.MESH
HEAD_SIZE = 128
F = 768
DM = 2048
CAP = 32
SLOTS = 8 * CAP
TOK = 128
CHAINS = ((0, 640), (1152, 640), (640, 512), (1792, 512))

epsilon = 1e-06
masked_score = -1e30


def mesh_place():
    ctx = lax.axis_index("ctx")
    e = lax.axis_index("exp")
    x = ctx // 8
    y = lax.rem(ctx // 2, 4)
    z = lax.rem(ctx, 2)
    return ctx, e, x, y, z


def ctx_of(x, y, z):
    return x * 8 + y * 2 + z


def wrap4(i):
    return lax.rem(i + 4, 4)


def greet(partners):
    barrier = pltpu.get_barrier_semaphore()
    for place in partners:
        pl.semaphore_signal(barrier, inc=1, device_id=place, device_id_type=MESH)
    pl.semaphore_wait(barrier, len(partners))


def all_partners(ctx, e, x, y, z):
    found = [{"exp": lax.rem(e + d, 8)} for d in range(1, 8)]
    found += [{"ctx": ctx_of(wrap4(x + d), y, z)} for d in (1, -1)]
    found += [{"ctx": ctx_of(x, wrap4(y + d), z)} for d in (1, -1)]
    found += [{"ctx": ctx_of(x, y, 1 - z)}]
    return found


def remote(src, dst, send, recv, place):
    return pltpu.make_async_remote_copy(
        src_ref=src, dst_ref=dst, send_sem=send, recv_sem=recv,
        device_id=place, device_id_type=MESH,
    )


class RingSum:
    def __init__(self, index, right, left, part, slots, send, recv, base, add):
        self.i, self.part, self.slots, self.add = index, part, slots, add
        i = index
        plan = [
            (part(wrap4(i + 2), 0), right),
            (part(wrap4(i + 2), 1), left),
            (part(wrap4(i + 1), 1), right),
            (part(wrap4(i - 1), 0), left),
            (part(wrap4(i + 1), 0), right),
            (part(wrap4(i - 1), 1), left),
        ]
        self.copies = [
            remote(src, slots.at[n], send.at[base + n], recv.at[base + n], place)
            for n, (src, place) in enumerate(plan)
        ]

    def start(self, *chosen):
        for n in chosen or range(4):
            self.copies[n].start()

    def middle(self):
        i = self.i
        self.copies[0].wait_recv()
        self.add(self.part(wrap4(i + 1), 0), [self.slots.at[0]])
        self.copies[4].start()
        self.copies[1].wait_recv()
        self.add(self.part(wrap4(i - 1), 1), [self.slots.at[1]])
        self.copies[5].start()

    def finish(self):
        i = self.i
        self.copies[3].wait_recv()
        self.copies[4].wait_recv()
        self.add(self.part(i, 0), [self.slots.at[3], self.slots.at[4]])
        self.copies[2].wait_recv()
        self.copies[5].wait_recv()
        self.add(self.part(i, 1), [self.slots.at[2], self.slots.at[5]])

    def drain(self):
        for copy in self.copies:
            copy.wait_send()


def add_rows(target, others):
    total = target[...].astype(jnp.float32)
    for other in others:
        total = total + other[...].astype(jnp.float32)
    target[...] = total.astype(jnp.bfloat16)


def add_blocks(target, others):
    def one(k, _):
        a, b = k // 2, lax.rem(k, 2)
        add_rows(target.at[a, b], [o.at[a, b] for o in others])
        return 0

    lax.fori_loop(0, 4, one, 0)


class RingGather:
    def __init__(self, index, right, left, part, send, recv, base):
        i = index
        plan = [
            (part(i, None), right),
            (part(i, None), left),
            (part(wrap4(i - 1), 0), right),
            (part(wrap4(i + 1), 1), left),
        ]
        self.copies = [
            remote(src, src, send.at[base + n], recv.at[base + n], place)
            for n, (src, place) in enumerate(plan)
        ]

    def start(self):
        self.copies[0].start()
        self.copies[1].start()

    def middle(self):
        self.copies[0].wait_recv()
        self.copies[2].start()
        self.copies[1].wait_recv()
        self.copies[3].start()

    def finish(self):
        self.copies[2].wait_recv()
        self.copies[3].wait_recv()

    def drain(self):
        for copy in self.copies:
            copy.wait_send()


def layer_kernel(
    q_in, k_in, v_in, o_in, gain_in, ids_in, weights_in, gate_in, up_in, down_in, grad_in,
    layer_out, hidden_grad_out, gg_out, gu_out, gd_out,
    qs, kv, w, best, tot, acc, att, part_f, part_b, got,
    sel, sel_t, hidden_s, rows_s, grads_s, inv_s, inv_r, xr, cr, wg, wu, wd,
    act_g, act_u, act_b, act, act_back, xt, ct, grad, res, back, res_r, back_r,
    slots1_wide, slots1_slim, slots2_wide, slots2_slim, slot3_wide, slot3_slim,
    lsem, q_send, q_recv, w_send, w_recv, z_send, z_recv, g_send, g_recv, s_send, s_recv,
    a2a_local, a2a_send, a2a_recv, r_local, r_send, r_recv, rs_send, rs_recv,
):
    ctx, e, x, y, z = mesh_place()
    f32, bf = jnp.float32, jnp.bfloat16
    seq, core = e // 2, lax.rem(e, 2)
    group, slot = e // 4, lax.rem(e, 4)
    head_cols = pl.ds(pl.multiple_of(core * HEAD_SIZE, HEAD_SIZE), HEAD_SIZE)
    own_k = pltpu.make_async_copy(k_in.at[seq, :, head_cols], kv.at[x, y, z, 0], lsem.at[0])
    own_v = pltpu.make_async_copy(v_in.at[seq, :, head_cols], kv.at[x, y, z, 1], lsem.at[1])
    own_k.start()
    own_v.start()
    weight_copies = [
        pltpu.make_async_copy(src, dst, lsem.at[2 + n])
        for n, (src, dst) in enumerate(((gate_in, wg), (up_in, wu), (down_in, wd)))
    ]
    greet(all_partners(ctx, e, x, y, z))

    x_right, x_left = {"ctx": ctx_of(wrap4(x + 1), y, z)}, {"ctx": ctx_of(wrap4(x - 1), y, z)}
    y_right, y_left = {"ctx": ctx_of(x, wrap4(y + 1), z)}, {"ctx": ctx_of(x, wrap4(y - 1), z)}

    def ring_x(base, part):
        return RingGather(x, x_right, x_left, part, g_send, g_recv, base)

    def ring_y(base, part):
        return RingGather(y, y_right, y_left, part, g_send, g_recv, base)

    def two(h):
        return slice(None) if h is None else pl.ds(2 * h, 2)

    kv_a1 = ring_x(0, lambda i, h: kv.at[i, y, 0] if h is None else kv.at[i, y, 0, h])
    kv_b1 = ring_y(4, lambda i, h: kv.at[x, i, 1] if h is None else kv.at[x, i, 1, h])
    kv_a2 = ring_y(8, lambda i, h: kv.at[two(h), i, 0])
    kv_b2 = ring_x(12, lambda i, h: kv.at[i, two(h), 1])
    w_a1 = ring_x(16, lambda i, h: w.at[pl.ds(0, 2), i, y] if h is None else w.at[h, i, y])
    w_b1 = ring_y(20, lambda i, h: w.at[pl.ds(2, 2), x, i] if h is None else w.at[2 + h, x, i])
    w_a2 = ring_y(24, lambda i, h: w.at[pl.ds(0, 2), :, i] if h is None else w.at[h, :, i])
    w_b2 = ring_x(28, lambda i, h: w.at[pl.ds(2, 2), i] if h is None else w.at[2 + h, i])
    z_partner = {"ctx": ctx_of(x, y, 1 - z)}
    z_copy = remote(kv.at[x, y, z], kv.at[x, y, z], z_send, z_recv, z_partner)

    own_k.wait()
    own_v.wait()
    z_copy.start()

    @pl.when(z == 0)
    def _():
        kv_a1.start()

    @pl.when(z == 1)
    def _():
        kv_b1.start()

    piece = pl.ds(pl.multiple_of((x * 4 + y) * 16, 16), 16)
    scatters = []
    for d in range(4):
        to = {"exp": 2 * lax.rem(seq + d, 4) + group}
        scatters.append((
            remote(
                q_in.at[lax.rem(seq + d, 4)], qs.at[slot], q_send.at[d], q_recv.at[slot], to
            ),
            remote(o_in.at[piece, :], w.at[slot, x, y], w_send.at[d], w_recv.at[slot], to),
        ))
    mine = core == group
    own_q = pltpu.make_async_copy(q_in.at[seq], qs.at[slot], q_recv.at[slot])
    own_w = pltpu.make_async_copy(o_in.at[piece, :], w.at[slot, x, y], w_recv.at[slot])
    for n, own in ((1, own_w), (0, own_q)):
        @pl.when(mine)
        def _():
            own.start()

        @pl.when(jnp.logical_not(mine))
        def _():
            scatters[0][n].start()

        for d in range(1, 4):
            scatters[d][n].start()
    for copy in weight_copies:
        copy.start()

    z_copy.wait_recv()

    @pl.when(z == 0)
    def _():
        kv_b1.start()

    @pl.when(z == 1)
    def _():
        kv_a1.start()

    def exchange(src, dst, number):
        own = pltpu.make_async_copy(src.at[e], dst.at[e], a2a_local.at[number])
        out = []
        for d in range(1, 8):
            to = lax.rem(e + d, 8)
            out.append(remote(
                src.at[to], dst.at[e],
                a2a_send.at[number, d], a2a_recv.at[number, d], {"exp": to},
            ))
        return own, out

    def begin(pair):
        own, out = pair
        for copy in out:
            copy.start()
        own.start()

    def arrive(pair):
        own, out = pair
        own.wait()
        for copy in out:
            copy.wait_recv()

    grads_x = exchange(grads_s, cr, 1)
    res_x = exchange(res, res_r, 2)
    back_x = exchange(back, back_r, 3)

    ids = ids_in[...]
    chosen = (lax.broadcasted_iota(jnp.int32, (16, TOK), 0) == ids).astype(f32)
    rows_at = lax.broadcasted_iota(jnp.int32, (TOK, TOK), 0)
    lanes_at = lax.broadcasted_iota(jnp.int32, (TOK, TOK), 1)
    before = (rows_at < lanes_at).astype(bf)
    earlier = jnp.dot(chosen.astype(bf), before, preferred_element_type=f32)
    place = ids.astype(f32) * CAP + jnp.sum(earlier * chosen, axis=0, keepdims=True)
    slot_at = lax.broadcasted_iota(jnp.int32, (SLOTS, TOK), 0).astype(f32)
    taken = (slot_at == place).astype(f32)
    sel[...] = taken.astype(bf)
    sel_t[...] = taken.T.astype(bf)
    gates = jnp.sum(jnp.where(rows_at == lanes_at, weights_in[...], 0.0), axis=1, keepdims=True)

    def dispatch(dst, value, first):
        width = value.shape[1]
        dst[:, :, first:first + width] = jnp.dot(
            sel[...], value, preferred_element_type=f32
        ).astype(bf).reshape(8, CAP, width)

    kv_a1.middle()
    kv_b1.middle()
    kv_a1.finish()
    kv_a2.start()
    kv_b1.finish()
    kv_b2.start()
    for j in range(4):
        pltpu.make_async_copy(w.at[j, x, y], w.at[j, x, y], w_recv.at[j]).wait()
    w_a1.start()
    w_b1.start()
    for n in range(8):
        cols = slice(n * 256, (n + 1) * 256)
        dispatch(grads_s, (grad_in[:, cols].astype(f32) * gates).astype(bf), n * 256)
    begin(grads_x)
    for j in range(4):
        pltpu.make_async_copy(qs.at[j], qs.at[j], q_recv.at[j]).wait()

    scale = math.log2(math.e) / math.sqrt(HEAD_SIZE)
    over_last = (((1,), (1,)), ((), ()))

    def head_scores(h, key):
        t = h % 2
        query = qs[h // 2, :, t * HEAD_SIZE:(t + 1) * HEAD_SIZE]
        return lax.dot_general(query, key, over_last, preferred_element_type=f32) * scale

    def with_ones(value):
        return jnp.concatenate([value, jnp.ones(value.shape, bf)], axis=1)

    key, value = kv[x, y, z, 0], with_ones(kv[x, y, z, 1])
    below = lax.broadcasted_iota(jnp.int32, (256, 256), 1) <= lax.broadcasted_iota(
        jnp.int32, (256, 256), 0
    )
    for h in range(8):
        scores = jnp.where(below, head_scores(h, key), masked_score)
        top = jnp.max(scores, axis=1, keepdims=True)
        blended = jnp.dot(jnp.exp2(scores - top).astype(bf), value, preferred_element_type=f32)
        best[h] = jnp.broadcast_to(top, (256, HEAD_SIZE))
        acc[h] = blended[:, :HEAD_SIZE]
        tot[h] = blended[:, HEAD_SIZE:]

    def fold(places):
        key = jnp.concatenate([kv[bx, by, bz, 0] for bx, by, bz in places], axis=0)
        value = with_ones(jnp.concatenate([kv[bx, by, bz, 1] for bx, by, bz in places], axis=0))
        for h in range(8):
            scores = head_scores(h, key)
            old = best[h]
            new = jnp.maximum(old, jnp.max(scores, axis=1, keepdims=True))
            weights = jnp.exp2(scores - jnp.concatenate([new] * (2 * len(places)), axis=1))
            factor = jnp.exp2(old - new)
            blended = jnp.dot(weights.astype(bf), value, preferred_element_type=f32)
            best[h] = new
            acc[h] = acc[h] * factor + blended[:, :HEAD_SIZE]
            tot[h] = tot[h] * factor + blended[:, HEAD_SIZE:]

    def four(g):
        even = lax.rem(g, 2) == 0
        k = g // 2
        off = jnp.where(k == 2, -1, jnp.where(k == 3, 2, k))
        line = jnp.where(even, wrap4(y + off), wrap4(x + off))

        def at(i):
            return jnp.where(even, i, line), jnp.where(even, line, i), jnp.where(even, 0, 1)

        whole = ctx_of(*at(3)) < ctx

        @pl.when(whole)
        def _():
            fold([at(i) for i in range(4)])

        @pl.when(jnp.logical_not(whole))
        def _():
            def one(i, _):
                bx, by, bz = at(i)

                @pl.when(ctx_of(bx, by, bz) < ctx)
                def _():
                    fold([(bx, by, bz)])

                return 0

            lax.fori_loop(0, 4, one, 0)

    w_a1.middle()
    w_b1.middle()

    def line(g, _):
        @pl.when(g == 2)
        def _():
            w_a1.finish()
            w_b1.finish()
            kv_a2.middle()
            kv_b2.middle()
            w_a2.start()
            w_b2.start()

        @pl.when(g == 6)
        def _():
            kv_a2.finish()
            kv_b2.finish()

        @pl.when(g == 7)
        def _():
            w_a2.middle()
            w_b2.middle()

        four(g)
        return 0

    lax.fori_loop(0, 8, line, 0)

    for h in range(8):
        att[:, :, h * HEAD_SIZE:(h + 1) * HEAD_SIZE] = (
            (acc[h] / tot[h]).astype(bf).reshape(2, 128, HEAD_SIZE)
        )
    w_a2.finish()
    w_b2.finish()

    sibling = {"exp": e + 1 - 2 * core}
    halves, row_copies = [], []
    for n in range(4):
        cols = pl.ds(n * 512, 512)
        halves.append(remote(
            part_b.at[:, cols], got.at[:, cols], s_send.at[n], s_recv.at[n], sibling
        ))
        own_rows = pltpu.make_async_copy(
            rows_s.at[e, :, cols], xr.at[e, :, cols], r_local.at[n]
        )
        out = []
        for d in range(1, 8):
            to = lax.rem(e + d, 8)
            out.append(remote(
                rows_s.at[to, :, cols], xr.at[e, :, cols],
                r_send.at[n, d], r_recv.at[n, d], {"exp": to},
            ))
        row_copies.append((own_rows, out))

    def project(rows, first):
        return jnp.dot(
            rows, w[:, :, :, :, first:first + 256].reshape(1024, 256), preferred_element_type=f32
        )

    for n in range(4):
        for first in (n * 512, n * 512 + 256):
            part_b[:, first:first + 256] = project(att[1 - core], first).astype(bf)
        halves[n].start()
    squares = jnp.zeros((TOK, 1), f32)
    for n in range(4):
        cols = slice(n * 512, (n + 1) * 512)
        for first in (n * 512, n * 512 + 256):
            part_f[:, first:first + 256] = project(att[core], first)
        halves[n].wait_recv()
        hidden = (part_f[:, cols] + got[:, cols].astype(f32)).astype(bf)
        hidden_s[:, cols] = hidden
        hidden = hidden.astype(f32)
        squares = squares + jnp.sum(hidden * hidden, axis=1, keepdims=True)
        dispatch(rows_s, (hidden * gain_in[:, cols]).astype(bf), n * 512)
        begin(row_copies[n])
    inv_rms = lax.rsqrt(squares * (1.0 / DM) + epsilon)
    inv_row = jnp.broadcast_to(inv_rms, (TOK, TOK)).T[0:1, :]
    inv_slots = jnp.sum(sel[...].astype(f32) * inv_row, axis=1, keepdims=True)
    inv_s[...] = jnp.broadcast_to(inv_slots, (SLOTS, 128)).reshape(8, CAP, 128)
    inv_x = exchange(inv_s, inv_r, 0)
    begin(inv_x)

    for copy in weight_copies:
        copy.wait()
    arrive(grads_x)
    cot = cr[...].reshape(SLOTS, DM)
    ct[...] = cot.T
    for n in range(3):
        cols = slice(n * 256, (n + 1) * 256)
        act_b[:, cols] = lax.dot_general(cot, wd[cols, :], over_last, preferred_element_type=f32)

    for pair in row_copies:
        arrive(pair)
    arrive(inv_x)
    inv_in = inv_r[...].reshape(SLOTS, 128)[:, 0:1]
    rows = xr[...].reshape(SLOTS, DM)
    for n in range(3):
        cols = slice(n * 256, (n + 1) * 256)
        act_g[:, cols] = jnp.dot(rows, wg[:, cols], preferred_element_type=f32) * inv_in
        act_u[:, cols] = jnp.dot(rows, wu[:, cols], preferred_element_type=f32) * inv_in
    xt[...] = rows.T
    for n in range(3):
        cols = slice(n * 256, (n + 1) * 256)
        gate_act, up_act, back_units = act_g[:, cols], act_u[:, cols], act_b[:, cols]
        sigma = jax.nn.sigmoid(gate_act)
        gated = gate_act * sigma
        act[:, 1536 + n * 256:1536 + (n + 1) * 256] = (gated * up_act).astype(bf)
        back_gate = back_units * up_act * sigma * (1.0 + gate_act * (1.0 - sigma))
        back_up = back_units * gated
        act[:, cols] = (back_gate * inv_in).astype(bf)
        act[:, 768 + n * 256:768 + (n + 1) * 256] = (back_up * inv_in).astype(bf)
        act_back[:, cols] = back_gate.astype(bf)
        act_back[:, 768 + n * 256:768 + (n + 1) * 256] = back_up.astype(bf)

    chains = []
    for c, (first, width) in enumerate(CHAINS):
        cols = pl.ds(first, width)
        wide = c < 2
        slots1 = (slots1_wide if wide else slots1_slim).at[c % 2]
        slots2 = (slots2_wide if wide else slots2_slim).at[c % 2]
        slot3 = (slot3_wide if wide else slot3_slim).at[c % 2]
        base = 13 * c
        if c % 2 == 0:
            one = RingSum(
                x, x_right, x_left, lambda i, h, cols=cols: grad.at[i, pl.ds(2 * h, 2), :, :, cols],
                slots1, rs_send, rs_recv, base, add_blocks)
            second = RingSum(
                y, y_right, y_left, lambda i, h, cols=cols: grad.at[x, i, h, :, cols],
                slots2, rs_send, rs_recv, base + 6, add_rows)
        else:
            one = RingSum(
                y, y_right, y_left, lambda i, h, cols=cols: grad.at[pl.ds(2 * h, 2), i, :, :, cols],
                slots1, rs_send, rs_recv, base, add_blocks)
            second = RingSum(
                x, x_right, x_left, lambda i, h, cols=cols: grad.at[i, y, h, :, cols],
                slots2, rs_send, rs_recv, base + 6, add_rows)
        last = remote(
            grad.at[x, y, 1 - z, :, cols], slot3,
            rs_send.at[base + 12], rs_recv.at[base + 12], z_partner,
        )
        chains.append((one, second, last, slot3))

    def weight_grads(step):
        px, py = wrap4(x + step), wrap4(y + step)
        for k in range(2):
            some = pl.ds(pl.multiple_of(px * 512 + k * 256, 256), 256)
            grad[px, 2 * k:2 * k + 2, :, :, 0:1152] = jnp.dot(
                xt[some, :], act[:, 0:1152], preferred_element_type=f32
            ).astype(bf).reshape(2, 2, 64, 1152)
        for k in range(4):
            some = pl.ds(pl.multiple_of(k * 512 + py * 128, 128), 128)
            grad[k, py, :, :, 1152:1536] = jnp.dot(
                xt[some, :], act[:, 1152:1536], preferred_element_type=f32
            ).astype(bf).reshape(2, 64, 384)
            grad[k, py, :, :, 1536:2304] = jnp.dot(
                ct[some, :], act[:, 1536:2304], preferred_element_type=f32
            ).astype(bf).reshape(2, 64, 768)

    def launch(*chosen):
        for chain in chains:
            chain[0].start(*chosen)

    weight_grads(2)
    launch(0, 1)
    for n in range(8):
        cols = slice(n * 256, (n + 1) * 256)
        res[:, :, cols] = jnp.dot(
            act[:, 1536:], wd[:, cols], preferred_element_type=f32
        ).astype(bf).reshape(8, CAP, 256)
    begin(res_x)
    weight_grads(1)
    launch(2)
    weight_grads(-1)
    launch(3)
    weight_grads(0)
    for n in range(8):
        cols = slice(n * 256, (n + 1) * 256)
        back[:, :, cols] = (
            lax.dot_general(act_back[:, 0:768], wg[cols, :], over_last, preferred_element_type=f32)
            + lax.dot_general(act_back[:, 768:1536], wu[cols, :], over_last, preferred_element_type=f32)
        ).astype(bf).reshape(8, CAP, 256)
    begin(back_x)

    for chain in chains:
        chain[0].middle()
    for chain in chains:
        chain[0].finish()
        chain[1].start()

    arrive(res_x)
    returned = res_r[...].reshape(SLOTS, DM)
    for n in range(8):
        cols = slice(n * 256, (n + 1) * 256)
        expert_sum = gates * jnp.dot(sel_t[...], returned[:, cols], preferred_element_type=f32)
        layer_out[:, cols] = (hidden_s[:, cols].astype(f32) + expert_sum).astype(bf)

    for chain in chains:
        chain[1].middle()
    for chain in chains:
        chain[1].finish()
        chain[2].start()

    arrive(back_x)
    returned = back_r[...].reshape(SLOTS, DM)
    shared = jnp.zeros((TOK, 1), f32)
    for n in range(8):
        cols = slice(n * 256, (n + 1) * 256)
        scaled = gain_in[:, cols] * jnp.dot(
            sel_t[...], returned[:, cols], preferred_element_type=f32
        )
        part_f[:, cols] = scaled
        unit = hidden_s[:, cols].astype(f32) * inv_rms
        shared = shared + jnp.sum(scaled * unit, axis=1, keepdims=True)
    shared = shared * (1.0 / DM)
    for n in range(8):
        cols = slice(n * 256, (n + 1) * 256)
        unit = hidden_s[:, cols].astype(f32) * inv_rms
        hidden_grad_out[:, cols] = (
            grad_in[:, cols].astype(f32) + inv_rms * (part_f[:, cols] - unit * shared)
        ).astype(bf)

    for (first, width), (_, _, last, slot3) in zip(CHAINS, chains):
        cols = slice(first, first + width)
        last.wait_recv()
        part_f[0:64, cols.start % 1152:cols.start % 1152 + width] = (
            grad[x, y, z, :, cols].astype(f32) + slot3[...].astype(f32)
        )
        if first == 0:
            gg_out[:, 0:640] = part_f[0:64, 0:640]
        elif first == 640:
            gg_out[:, 640:768] = part_f[0:64, 640:768]
            gu_out[:, 0:384] = part_f[0:64, 768:1152]
        elif first == 1152:
            gu_out[:, 384:768] = part_f[0:64, 0:384]
            gd_out[:, 0:256] = part_f[0:64, 384:640]
        else:
            gd_out[:, 256:768] = part_f[0:64, 640:1152]

    for half in halves:
        half.wait_send()
    z_copy.wait_send()
    for ring in (kv_a1, kv_b1, kv_a2, kv_b2, w_a1, w_b1, w_a2, w_b2):
        ring.drain()
    for n in range(2):
        @pl.when(jnp.logical_not(mine))
        def _():
            scatters[0][n].wait_send()

        for d in range(1, 4):
            scatters[d][n].wait_send()
    for one, second, last, _ in chains:
        one.drain()
        second.drain()
        last.wait_send()
    for pair in row_copies + [inv_x, grads_x, res_x, back_x]:
        for copy in pair[1]:
            copy.wait_send()


def hand_over(*refs):
    sems = refs[10]
    copies = [
        pltpu.make_async_copy(src, dst, sems.at[n])
        for n, (src, dst) in enumerate(zip(refs[:5], refs[5:10]))
    ]
    for copy in copies:
        copy.start()
    for copy in copies:
        copy.wait()


def on_device(
    queries, rotated_key_heads, value_head_rows, out_proj, norm_gain, expert_ids,
    gate_weights, expert_gate, expert_up, expert_down, grad_out,
):
    bf, f32 = jnp.bfloat16, jnp.float32
    anywhere = pl.BlockSpec(memory_space=pl.ANY)
    vmem = pl.BlockSpec(memory_space=pltpu.VMEM)
    dma = pltpu.SemaphoreType.DMA
    rows = jax.ShapeDtypeStruct((TOK, DM), bf)
    shard = jax.ShapeDtypeStruct((64, F), f32)
    swapped = pltpu.VMEM((8, CAP, DM), bf)
    units = pltpu.VMEM((SLOTS, F), f32)
    state = pltpu.VMEM((8, 256, HEAD_SIZE), f32)
    layer, hidden_grad, gg, gu, gd = pl.pallas_call(
        layer_kernel,
        out_shape=(rows, rows, shard, shard, shard),
        in_specs=[anywhere] * 4 + [vmem] * 3 + [anywhere] * 3 + [vmem],
        out_specs=(vmem,) * 5,
        scratch_shapes=[
            pltpu.VMEM((4, 256, 256), bf),
            pltpu.VMEM((4, 4, 2, 2, 256, HEAD_SIZE), bf),
            pltpu.VMEM((4, 4, 4, 16, DM), bf),
            state, state, state,
            pltpu.VMEM((2, 128, 1024), bf),
            pltpu.VMEM((TOK, DM), f32),
            pltpu.VMEM((TOK, DM), bf),
            pltpu.VMEM((TOK, DM), bf),
            pltpu.VMEM((SLOTS, TOK), bf),
            pltpu.VMEM((TOK, SLOTS), bf),
            pltpu.VMEM((TOK, DM), bf),
            swapped, swapped,
            pltpu.VMEM((8, CAP, 128), f32),
            pltpu.VMEM((8, CAP, 128), f32),
            swapped, swapped,
            pltpu.VMEM((DM, F), bf),
            pltpu.VMEM((DM, F), bf),
            pltpu.VMEM((F, DM), bf),
            units, units, units,
            pltpu.VMEM((SLOTS, 3 * F), bf),
            pltpu.VMEM((SLOTS, 2 * F), bf),
            pltpu.VMEM((DM, SLOTS), bf),
            pltpu.VMEM((DM, SLOTS), bf),
            pltpu.VMEM((4, 4, 2, 64, 3 * F), bf),
            swapped, swapped, swapped, swapped,
            pltpu.VMEM((2, 6, 2, 2, 64, 640), bf),
            pltpu.VMEM((2, 6, 2, 2, 64, 512), bf),
            pltpu.VMEM((2, 6, 64, 640), bf),
            pltpu.VMEM((2, 6, 64, 512), bf),
            pltpu.VMEM((2, 64, 640), bf),
            pltpu.VMEM((2, 64, 512), bf),
            dma((5,)), dma((4,)), dma((4,)), dma((4,)), dma((4,)),
            dma(()), dma(()), dma((32,)), dma((32,)), dma((4,)), dma((4,)),
            dma((4,)), dma((4, 8)), dma((4, 8)), dma((4,)), dma((4, 8)), dma((4, 8)),
            dma((52,)), dma((52,)),
        ],
        compiler_params=pltpu.CompilerParams(
            collective_id=1, has_side_effects=True, vmem_limit_bytes=62 * 1024 * 1024
        ),
        name="layer",
    )(
        queries, rotated_key_heads, value_head_rows, out_proj, norm_gain[None],
        expert_ids.reshape(1, TOK), gate_weights.reshape(1, TOK), expert_gate[0], expert_up[0], expert_down[0], grad_out,
    )
    shapes = (rows, rows, shard, shard, shard)
    layer, hidden_grad, gg, gu, gd = pl.pallas_call(
        hand_over,
        out_shape=shapes,
        in_specs=[anywhere] * 5,
        out_specs=[anywhere] * 5,
        scratch_shapes=[dma((5,))],
        compiler_params=pltpu.CompilerParams(vmem_limit_bytes=62 * 1024 * 1024),
        name="hand_over",
    )(layer, hidden_grad, gg, gu, gd)
    return (layer, hidden_grad, gg[None], gu[None], gd.T[None])


def solution(mesh):
    in_specs = (
        P(None, "ctx", "exp"),
        P(None, "ctx", None),
        P(None, "ctx", None),
        P("exp", None),
        P(),
        P(("ctx", "exp"), None),
        P(("ctx", "exp"), None),
        P("exp", None, None),
        P("exp", None, None),
        P("exp", None, None),
        P(("ctx", "exp"), None),
    )
    out_specs = (
        P(("ctx", "exp"), None),
        P(("ctx", "exp"), None),
        P("exp", "ctx", None),
        P("exp", "ctx", None),
        P("exp", None, "ctx"),
    )
    return jax.shard_map(
        on_device, mesh=mesh, in_specs=in_specs, out_specs=out_specs, check_vma=False
    )
```

```python
import math

import jax
import jax.numpy as jnp
from jax import lax
from jax.experimental import pallas as pl
from jax.experimental.pallas import tpu as pltpu
from jax.sharding import PartitionSpec as P

MESH = pl.DeviceIdType.MESH
HEAD_SIZE = 128
F = 768
DM = 2048
CAP = 32
SLOTS = 8 * CAP
TOK = 128
CHAINS = ((0, 640), (1152, 640), (640, 512), (1792, 512))

epsilon = 1e-06
masked_score = -1e30


def mesh_place():
    ctx = lax.axis_index("ctx")
    e = lax.axis_index("exp")
    x = ctx // 8
    y = lax.rem(ctx // 2, 4)
    z = lax.rem(ctx, 2)
    return ctx, e, x, y, z


def ctx_of(x, y, z):
    return x * 8 + y * 2 + z


def wrap4(i):
    return lax.rem(i + 4, 4)


def greet(partners):
    barrier = pltpu.get_barrier_semaphore()
    for place in partners:
        pl.semaphore_signal(barrier, inc=1, device_id=place, device_id_type=MESH)
    pl.semaphore_wait(barrier, len(partners))


def all_partners(ctx, e, x, y, z):
    found = [{"exp": lax.rem(e + d, 8)} for d in range(1, 8)]
    found += [{"ctx": ctx_of(wrap4(x + d), y, z)} for d in (1, -1)]
    found += [{"ctx": ctx_of(x, wrap4(y + d), z)} for d in (1, -1)]
    found += [{"ctx": ctx_of(x, y, 1 - z)}]
    return found


def remote(src, dst, send, recv, place):
    return pltpu.make_async_remote_copy(
        src_ref=src, dst_ref=dst, send_sem=send, recv_sem=recv,
        device_id=place, device_id_type=MESH,
    )


class RingSum:
    def __init__(self, index, right, left, part, slots, send, recv, base, add):
        self.i, self.part, self.slots, self.add = index, part, slots, add
        i = index
        plan = [
            (part(wrap4(i + 2), 0), right),
            (part(wrap4(i + 2), 1), left),
            (part(wrap4(i + 1), 1), right),
            (part(wrap4(i - 1), 0), left),
            (part(wrap4(i + 1), 0), right),
            (part(wrap4(i - 1), 1), left),
        ]
        self.copies = [
            remote(src, slots.at[n], send.at[base + n], recv.at[base + n], place)
            for n, (src, place) in enumerate(plan)
        ]

    def start(self, *chosen):
        for n in chosen or range(4):
            self.copies[n].start()

    def middle(self):
        i = self.i
        self.copies[0].wait_recv()
        self.add(self.part(wrap4(i + 1), 0), [self.slots.at[0]])
        self.copies[4].start()
        self.copies[1].wait_recv()
        self.add(self.part(wrap4(i - 1), 1), [self.slots.at[1]])
        self.copies[5].start()

    def finish(self):
        i = self.i
        self.copies[3].wait_recv()
        self.copies[4].wait_recv()
        self.add(self.part(i, 0), [self.slots.at[3], self.slots.at[4]])
        self.copies[2].wait_recv()
        self.copies[5].wait_recv()
        self.add(self.part(i, 1), [self.slots.at[2], self.slots.at[5]])

    def drain(self):
        for copy in self.copies:
            copy.wait_send()


def add_rows(target, others):
    total = target[...].astype(jnp.float32)
    for other in others:
        total = total + other[...].astype(jnp.float32)
    target[...] = total.astype(jnp.bfloat16)


def add_blocks(target, others):
    def one(k, _):
        a, b = k // 2, lax.rem(k, 2)
        add_rows(target.at[a, b], [o.at[a, b] for o in others])
        return 0

    lax.fori_loop(0, 4, one, 0)


class RingGather:
    def __init__(self, index, right, left, part, send, recv, base):
        i = index
        plan = [
            (part(i, None), right),
            (part(i, None), left),
            (part(wrap4(i - 1), 0), right),
            (part(wrap4(i + 1), 1), left),
        ]
        self.copies = [
            remote(src, src, send.at[base + n], recv.at[base + n], place)
            for n, (src, place) in enumerate(plan)
        ]

    def start(self):
        self.copies[0].start()
        self.copies[1].start()

    def middle(self):
        self.copies[0].wait_recv()
        self.copies[2].start()
        self.copies[1].wait_recv()
        self.copies[3].start()

    def finish(self):
        self.copies[2].wait_recv()
        self.copies[3].wait_recv()

    def drain(self):
        for copy in self.copies:
            copy.wait_send()


def layer_kernel(
    q_in, k_in, v_in, o_in, gain_in, ids_in, weights_in, gate_in, up_in, down_in, grad_in,
    layer_out, hidden_grad_out, gg_out, gu_out, gd_out,
    qs, kv, w, best, tot, acc, att, part_f, part_b, got,
    sel, sel_t, hidden_s, rows_s, grads_s, inv_s, inv_r, xr, cr, wg, wu, wd,
    act_g, act_u, act_b, act, act_back, xt, ct, grad, res, back, res_r, back_r,
    slots1_wide, slots1_slim, slots2_wide, slots2_slim, slot3_wide, slot3_slim,
    lsem, q_send, q_recv, w_send, w_recv, z_send, z_recv, g_send, g_recv, s_send, s_recv,
    a2a_local, a2a_send, a2a_recv, r_local, r_send, r_recv, rs_send, rs_recv,
):
    ctx, e, x, y, z = mesh_place()
    f32, bf = jnp.float32, jnp.bfloat16
    seq, core = e // 2, lax.rem(e, 2)
    group, slot = e // 4, lax.rem(e, 4)
    head_cols = pl.ds(pl.multiple_of(core * HEAD_SIZE, HEAD_SIZE), HEAD_SIZE)
    own_k = pltpu.make_async_copy(k_in.at[seq, :, head_cols], kv.at[x, y, z, 0], lsem.at[0])
    own_v = pltpu.make_async_copy(v_in.at[seq, :, head_cols], kv.at[x, y, z, 1], lsem.at[1])
    own_k.start()
    own_v.start()
    weight_copies = [
        pltpu.make_async_copy(src, dst, lsem.at[2 + n])
        for n, (src, dst) in enumerate(((gate_in, wg), (up_in, wu), (down_in, wd)))
    ]
    greet(all_partners(ctx, e, x, y, z))

    x_right, x_left = {"ctx": ctx_of(wrap4(x + 1), y, z)}, {"ctx": ctx_of(wrap4(x - 1), y, z)}
    y_right, y_left = {"ctx": ctx_of(x, wrap4(y + 1), z)}, {"ctx": ctx_of(x, wrap4(y - 1), z)}

    def ring_x(base, part):
        return RingGather(x, x_right, x_left, part, g_send, g_recv, base)

    def ring_y(base, part):
        return RingGather(y, y_right, y_left, part, g_send, g_recv, base)

    def two(h):
        return slice(None) if h is None else pl.ds(2 * h, 2)

    kv_a1 = ring_x(0, lambda i, h: kv.at[i, y, 0] if h is None else kv.at[i, y, 0, h])
    kv_b1 = ring_y(4, lambda i, h: kv.at[x, i, 1] if h is None else kv.at[x, i, 1, h])
    kv_a2 = ring_y(8, lambda i, h: kv.at[two(h), i, 0])
    kv_b2 = ring_x(12, lambda i, h: kv.at[i, two(h), 1])
    w_rings = []
    for c in range(2):
        cw = w.at[c]
        w_rings.append((
            ring_x(16 + 16 * c, lambda i, h, cw=cw: (
                cw.at[pl.ds(0, 2), i, y] if h is None else cw.at[h, i, y])),
            ring_y(20 + 16 * c, lambda i, h, cw=cw: (
                cw.at[pl.ds(2, 2), x, i] if h is None else cw.at[2 + h, x, i])),
            ring_y(24 + 16 * c, lambda i, h, cw=cw: (
                cw.at[pl.ds(0, 2), :, i] if h is None else cw.at[h, :, i])),
            ring_x(28 + 16 * c, lambda i, h, cw=cw: (
                cw.at[pl.ds(2, 2), i] if h is None else cw.at[2 + h, i])),
        ))
    z_partner = {"ctx": ctx_of(x, y, 1 - z)}
    z_copy = remote(kv.at[x, y, z], kv.at[x, y, z], z_send, z_recv, z_partner)

    own_k.wait()
    own_v.wait()
    z_copy.start()

    @pl.when(z == 0)
    def _():
        kv_a1.start()

    @pl.when(z == 1)
    def _():
        kv_b1.start()

    piece = pl.ds(pl.multiple_of((x * 4 + y) * 16, 16), 16)
    scatters = []
    for d in range(4):
        to = {"exp": 2 * lax.rem(seq + d, 4) + group}
        sends = [
            remote(
                o_in.at[piece, pl.ds(c * 1024, 1024)], w.at[c, slot, x, y],
                w_send.at[c, d], w_recv.at[c, slot], to,
            )
            for c in range(2)
        ]
        sends.append(remote(
            q_in.at[lax.rem(seq + d, 4)], qs.at[slot], q_send.at[d], q_recv.at[slot], to
        ))
        scatters.append(sends)
    mine = core == group
    own_pieces = [
        pltpu.make_async_copy(
            o_in.at[piece, pl.ds(c * 1024, 1024)], w.at[c, slot, x, y], w_recv.at[c, slot]
        )
        for c in range(2)
    ]
    own_pieces.append(pltpu.make_async_copy(q_in.at[seq], qs.at[slot], q_recv.at[slot]))
    for n in range(3):
        @pl.when(mine)
        def _():
            own_pieces[n].start()

        @pl.when(jnp.logical_not(mine))
        def _():
            scatters[0][n].start()

        for d in range(1, 4):
            scatters[d][n].start()
    for copy in weight_copies:
        copy.start()

    z_copy.wait_recv()

    @pl.when(z == 0)
    def _():
        kv_b1.start()

    @pl.when(z == 1)
    def _():
        kv_a1.start()

    def exchange(src, dst, number):
        own = pltpu.make_async_copy(src.at[e], dst.at[e], a2a_local.at[number])
        out = []
        for d in range(1, 8):
            to = lax.rem(e + d, 8)
            out.append(remote(
                src.at[to], dst.at[e],
                a2a_send.at[number, d], a2a_recv.at[number, d], {"exp": to},
            ))
        return own, out

    def begin(pair):
        own, out = pair
        for copy in out:
            copy.start()
        own.start()

    def arrive(pair):
        own, out = pair
        own.wait()
        for copy in out:
            copy.wait_recv()

    grads_x = exchange(grads_s, cr, 1)
    res_x = exchange(res, res_r, 2)
    back_x = exchange(back, back_r, 3)

    ids = ids_in[...]
    chosen = (lax.broadcasted_iota(jnp.int32, (16, TOK), 0) == ids).astype(f32)
    rows_at = lax.broadcasted_iota(jnp.int32, (TOK, TOK), 0)
    lanes_at = lax.broadcasted_iota(jnp.int32, (TOK, TOK), 1)
    before = (rows_at < lanes_at).astype(bf)
    earlier = jnp.dot(chosen.astype(bf), before, preferred_element_type=f32)
    place = ids.astype(f32) * CAP + jnp.sum(earlier * chosen, axis=0, keepdims=True)
    slot_at = lax.broadcasted_iota(jnp.int32, (SLOTS, TOK), 0).astype(f32)
    taken = (slot_at == place).astype(f32)
    sel[...] = taken.astype(bf)
    sel_t[...] = taken.T.astype(bf)
    gates = jnp.sum(jnp.where(rows_at == lanes_at, weights_in[...], 0.0), axis=1, keepdims=True)

    def dispatch(dst, value, first):
        width = value.shape[1]
        dst[:, :, first:first + width] = jnp.dot(
            sel[...], value, preferred_element_type=f32
        ).astype(bf).reshape(8, CAP, width)

    kv_a1.middle()
    kv_b1.middle()
    kv_a1.finish()
    kv_a2.start()
    kv_b1.finish()
    kv_b2.start()
    for c in range(2):
        for j in range(4):
            pltpu.make_async_copy(w.at[c, j, x, y], w.at[c, j, x, y], w_recv.at[c, j]).wait()
        for ring in w_rings[c][:2]:
            ring.start()
    for n in range(8):
        cols = slice(n * 256, (n + 1) * 256)
        dispatch(grads_s, (grad_in[:, cols].astype(f32) * gates).astype(bf), n * 256)
    for c in range(2):
        for ring in w_rings[c][:2]:
            ring.middle()
    for ring in w_rings[0][:2]:
        ring.finish()
    for ring in w_rings[0][2:]:
        ring.start()
    for j in range(4):
        pltpu.make_async_copy(qs.at[j], qs.at[j], q_recv.at[j]).wait()
    begin(grads_x)

    scale = math.log2(math.e) / math.sqrt(HEAD_SIZE)
    over_last = (((1,), (1,)), ((), ()))

    def head_scores(h, key):
        t = h % 2
        query = qs[h // 2, :, t * HEAD_SIZE:(t + 1) * HEAD_SIZE]
        return lax.dot_general(query, key, over_last, preferred_element_type=f32) * scale

    def with_ones(value):
        return jnp.concatenate([value, jnp.ones(value.shape, bf)], axis=1)

    key, value = kv[x, y, z, 0], with_ones(kv[x, y, z, 1])
    below = lax.broadcasted_iota(jnp.int32, (256, 256), 1) <= lax.broadcasted_iota(
        jnp.int32, (256, 256), 0
    )
    for h in range(8):
        scores = jnp.where(below, head_scores(h, key), masked_score)
        top = jnp.max(scores, axis=1, keepdims=True)
        blended = jnp.dot(jnp.exp2(scores - top).astype(bf), value, preferred_element_type=f32)
        best[h] = jnp.broadcast_to(top, (256, HEAD_SIZE))
        acc[h] = blended[:, :HEAD_SIZE]
        tot[h] = blended[:, HEAD_SIZE:]

    def fold(places):
        key = jnp.concatenate([kv[bx, by, bz, 0] for bx, by, bz in places], axis=0)
        value = with_ones(jnp.concatenate([kv[bx, by, bz, 1] for bx, by, bz in places], axis=0))
        for h in range(8):
            scores = head_scores(h, key)
            old = best[h]
            new = jnp.maximum(old, jnp.max(scores, axis=1, keepdims=True))
            weights = jnp.exp2(scores - jnp.concatenate([new] * (2 * len(places)), axis=1))
            factor = jnp.exp2(old - new)
            blended = jnp.dot(weights.astype(bf), value, preferred_element_type=f32)
            best[h] = new
            acc[h] = acc[h] * factor + blended[:, :HEAD_SIZE]
            tot[h] = tot[h] * factor + blended[:, HEAD_SIZE:]

    def four(g):
        even = lax.rem(g, 2) == 0
        k = g // 2
        off = jnp.where(k == 2, -1, jnp.where(k == 3, 2, k))
        line = jnp.where(even, wrap4(y + off), wrap4(x + off))

        def at(i):
            return jnp.where(even, i, line), jnp.where(even, line, i), jnp.where(even, 0, 1)

        whole = ctx_of(*at(3)) < ctx

        @pl.when(whole)
        def _():
            fold([at(i) for i in range(4)])

        @pl.when(jnp.logical_not(whole))
        def _():
            def one(i, _):
                bx, by, bz = at(i)

                @pl.when(ctx_of(bx, by, bz) < ctx)
                def _():
                    fold([(bx, by, bz)])

                return 0

            lax.fori_loop(0, 4, one, 0)

    def line(g, _):
        @pl.when(g == 2)
        def _():
            kv_a2.middle()
            kv_b2.middle()
            for ring in w_rings[1][:2]:
                ring.finish()
            for ring in w_rings[1][2:]:
                ring.start()

        @pl.when(g == 4)
        def _():
            for ring in w_rings[0][2:]:
                ring.middle()

        @pl.when(g == 6)
        def _():
            kv_a2.finish()
            kv_b2.finish()

        four(g)
        return 0

    lax.fori_loop(0, 8, line, 0)

    for h in range(8):
        att[:, :, h * HEAD_SIZE:(h + 1) * HEAD_SIZE] = (
            (acc[h] / tot[h]).astype(bf).reshape(2, 128, HEAD_SIZE)
        )

    sibling = {"exp": e + 1 - 2 * core}
    halves, row_copies = [], []
    for n in range(4):
        cols = pl.ds(n * 512, 512)
        halves.append(remote(
            part_b.at[:, cols], got.at[:, cols], s_send.at[n], s_recv.at[n], sibling
        ))
        own_rows = pltpu.make_async_copy(
            rows_s.at[e, :, cols], xr.at[e, :, cols], r_local.at[n]
        )
        out = []
        for d in range(1, 8):
            to = lax.rem(e + d, 8)
            out.append(remote(
                rows_s.at[to, :, cols], xr.at[e, :, cols],
                r_send.at[n, d], r_recv.at[n, d], {"exp": to},
            ))
        row_copies.append((own_rows, out))

    def project(rows, first):
        return jnp.dot(
            rows, w[first // 1024, :, :, :, :, first % 1024:first % 1024 + 256].reshape(1024, 256),
            preferred_element_type=f32,
        )

    squares = jnp.zeros((TOK, 1), f32)
    for c in range(2):
        for ring in w_rings[c][2:]:
            if c == 1:
                ring.middle()
        for ring in w_rings[c][2:]:
            ring.finish()
        for n in (2 * c, 2 * c + 1):
            for first in (n * 512, n * 512 + 256):
                part_b[:, first:first + 256] = project(att[1 - core], first).astype(bf)
            halves[n].start()
        for n in (2 * c, 2 * c + 1):
            cols = slice(n * 512, (n + 1) * 512)
            for first in (n * 512, n * 512 + 256):
                part_f[:, first:first + 256] = project(att[core], first)
            halves[n].wait_recv()
            hidden = (part_f[:, cols] + got[:, cols].astype(f32)).astype(bf)
            hidden_s[:, cols] = hidden
            hidden = hidden.astype(f32)
            squares = squares + jnp.sum(hidden * hidden, axis=1, keepdims=True)
            dispatch(rows_s, (hidden * gain_in[:, cols]).astype(bf), n * 512)
            begin(row_copies[n])
    inv_rms = lax.rsqrt(squares * (1.0 / DM) + epsilon)
    inv_row = jnp.broadcast_to(inv_rms, (TOK, TOK)).T[0:1, :]
    inv_slots = jnp.sum(sel[...].astype(f32) * inv_row, axis=1, keepdims=True)
    inv_s[...] = jnp.broadcast_to(inv_slots, (SLOTS, 128)).reshape(8, CAP, 128)
    inv_x = exchange(inv_s, inv_r, 0)
    begin(inv_x)

    for copy in weight_copies:
        copy.wait()
    arrive(grads_x)
    cot = cr[...].reshape(SLOTS, DM)
    ct[...] = cot.T
    for n in range(3):
        cols = slice(n * 256, (n + 1) * 256)
        act_b[:, cols] = lax.dot_general(cot, wd[cols, :], over_last, preferred_element_type=f32)

    for pair in row_copies:
        arrive(pair)
    arrive(inv_x)
    inv_in = inv_r[...].reshape(SLOTS, 128)[:, 0:1]
    rows = xr[...].reshape(SLOTS, DM)
    for n in range(3):
        cols = slice(n * 256, (n + 1) * 256)
        act_g[:, cols] = jnp.dot(rows, wg[:, cols], preferred_element_type=f32) * inv_in
        act_u[:, cols] = jnp.dot(rows, wu[:, cols], preferred_element_type=f32) * inv_in
    xt[...] = rows.T
    for n in range(3):
        cols = slice(n * 256, (n + 1) * 256)
        gate_act, up_act, back_units = act_g[:, cols], act_u[:, cols], act_b[:, cols]
        sigma = jax.nn.sigmoid(gate_act)
        gated = gate_act * sigma
        act[:, 1536 + n * 256:1536 + (n + 1) * 256] = (gated * up_act).astype(bf)
        back_gate = back_units * up_act * sigma * (1.0 + gate_act * (1.0 - sigma))
        back_up = back_units * gated
        act[:, cols] = (back_gate * inv_in).astype(bf)
        act[:, 768 + n * 256:768 + (n + 1) * 256] = (back_up * inv_in).astype(bf)
        act_back[:, cols] = back_gate.astype(bf)
        act_back[:, 768 + n * 256:768 + (n + 1) * 256] = back_up.astype(bf)

    chains = []
    for c, (first, width) in enumerate(CHAINS):
        cols = pl.ds(first, width)
        wide = c < 2
        slots1 = (slots1_wide if wide else slots1_slim).at[c % 2]
        slots2 = (slots2_wide if wide else slots2_slim).at[c % 2]
        slot3 = (slot3_wide if wide else slot3_slim).at[c % 2]
        base = 13 * c
        if c % 2 == 0:
            one = RingSum(
                x, x_right, x_left, lambda i, h, cols=cols: grad.at[i, pl.ds(2 * h, 2), :, :, cols],
                slots1, rs_send, rs_recv, base, add_blocks)
            second = RingSum(
                y, y_right, y_left, lambda i, h, cols=cols: grad.at[x, i, h, :, cols],
                slots2, rs_send, rs_recv, base + 6, add_rows)
        else:
            one = RingSum(
                y, y_right, y_left, lambda i, h, cols=cols: grad.at[pl.ds(2 * h, 2), i, :, :, cols],
                slots1, rs_send, rs_recv, base, add_blocks)
            second = RingSum(
                x, x_right, x_left, lambda i, h, cols=cols: grad.at[i, y, h, :, cols],
                slots2, rs_send, rs_recv, base + 6, add_rows)
        last = remote(
            grad.at[x, y, 1 - z, :, cols], slot3,
            rs_send.at[base + 12], rs_recv.at[base + 12], z_partner,
        )
        chains.append((one, second, last, slot3))

    def weight_grads(step):
        px, py = wrap4(x + step), wrap4(y + step)
        for k in range(2):
            some = pl.ds(pl.multiple_of(px * 512 + k * 256, 256), 256)
            grad[px, 2 * k:2 * k + 2, :, :, 0:1152] = jnp.dot(
                xt[some, :], act[:, 0:1152], preferred_element_type=f32
            ).astype(bf).reshape(2, 2, 64, 1152)
        for k in range(4):
            some = pl.ds(pl.multiple_of(k * 512 + py * 128, 128), 128)
            grad[k, py, :, :, 1152:1536] = jnp.dot(
                xt[some, :], act[:, 1152:1536], preferred_element_type=f32
            ).astype(bf).reshape(2, 64, 384)
            grad[k, py, :, :, 1536:2304] = jnp.dot(
                ct[some, :], act[:, 1536:2304], preferred_element_type=f32
            ).astype(bf).reshape(2, 64, 768)

    def launch(*chosen):
        for chain in chains:
            chain[0].start(*chosen)

    weight_grads(2)
    launch(0, 1)
    for n in range(8):
        cols = slice(n * 256, (n + 1) * 256)
        res[:, :, cols] = jnp.dot(
            act[:, 1536:], wd[:, cols], preferred_element_type=f32
        ).astype(bf).reshape(8, CAP, 256)
    begin(res_x)
    weight_grads(1)
    launch(2)
    weight_grads(-1)
    launch(3)
    weight_grads(0)
    for n in range(8):
        cols = slice(n * 256, (n + 1) * 256)
        back[:, :, cols] = (
            lax.dot_general(act_back[:, 0:768], wg[cols, :], over_last, preferred_element_type=f32)
            + lax.dot_general(act_back[:, 768:1536], wu[cols, :], over_last, preferred_element_type=f32)
        ).astype(bf).reshape(8, CAP, 256)
    begin(back_x)

    for chain in chains:
        chain[0].middle()
    for chain in chains:
        chain[0].finish()
        chain[1].start()

    for chain in chains:
        chain[1].middle()
    for chain in chains:
        chain[1].finish()
        chain[2].start()

    arrive(res_x)
    returned = res_r[...].reshape(SLOTS, DM)
    for n in range(8):
        cols = slice(n * 256, (n + 1) * 256)
        expert_sum = gates * jnp.dot(sel_t[...], returned[:, cols], preferred_element_type=f32)
        layer_out[:, cols] = (hidden_s[:, cols].astype(f32) + expert_sum).astype(bf)

    arrive(back_x)
    returned = back_r[...].reshape(SLOTS, DM)
    shared = jnp.zeros((TOK, 1), f32)
    for n in range(8):
        cols = slice(n * 256, (n + 1) * 256)
        scaled = gain_in[:, cols] * jnp.dot(
            sel_t[...], returned[:, cols], preferred_element_type=f32
        )
        part_f[:, cols] = scaled
        unit = hidden_s[:, cols].astype(f32) * inv_rms
        shared = shared + jnp.sum(scaled * unit, axis=1, keepdims=True)
    shared = shared * (1.0 / DM)
    for n in range(8):
        cols = slice(n * 256, (n + 1) * 256)
        unit = hidden_s[:, cols].astype(f32) * inv_rms
        hidden_grad_out[:, cols] = (
            grad_in[:, cols].astype(f32) + inv_rms * (part_f[:, cols] - unit * shared)
        ).astype(bf)

    for (first, width), (_, _, last, slot3) in zip(CHAINS, chains):
        cols = slice(first, first + width)
        last.wait_recv()
        part_f[0:64, cols.start % 1152:cols.start % 1152 + width] = (
            grad[x, y, z, :, cols].astype(f32) + slot3[...].astype(f32)
        )
        if first == 0:
            gg_out[:, 0:640] = part_f[0:64, 0:640]
        elif first == 640:
            gg_out[:, 640:768] = part_f[0:64, 640:768]
            gu_out[:, 0:384] = part_f[0:64, 768:1152]
        elif first == 1152:
            gu_out[:, 384:768] = part_f[0:64, 0:384]
            gd_out[:, 0:256] = part_f[0:64, 384:640]
        else:
            gd_out[:, 256:768] = part_f[0:64, 640:1152]

    for half in halves:
        half.wait_send()
    z_copy.wait_send()
    for ring in [kv_a1, kv_b1, kv_a2, kv_b2] + list(w_rings[0]) + list(w_rings[1]):
        ring.drain()
    for n in range(3):
        @pl.when(jnp.logical_not(mine))
        def _():
            scatters[0][n].wait_send()

        for d in range(1, 4):
            scatters[d][n].wait_send()
    for one, second, last, _ in chains:
        one.drain()
        second.drain()
        last.wait_send()
    for pair in row_copies + [inv_x, grads_x, res_x, back_x]:
        for copy in pair[1]:
            copy.wait_send()


def hand_over(*refs):
    for src, dst in zip(refs[:5], refs[5:]):
        dst[...] = src[...]


def on_device(
    queries, rotated_key_heads, value_head_rows, out_proj, norm_gain, expert_ids,
    gate_weights, expert_gate, expert_up, expert_down, grad_out,
):
    bf, f32 = jnp.bfloat16, jnp.float32
    anywhere = pl.BlockSpec(memory_space=pl.ANY)
    vmem = pl.BlockSpec(memory_space=pltpu.VMEM)
    dma = pltpu.SemaphoreType.DMA
    rows = jax.ShapeDtypeStruct((TOK, DM), bf)
    shard = jax.ShapeDtypeStruct((64, F), f32)
    swapped = pltpu.VMEM((8, CAP, DM), bf)
    units = pltpu.VMEM((SLOTS, F), f32)
    state = pltpu.VMEM((8, 256, HEAD_SIZE), f32)
    layer, hidden_grad, gg, gu, gd = pl.pallas_call(
        layer_kernel,
        out_shape=(rows, rows, shard, shard, shard),
        in_specs=[anywhere] * 4 + [vmem] * 3 + [anywhere] * 3 + [vmem],
        out_specs=(vmem,) * 5,
        scratch_shapes=[
            pltpu.VMEM((4, 256, 256), bf),
            pltpu.VMEM((4, 4, 2, 2, 256, HEAD_SIZE), bf),
            pltpu.VMEM((2, 4, 4, 4, 16, 1024), bf),
            state, state, state,
            pltpu.VMEM((2, 128, 1024), bf),
            pltpu.VMEM((TOK, DM), f32),
            pltpu.VMEM((TOK, DM), bf),
            pltpu.VMEM((TOK, DM), bf),
            pltpu.VMEM((SLOTS, TOK), bf),
            pltpu.VMEM((TOK, SLOTS), bf),
            pltpu.VMEM((TOK, DM), bf),
            swapped, swapped,
            pltpu.VMEM((8, CAP, 128), f32),
            pltpu.VMEM((8, CAP, 128), f32),
            swapped, swapped,
            pltpu.VMEM((DM, F), bf),
            pltpu.VMEM((DM, F), bf),
            pltpu.VMEM((F, DM), bf),
            units, units, units,
            pltpu.VMEM((SLOTS, 3 * F), bf),
            pltpu.VMEM((SLOTS, 2 * F), bf),
            pltpu.VMEM((DM, SLOTS), bf),
            pltpu.VMEM((DM, SLOTS), bf),
            pltpu.VMEM((4, 4, 2, 64, 3 * F), bf),
            swapped, swapped, swapped, swapped,
            pltpu.VMEM((2, 6, 2, 2, 64, 640), bf),
            pltpu.VMEM((2, 6, 2, 2, 64, 512), bf),
            pltpu.VMEM((2, 6, 64, 640), bf),
            pltpu.VMEM((2, 6, 64, 512), bf),
            pltpu.VMEM((2, 64, 640), bf),
            pltpu.VMEM((2, 64, 512), bf),
            dma((5,)), dma((4,)), dma((4,)), dma((2, 4)), dma((2, 4)),
            dma(()), dma(()), dma((48,)), dma((48,)), dma((4,)), dma((4,)),
            dma((4,)), dma((4, 8)), dma((4, 8)), dma((4,)), dma((4, 8)), dma((4, 8)),
            dma((52,)), dma((52,)),
        ],
        compiler_params=pltpu.CompilerParams(
            collective_id=1, has_side_effects=True, vmem_limit_bytes=62 * 1024 * 1024
        ),
        name="layer",
    )(
        queries, rotated_key_heads, value_head_rows, out_proj, norm_gain[None],
        expert_ids.reshape(1, TOK), gate_weights.reshape(1, TOK), expert_gate[0], expert_up[0], expert_down[0], grad_out,
    )
    shapes = (rows, rows, shard, shard, shard)
    layer, hidden_grad, gg, gu, gd = pl.pallas_call(
        hand_over,
        out_shape=shapes,
        in_specs=[vmem] * 5,
        out_specs=[vmem] * 5,
        compiler_params=pltpu.CompilerParams(vmem_limit_bytes=62 * 1024 * 1024),
        name="hand_over",
    )(layer, hidden_grad, gg, gu, gd)
    return (layer, hidden_grad, gg[None], gu[None], gd.T[None])


def solution(mesh):
    in_specs = (
        P(None, "ctx", "exp"),
        P(None, "ctx", None),
        P(None, "ctx", None),
        P("exp", None),
        P(),
        P(("ctx", "exp"), None),
        P(("ctx", "exp"), None),
        P("exp", None, None),
        P("exp", None, None),
        P("exp", None, None),
        P(("ctx", "exp"), None),
    )
    out_specs = (
        P(("ctx", "exp"), None),
        P(("ctx", "exp"), None),
        P("exp", "ctx", None),
        P("exp", "ctx", None),
        P("exp", None, "ctx"),
    )
    return jax.shard_map(
        on_device, mesh=mesh, in_specs=in_specs, out_specs=out_specs, check_vma=False
    )
```

```python
import math

import jax
import jax.numpy as jnp
from jax import lax
from jax.experimental import pallas as pl
from jax.experimental.pallas import tpu as pltpu
from jax.sharding import PartitionSpec as P

MESH = pl.DeviceIdType.MESH
HEAD_SIZE = 128
F = 768
DM = 2048
CAP = 32
SLOTS = 8 * CAP
TOK = 128
CHAINS = ((0, 640), (1152, 640), (640, 512), (1792, 512))

epsilon = 1e-06
masked_score = -1e30


def mesh_place():
    ctx = lax.axis_index("ctx")
    e = lax.axis_index("exp")
    x = ctx // 8
    y = lax.rem(ctx // 2, 4)
    z = lax.rem(ctx, 2)
    return ctx, e, x, y, z


def ctx_of(x, y, z):
    return x * 8 + y * 2 + z


def wrap4(i):
    return lax.rem(i + 4, 4)


def greet(partners):
    barrier = pltpu.get_barrier_semaphore()
    for place in partners:
        pl.semaphore_signal(barrier, inc=1, device_id=place, device_id_type=MESH)
    pl.semaphore_wait(barrier, len(partners))


def all_partners(ctx, e, x, y, z):
    found = [{"exp": lax.rem(e + d, 8)} for d in range(1, 8)]
    found += [{"ctx": ctx_of(wrap4(x + d), y, z)} for d in (1, -1)]
    found += [{"ctx": ctx_of(x, wrap4(y + d), z)} for d in (1, -1)]
    found += [{"ctx": ctx_of(x, y, 1 - z)}]
    return found


def remote(src, dst, send, recv, place):
    return pltpu.make_async_remote_copy(
        src_ref=src, dst_ref=dst, send_sem=send, recv_sem=recv,
        device_id=place, device_id_type=MESH,
    )


class RingSum:
    def __init__(self, index, right, left, part, slots, send, recv, base, add):
        self.i, self.part, self.slots, self.add = index, part, slots, add
        i = index
        plan = [
            (part(wrap4(i + 2), 0), right),
            (part(wrap4(i + 2), 1), left),
            (part(wrap4(i + 1), 1), right),
            (part(wrap4(i - 1), 0), left),
            (part(wrap4(i + 1), 0), right),
            (part(wrap4(i - 1), 1), left),
        ]
        self.copies = [
            remote(src, slots.at[n], send.at[base + n], recv.at[base + n], place)
            for n, (src, place) in enumerate(plan)
        ]

    def start(self, *chosen):
        for n in chosen or range(4):
            self.copies[n].start()

    def middle(self):
        i = self.i
        self.copies[0].wait_recv()
        self.add(self.part(wrap4(i + 1), 0), [self.slots.at[0]])
        self.copies[4].start()
        self.copies[1].wait_recv()
        self.add(self.part(wrap4(i - 1), 1), [self.slots.at[1]])
        self.copies[5].start()

    def finish(self):
        i = self.i
        self.copies[3].wait_recv()
        self.copies[4].wait_recv()
        self.add(self.part(i, 0), [self.slots.at[3], self.slots.at[4]])
        self.copies[2].wait_recv()
        self.copies[5].wait_recv()
        self.add(self.part(i, 1), [self.slots.at[2], self.slots.at[5]])

    def drain(self):
        for copy in self.copies:
            copy.wait_send()


def add_rows(target, others):
    total = target[...].astype(jnp.float32)
    for other in others:
        total = total + other[...].astype(jnp.float32)
    target[...] = total.astype(jnp.bfloat16)


def add_blocks(target, others):
    def one(k, _):
        a, b = k // 2, lax.rem(k, 2)
        add_rows(target.at[a, b], [o.at[a, b] for o in others])
        return 0

    lax.fori_loop(0, 4, one, 0)


class RingGather:
    def __init__(self, index, right, left, part, send, recv, base):
        i = index
        plan = [
            (part(i, None), right),
            (part(i, None), left),
            (part(wrap4(i - 1), 0), right),
            (part(wrap4(i + 1), 1), left),
        ]
        self.copies = [
            remote(src, src, send.at[base + n], recv.at[base + n], place)
            for n, (src, place) in enumerate(plan)
        ]

    def start(self):
        self.copies[0].start()
        self.copies[1].start()

    def middle(self):
        self.copies[0].wait_recv()
        self.copies[2].start()
        self.copies[1].wait_recv()
        self.copies[3].start()

    def finish(self):
        self.copies[2].wait_recv()
        self.copies[3].wait_recv()

    def drain(self):
        for copy in self.copies:
            copy.wait_send()


def layer_kernel(
    q_in, k_in, v_in, o_in, gain_in, ids_in, weights_in, gate_in, up_in, down_in, grad_in,
    layer_out, hidden_grad_out, gg_out, gu_out, gd_out,
    qs, kv, w, best, tot, acc, att, part_f, part_b, got,
    sel, sel_t, hidden_s, rows_s, grads_s, inv_s, inv_r, xr, cr, wg, wu, wd,
    act_g, act_u, act_b, act, act_back, xt, ct, grad, res, back, res_r, back_r,
    slots1_wide, slots1_slim, slots2_wide, slots2_slim, slot3_wide, slot3_slim,
    lsem, q_send, q_recv, w_send, w_recv, z_send, z_recv, g_send, g_recv, s_send, s_recv,
    a2a_local, a2a_send, a2a_recv, r_local, r_send, r_recv, rs_send, rs_recv,
):
    ctx, e, x, y, z = mesh_place()
    f32, bf = jnp.float32, jnp.bfloat16
    seq, core = e // 2, lax.rem(e, 2)
    group, slot = e // 4, lax.rem(e, 4)
    head_cols = pl.ds(pl.multiple_of(core * HEAD_SIZE, HEAD_SIZE), HEAD_SIZE)
    own_k = pltpu.make_async_copy(k_in.at[seq, :, head_cols], kv.at[x, y, z, 0], lsem.at[0])
    own_v = pltpu.make_async_copy(v_in.at[seq, :, head_cols], kv.at[x, y, z, 1], lsem.at[1])
    own_k.start()
    own_v.start()
    weight_copies = [
        pltpu.make_async_copy(src, dst, lsem.at[2 + n])
        for n, (src, dst) in enumerate(((gate_in, wg), (up_in, wu), (down_in, wd)))
    ]
    greet(all_partners(ctx, e, x, y, z))

    x_right, x_left = {"ctx": ctx_of(wrap4(x + 1), y, z)}, {"ctx": ctx_of(wrap4(x - 1), y, z)}
    y_right, y_left = {"ctx": ctx_of(x, wrap4(y + 1), z)}, {"ctx": ctx_of(x, wrap4(y - 1), z)}

    def ring_x(base, part):
        return RingGather(x, x_right, x_left, part, g_send, g_recv, base)

    def ring_y(base, part):
        return RingGather(y, y_right, y_left, part, g_send, g_recv, base)

    def two(h):
        return slice(None) if h is None else pl.ds(2 * h, 2)

    kv_a1 = ring_x(0, lambda i, h: kv.at[i, y, 0] if h is None else kv.at[i, y, 0, h])
    kv_b1 = ring_y(4, lambda i, h: kv.at[x, i, 1] if h is None else kv.at[x, i, 1, h])
    kv_a2 = ring_y(8, lambda i, h: kv.at[two(h), i, 0])
    kv_b2 = ring_x(12, lambda i, h: kv.at[i, two(h), 1])
    w_rings = []
    for c in range(2):
        cw = w.at[c]
        w_rings.append((
            ring_x(16 + 16 * c, lambda i, h, cw=cw: (
                cw.at[pl.ds(0, 2), i, y] if h is None else cw.at[h, i, y])),
            ring_y(20 + 16 * c, lambda i, h, cw=cw: (
                cw.at[pl.ds(2, 2), x, i] if h is None else cw.at[2 + h, x, i])),
            ring_y(24 + 16 * c, lambda i, h, cw=cw: (
                cw.at[pl.ds(0, 2), :, i] if h is None else cw.at[h, :, i])),
            ring_x(28 + 16 * c, lambda i, h, cw=cw: (
                cw.at[pl.ds(2, 2), i] if h is None else cw.at[2 + h, i])),
        ))
    z_partner = {"ctx": ctx_of(x, y, 1 - z)}
    z_copy = remote(kv.at[x, y, z], kv.at[x, y, z], z_send, z_recv, z_partner)

    own_k.wait()
    own_v.wait()
    z_copy.start()

    @pl.when(z == 0)
    def _():
        kv_a1.start()

    @pl.when(z == 1)
    def _():
        kv_b1.start()

    piece = pl.ds(pl.multiple_of((x * 4 + y) * 16, 16), 16)
    scatters = []
    for d in range(4):
        to = {"exp": 2 * lax.rem(seq + d, 4) + group}
        sends = [
            remote(
                o_in.at[piece, pl.ds(c * 1024, 1024)], w.at[c, slot, x, y],
                w_send.at[c, d], w_recv.at[c, slot], to,
            )
            for c in range(2)
        ]
        sends.append(remote(
            q_in.at[lax.rem(seq + d, 4)], qs.at[slot], q_send.at[d], q_recv.at[slot], to
        ))
        scatters.append(sends)
    mine = core == group
    own_pieces = [
        pltpu.make_async_copy(
            o_in.at[piece, pl.ds(c * 1024, 1024)], w.at[c, slot, x, y], w_recv.at[c, slot]
        )
        for c in range(2)
    ]
    own_pieces.append(pltpu.make_async_copy(q_in.at[seq], qs.at[slot], q_recv.at[slot]))
    for n in (2, 0, 1):
        @pl.when(mine)
        def _():
            own_pieces[n].start()

        @pl.when(jnp.logical_not(mine))
        def _():
            scatters[0][n].start()

        for d in range(1, 4):
            scatters[d][n].start()
    for copy in weight_copies:
        copy.start()

    z_copy.wait_recv()

    @pl.when(z == 0)
    def _():
        kv_b1.start()

    @pl.when(z == 1)
    def _():
        kv_a1.start()

    def exchange(src, dst, number):
        own = pltpu.make_async_copy(src.at[e], dst.at[e], a2a_local.at[number])
        out = []
        for d in range(1, 8):
            to = lax.rem(e + d, 8)
            out.append(remote(
                src.at[to], dst.at[e],
                a2a_send.at[number, d], a2a_recv.at[number, d], {"exp": to},
            ))
        return own, out

    def begin(pair):
        own, out = pair
        for copy in out:
            copy.start()
        own.start()

    def arrive(pair):
        own, out = pair
        own.wait()
        for copy in out:
            copy.wait_recv()

    grads_x = exchange(grads_s, cr, 1)
    res_x = exchange(res, res_r, 2)
    back_x = exchange(back, back_r, 3)

    ids = ids_in[...]
    chosen = (lax.broadcasted_iota(jnp.int32, (16, TOK), 0) == ids).astype(f32)
    rows_at = lax.broadcasted_iota(jnp.int32, (TOK, TOK), 0)
    lanes_at = lax.broadcasted_iota(jnp.int32, (TOK, TOK), 1)
    before = (rows_at < lanes_at).astype(bf)
    earlier = jnp.dot(chosen.astype(bf), before, preferred_element_type=f32)
    place = ids.astype(f32) * CAP + jnp.sum(earlier * chosen, axis=0, keepdims=True)
    slot_at = lax.broadcasted_iota(jnp.int32, (SLOTS, TOK), 0).astype(f32)
    taken = (slot_at == place).astype(f32)
    sel[...] = taken.astype(bf)
    sel_t[...] = taken.T.astype(bf)
    gates = jnp.sum(jnp.where(rows_at == lanes_at, weights_in[...], 0.0), axis=1, keepdims=True)

    def dispatch(dst, value, first):
        width = value.shape[1]
        dst[:, :, first:first + width] = jnp.dot(
            sel[...], value, preferred_element_type=f32
        ).astype(bf).reshape(8, CAP, width)

    kv_a1.middle()
    kv_b1.middle()
    kv_a1.finish()
    kv_a2.start()
    kv_b1.finish()
    kv_b2.start()
    for c in range(2):
        for j in range(4):
            pltpu.make_async_copy(w.at[c, j, x, y], w.at[c, j, x, y], w_recv.at[c, j]).wait()
        for ring in w_rings[c][:2]:
            ring.start()
    for n in range(8):
        cols = slice(n * 256, (n + 1) * 256)
        dispatch(grads_s, (grad_in[:, cols].astype(f32) * gates).astype(bf), n * 256)
    for c in range(2):
        for ring in w_rings[c][:2]:
            ring.middle()
    for ring in w_rings[0][:2]:
        ring.finish()
    for ring in w_rings[0][2:]:
        ring.start()
    for j in range(4):
        pltpu.make_async_copy(qs.at[j], qs.at[j], q_recv.at[j]).wait()
    begin(grads_x)

    scale = math.log2(math.e) / math.sqrt(HEAD_SIZE)
    over_last = (((1,), (1,)), ((), ()))

    def head_scores(h, key):
        t = h % 2
        query = qs[h // 2, :, t * HEAD_SIZE:(t + 1) * HEAD_SIZE]
        return lax.dot_general(query, key, over_last, preferred_element_type=f32) * scale

    def with_ones(value):
        return jnp.concatenate([value, jnp.ones(value.shape, bf)], axis=1)

    key, value = kv[x, y, z, 0], with_ones(kv[x, y, z, 1])
    below = lax.broadcasted_iota(jnp.int32, (256, 256), 1) <= lax.broadcasted_iota(
        jnp.int32, (256, 256), 0
    )
    for h in range(8):
        scores = jnp.where(below, head_scores(h, key), masked_score)
        top = jnp.max(scores, axis=1, keepdims=True)
        blended = jnp.dot(jnp.exp2(scores - top).astype(bf), value, preferred_element_type=f32)
        best[h] = jnp.broadcast_to(top, (256, HEAD_SIZE))
        acc[h] = blended[:, :HEAD_SIZE]
        tot[h] = blended[:, HEAD_SIZE:]

    def fold(places):
        key = jnp.concatenate([kv[bx, by, bz, 0] for bx, by, bz in places], axis=0)
        value = with_ones(jnp.concatenate([kv[bx, by, bz, 1] for bx, by, bz in places], axis=0))
        for h in range(8):
            scores = head_scores(h, key)
            old = best[h]
            new = jnp.maximum(old, jnp.max(scores, axis=1, keepdims=True))
            weights = jnp.exp2(scores - jnp.concatenate([new] * (2 * len(places)), axis=1))
            factor = jnp.exp2(old - new)
            blended = jnp.dot(weights.astype(bf), value, preferred_element_type=f32)
            best[h] = new
            acc[h] = acc[h] * factor + blended[:, :HEAD_SIZE]
            tot[h] = tot[h] * factor + blended[:, HEAD_SIZE:]

    def four(g):
        even = lax.rem(g, 2) == 0
        k = g // 2
        off = jnp.where(k == 2, -1, jnp.where(k == 3, 2, k))
        line = jnp.where(even, wrap4(y + off), wrap4(x + off))

        def at(i):
            return jnp.where(even, i, line), jnp.where(even, line, i), jnp.where(even, 0, 1)

        whole = ctx_of(*at(3)) < ctx

        @pl.when(whole)
        def _():
            fold([at(i) for i in range(4)])

        @pl.when(jnp.logical_not(whole))
        def _():
            def one(i, _):
                bx, by, bz = at(i)

                @pl.when(ctx_of(bx, by, bz) < ctx)
                def _():
                    fold([(bx, by, bz)])

                return 0

            lax.fori_loop(0, 4, one, 0)

    def line(g, _):
        @pl.when(g == 2)
        def _():
            kv_a2.middle()
            kv_b2.middle()

        @pl.when(g == 4)
        def _():
            for ring in w_rings[0][2:]:
                ring.middle()
            for ring in w_rings[1][:2]:
                ring.finish()
            for ring in w_rings[1][2:]:
                ring.start()

        @pl.when(g == 6)
        def _():
            kv_a2.finish()
            kv_b2.finish()

        four(g)
        return 0

    lax.fori_loop(0, 8, line, 0)

    for h in range(8):
        att[:, :, h * HEAD_SIZE:(h + 1) * HEAD_SIZE] = (
            (acc[h] / tot[h]).astype(bf).reshape(2, 128, HEAD_SIZE)
        )

    sibling = {"exp": e + 1 - 2 * core}
    halves, row_copies = [], []
    for n in range(4):
        cols = pl.ds(n * 512, 512)
        halves.append(remote(
            part_b.at[:, cols], got.at[:, cols], s_send.at[n], s_recv.at[n], sibling
        ))
        own_rows = pltpu.make_async_copy(
            rows_s.at[e, :, cols], xr.at[e, :, cols], r_local.at[n]
        )
        out = []
        for d in range(1, 8):
            to = lax.rem(e + d, 8)
            out.append(remote(
                rows_s.at[to, :, cols], xr.at[e, :, cols],
                r_send.at[n, d], r_recv.at[n, d], {"exp": to},
            ))
        row_copies.append((own_rows, out))

    def project(rows, first):
        return jnp.dot(
            rows, w[first // 1024, :, :, :, :, first % 1024:first % 1024 + 256].reshape(1024, 256),
            preferred_element_type=f32,
        )

    squares = jnp.zeros((TOK, 1), f32)
    for c in range(2):
        for ring in w_rings[c][2:]:
            if c == 1:
                ring.middle()
        for ring in w_rings[c][2:]:
            ring.finish()
        for n in (2 * c, 2 * c + 1):
            for first in (n * 512, n * 512 + 256):
                part_b[:, first:first + 256] = project(att[1 - core], first).astype(bf)
            halves[n].start()
        for n in (2 * c, 2 * c + 1):
            cols = slice(n * 512, (n + 1) * 512)
            for first in (n * 512, n * 512 + 256):
                part_f[:, first:first + 256] = project(att[core], first)
            halves[n].wait_recv()
            hidden = (part_f[:, cols] + got[:, cols].astype(f32)).astype(bf)
            hidden_s[:, cols] = hidden
            hidden = hidden.astype(f32)
            squares = squares + jnp.sum(hidden * hidden, axis=1, keepdims=True)
            dispatch(rows_s, (hidden * gain_in[:, cols]).astype(bf), n * 512)
            begin(row_copies[n])
    inv_rms = lax.rsqrt(squares * (1.0 / DM) + epsilon)
    inv_row = jnp.broadcast_to(inv_rms, (TOK, TOK)).T[0:1, :]
    inv_slots = jnp.sum(sel[...].astype(f32) * inv_row, axis=1, keepdims=True)
    inv_s[...] = jnp.broadcast_to(inv_slots, (SLOTS, 128)).reshape(8, CAP, 128)
    inv_x = exchange(inv_s, inv_r, 0)
    begin(inv_x)

    for copy in weight_copies:
        copy.wait()
    arrive(grads_x)
    cot = cr[...].reshape(SLOTS, DM)
    ct[...] = cot.T
    for n in range(3):
        cols = slice(n * 256, (n + 1) * 256)
        act_b[:, cols] = lax.dot_general(cot, wd[cols, :], over_last, preferred_element_type=f32)

    for c in range(2):
        for pair in row_copies[2 * c:2 * c + 2]:
            arrive(pair)
        part = slice(c * 1024, (c + 1) * 1024)
        rows = xr[:, :, part].reshape(SLOTS, 1024)
        for n in range(3):
            cols = slice(n * 256, (n + 1) * 256)
            gate_part = jnp.dot(rows, wg[part, cols], preferred_element_type=f32)
            up_part = jnp.dot(rows, wu[part, cols], preferred_element_type=f32)
            if c == 0:
                act_g[:, cols] = gate_part
                act_u[:, cols] = up_part
            else:
                act_g[:, cols] = act_g[:, cols] + gate_part
                act_u[:, cols] = act_u[:, cols] + up_part
        xt[part, :] = rows.T
    arrive(inv_x)
    inv_in = inv_r[...].reshape(SLOTS, 128)[:, 0:1]
    for n in range(3):
        cols = slice(n * 256, (n + 1) * 256)
        gate_act, up_act = act_g[:, cols] * inv_in, act_u[:, cols] * inv_in
        back_units = act_b[:, cols]
        sigma = jax.nn.sigmoid(gate_act)
        gated = gate_act * sigma
        act[:, 1536 + n * 256:1536 + (n + 1) * 256] = (gated * up_act).astype(bf)
        back_gate = back_units * up_act * sigma * (1.0 + gate_act * (1.0 - sigma))
        back_up = back_units * gated
        act[:, cols] = (back_gate * inv_in).astype(bf)
        act[:, 768 + n * 256:768 + (n + 1) * 256] = (back_up * inv_in).astype(bf)
        act_back[:, cols] = back_gate.astype(bf)
        act_back[:, 768 + n * 256:768 + (n + 1) * 256] = back_up.astype(bf)

    chains = []
    for c, (first, width) in enumerate(CHAINS):
        cols = pl.ds(first, width)
        wide = c < 2
        slots1 = (slots1_wide if wide else slots1_slim).at[c % 2]
        slots2 = (slots2_wide if wide else slots2_slim).at[c % 2]
        slot3 = (slot3_wide if wide else slot3_slim).at[c % 2]
        base = 13 * c
        if c % 2 == 0:
            one = RingSum(
                x, x_right, x_left, lambda i, h, cols=cols: grad.at[i, pl.ds(2 * h, 2), :, :, cols],
                slots1, rs_send, rs_recv, base, add_blocks)
            second = RingSum(
                y, y_right, y_left, lambda i, h, cols=cols: grad.at[x, i, h, :, cols],
                slots2, rs_send, rs_recv, base + 6, add_rows)
        else:
            one = RingSum(
                y, y_right, y_left, lambda i, h, cols=cols: grad.at[pl.ds(2 * h, 2), i, :, :, cols],
                slots1, rs_send, rs_recv, base, add_blocks)
            second = RingSum(
                x, x_right, x_left, lambda i, h, cols=cols: grad.at[i, y, h, :, cols],
                slots2, rs_send, rs_recv, base + 6, add_rows)
        last = remote(
            grad.at[x, y, 1 - z, :, cols], slot3,
            rs_send.at[base + 12], rs_recv.at[base + 12], z_partner,
        )
        chains.append((one, second, last, slot3))

    def weight_grads(step):
        px, py = wrap4(x + step), wrap4(y + step)
        for k in range(2):
            some = pl.ds(pl.multiple_of(px * 512 + k * 256, 256), 256)
            grad[px, 2 * k:2 * k + 2, :, :, 0:1152] = jnp.dot(
                xt[some, :], act[:, 0:1152], preferred_element_type=f32
            ).astype(bf).reshape(2, 2, 64, 1152)
        for k in range(4):
            some = pl.ds(pl.multiple_of(k * 512 + py * 128, 128), 128)
            grad[k, py, :, :, 1152:1536] = jnp.dot(
                xt[some, :], act[:, 1152:1536], preferred_element_type=f32
            ).astype(bf).reshape(2, 64, 384)
            grad[k, py, :, :, 1536:2304] = jnp.dot(
                ct[some, :], act[:, 1536:2304], preferred_element_type=f32
            ).astype(bf).reshape(2, 64, 768)

    def launch(*chosen):
        for chain in chains:
            chain[0].start(*chosen)

    weight_grads(2)
    launch(0, 1)
    for n in range(8):
        cols = slice(n * 256, (n + 1) * 256)
        res[:, :, cols] = jnp.dot(
            act[:, 1536:], wd[:, cols], preferred_element_type=f32
        ).astype(bf).reshape(8, CAP, 256)
    begin(res_x)
    weight_grads(1)
    launch(2)
    weight_grads(-1)
    launch(3)
    weight_grads(0)
    for n in range(8):
        cols = slice(n * 256, (n + 1) * 256)
        back[:, :, cols] = (
            lax.dot_general(act_back[:, 0:768], wg[cols, :], over_last, preferred_element_type=f32)
            + lax.dot_general(act_back[:, 768:1536], wu[cols, :], over_last, preferred_element_type=f32)
        ).astype(bf).reshape(8, CAP, 256)
    begin(back_x)

    for chain in chains:
        chain[0].middle()
    for chain in chains:
        chain[0].finish()
        chain[1].start()

    for chain in chains:
        chain[1].middle()
    for chain in chains:
        chain[1].finish()
        chain[2].start()

    arrive(res_x)
    returned = res_r[...].reshape(SLOTS, DM)
    for n in range(8):
        cols = slice(n * 256, (n + 1) * 256)
        expert_sum = gates * jnp.dot(sel_t[...], returned[:, cols], preferred_element_type=f32)
        layer_out[:, cols] = (hidden_s[:, cols].astype(f32) + expert_sum).astype(bf)

    arrive(back_x)
    returned = back_r[...].reshape(SLOTS, DM)
    shared = jnp.zeros((TOK, 1), f32)
    for n in range(8):
        cols = slice(n * 256, (n + 1) * 256)
        scaled = gain_in[:, cols] * jnp.dot(
            sel_t[...], returned[:, cols], preferred_element_type=f32
        )
        part_f[:, cols] = scaled
        unit = hidden_s[:, cols].astype(f32) * inv_rms
        shared = shared + jnp.sum(scaled * unit, axis=1, keepdims=True)
    shared = shared * (1.0 / DM)
    for n in range(8):
        cols = slice(n * 256, (n + 1) * 256)
        unit = hidden_s[:, cols].astype(f32) * inv_rms
        hidden_grad_out[:, cols] = (
            grad_in[:, cols].astype(f32) + inv_rms * (part_f[:, cols] - unit * shared)
        ).astype(bf)

    for (first, width), (_, _, last, slot3) in zip(CHAINS, chains):
        cols = slice(first, first + width)
        last.wait_recv()
        part_f[0:64, cols.start % 1152:cols.start % 1152 + width] = (
            grad[x, y, z, :, cols].astype(f32) + slot3[...].astype(f32)
        )
        if first == 0:
            gg_out[:, 0:640] = part_f[0:64, 0:640]
        elif first == 640:
            gg_out[:, 640:768] = part_f[0:64, 640:768]
            gu_out[:, 0:384] = part_f[0:64, 768:1152]
        elif first == 1152:
            gu_out[:, 384:768] = part_f[0:64, 0:384]
            gd_out[:, 0:256] = part_f[0:64, 384:640]
        else:
            gd_out[:, 256:768] = part_f[0:64, 640:1152]

    for half in halves:
        half.wait_send()
    z_copy.wait_send()
    for ring in [kv_a1, kv_b1, kv_a2, kv_b2] + list(w_rings[0]) + list(w_rings[1]):
        ring.drain()
    for n in range(3):
        @pl.when(jnp.logical_not(mine))
        def _():
            scatters[0][n].wait_send()

        for d in range(1, 4):
            scatters[d][n].wait_send()
    for one, second, last, _ in chains:
        one.drain()
        second.drain()
        last.wait_send()
    for pair in row_copies + [inv_x, grads_x, res_x, back_x]:
        for copy in pair[1]:
            copy.wait_send()


def hand_over(*refs):
    for src, dst in zip(refs[:5], refs[5:]):
        dst[...] = src[...]


def on_device(
    queries, rotated_key_heads, value_head_rows, out_proj, norm_gain, expert_ids,
    gate_weights, expert_gate, expert_up, expert_down, grad_out,
):
    bf, f32 = jnp.bfloat16, jnp.float32
    anywhere = pl.BlockSpec(memory_space=pl.ANY)
    vmem = pl.BlockSpec(memory_space=pltpu.VMEM)
    dma = pltpu.SemaphoreType.DMA
    rows = jax.ShapeDtypeStruct((TOK, DM), bf)
    shard = jax.ShapeDtypeStruct((64, F), f32)
    swapped = pltpu.VMEM((8, CAP, DM), bf)
    units = pltpu.VMEM((SLOTS, F), f32)
    state = pltpu.VMEM((8, 256, HEAD_SIZE), f32)
    layer, hidden_grad, gg, gu, gd = pl.pallas_call(
        layer_kernel,
        out_shape=(rows, rows, shard, shard, shard),
        in_specs=[anywhere] * 4 + [vmem] * 3 + [anywhere] * 3 + [vmem],
        out_specs=(vmem,) * 5,
        scratch_shapes=[
            pltpu.VMEM((4, 256, 256), bf),
            pltpu.VMEM((4, 4, 2, 2, 256, HEAD_SIZE), bf),
            pltpu.VMEM((2, 4, 4, 4, 16, 1024), bf),
            state, state, state,
            pltpu.VMEM((2, 128, 1024), bf),
            pltpu.VMEM((TOK, DM), f32),
            pltpu.VMEM((TOK, DM), bf),
            pltpu.VMEM((TOK, DM), bf),
            pltpu.VMEM((SLOTS, TOK), bf),
            pltpu.VMEM((TOK, SLOTS), bf),
            pltpu.VMEM((TOK, DM), bf),
            swapped, swapped,
            pltpu.VMEM((8, CAP, 128), f32),
            pltpu.VMEM((8, CAP, 128), f32),
            swapped, swapped,
            pltpu.VMEM((DM, F), bf),
            pltpu.VMEM((DM, F), bf),
            pltpu.VMEM((F, DM), bf),
            units, units, units,
            pltpu.VMEM((SLOTS, 3 * F), bf),
            pltpu.VMEM((SLOTS, 2 * F), bf),
            pltpu.VMEM((DM, SLOTS), bf),
            pltpu.VMEM((DM, SLOTS), bf),
            pltpu.VMEM((4, 4, 2, 64, 3 * F), bf),
            swapped, swapped, swapped, swapped,
            pltpu.VMEM((2, 6, 2, 2, 64, 640), bf),
            pltpu.VMEM((2, 6, 2, 2, 64, 512), bf),
            pltpu.VMEM((2, 6, 64, 640), bf),
            pltpu.VMEM((2, 6, 64, 512), bf),
            pltpu.VMEM((2, 64, 640), bf),
            pltpu.VMEM((2, 64, 512), bf),
            dma((5,)), dma((4,)), dma((4,)), dma((2, 4)), dma((2, 4)),
            dma(()), dma(()), dma((48,)), dma((48,)), dma((4,)), dma((4,)),
            dma((4,)), dma((4, 8)), dma((4, 8)), dma((4,)), dma((4, 8)), dma((4, 8)),
            dma((52,)), dma((52,)),
        ],
        compiler_params=pltpu.CompilerParams(
            collective_id=1, has_side_effects=True, vmem_limit_bytes=62 * 1024 * 1024
        ),
        name="layer",
    )(
        queries, rotated_key_heads, value_head_rows, out_proj, norm_gain[None],
        expert_ids.reshape(1, TOK), gate_weights.reshape(1, TOK), expert_gate[0], expert_up[0], expert_down[0], grad_out,
    )
    shapes = (rows, rows, shard, shard, shard)
    layer, hidden_grad, gg, gu, gd = pl.pallas_call(
        hand_over,
        out_shape=shapes,
        in_specs=[vmem] * 5,
        out_specs=[vmem] * 5,
        compiler_params=pltpu.CompilerParams(vmem_limit_bytes=62 * 1024 * 1024),
        name="hand_over",
    )(layer, hidden_grad, gg, gu, gd)
    return (layer, hidden_grad, gg[None], gu[None], gd.T[None])


def solution(mesh):
    in_specs = (
        P(None, "ctx", "exp"),
        P(None, "ctx", None),
        P(None, "ctx", None),
        P("exp", None),
        P(),
        P(("ctx", "exp"), None),
        P(("ctx", "exp"), None),
        P("exp", None, None),
        P("exp", None, None),
        P("exp", None, None),
        P(("ctx", "exp"), None),
    )
    out_specs = (
        P(("ctx", "exp"), None),
        P(("ctx", "exp"), None),
        P("exp", "ctx", None),
        P("exp", "ctx", None),
        P("exp", None, "ctx"),
    )
    return jax.shard_map(
        on_device, mesh=mesh, in_specs=in_specs, out_specs=out_specs, check_vma=False
    )
```

```python
import math

import jax
import jax.numpy as jnp
from jax import lax
from jax.experimental import pallas as pl
from jax.experimental.pallas import tpu as pltpu
from jax.sharding import PartitionSpec as P

MESH = pl.DeviceIdType.MESH
HEAD_SIZE = 128
F = 768
DM = 2048
CAP = 32
SLOTS = 8 * CAP
TOK = 128
CHAINS = ((0, 640), (1152, 640), (640, 512), (1792, 512))

epsilon = 1e-06
masked_score = -1e30


def mesh_place():
    ctx = lax.axis_index("ctx")
    e = lax.axis_index("exp")
    x = ctx // 8
    y = lax.rem(ctx // 2, 4)
    z = lax.rem(ctx, 2)
    return ctx, e, x, y, z


def ctx_of(x, y, z):
    return x * 8 + y * 2 + z


def wrap4(i):
    return lax.rem(i + 4, 4)


def greet(partners):
    barrier = pltpu.get_barrier_semaphore()
    for place in partners:
        pl.semaphore_signal(barrier, inc=1, device_id=place, device_id_type=MESH)
    pl.semaphore_wait(barrier, len(partners))


def all_partners(ctx, e, x, y, z):
    found = [{"exp": lax.rem(e + d, 8)} for d in range(1, 8)]
    found += [{"ctx": ctx_of(wrap4(x + d), y, z)} for d in (1, -1)]
    found += [{"ctx": ctx_of(x, wrap4(y + d), z)} for d in (1, -1)]
    found += [{"ctx": ctx_of(x, y, 1 - z)}]
    return found


def remote(src, dst, send, recv, place):
    return pltpu.make_async_remote_copy(
        src_ref=src, dst_ref=dst, send_sem=send, recv_sem=recv,
        device_id=place, device_id_type=MESH,
    )


class RingSum:
    def __init__(self, index, right, left, part, slots, send, recv, base, add):
        self.i, self.part, self.slots, self.add = index, part, slots, add
        i = index
        plan = [
            (part(wrap4(i + 2), 0), right),
            (part(wrap4(i + 2), 1), left),
            (part(wrap4(i + 1), 1), right),
            (part(wrap4(i - 1), 0), left),
            (part(wrap4(i + 1), 0), right),
            (part(wrap4(i - 1), 1), left),
        ]
        self.copies = [
            remote(src, slots.at[n], send.at[base + n], recv.at[base + n], place)
            for n, (src, place) in enumerate(plan)
        ]

    def start(self, *chosen):
        for n in chosen or range(4):
            self.copies[n].start()

    def middle(self):
        i = self.i
        self.copies[0].wait_recv()
        self.add(self.part(wrap4(i + 1), 0), [self.slots.at[0]])
        self.copies[4].start()
        self.copies[1].wait_recv()
        self.add(self.part(wrap4(i - 1), 1), [self.slots.at[1]])
        self.copies[5].start()

    def finish(self):
        i = self.i
        self.copies[3].wait_recv()
        self.copies[4].wait_recv()
        self.add(self.part(i, 0), [self.slots.at[3], self.slots.at[4]])
        self.copies[2].wait_recv()
        self.copies[5].wait_recv()
        self.add(self.part(i, 1), [self.slots.at[2], self.slots.at[5]])

    def drain(self):
        for copy in self.copies:
            copy.wait_send()


def add_rows(target, others):
    total = target[...].astype(jnp.float32)
    for other in others:
        total = total + other[...].astype(jnp.float32)
    target[...] = total.astype(jnp.bfloat16)


def add_blocks(target, others):
    def one(k, _):
        a, b = k // 2, lax.rem(k, 2)
        add_rows(target.at[a, b], [o.at[a, b] for o in others])
        return 0

    lax.fori_loop(0, 4, one, 0)


class RingGather:
    def __init__(self, index, right, left, part, send, recv, base):
        i = index
        plan = [
            (part(i, None), right),
            (part(i, None), left),
            (part(wrap4(i - 1), 0), right),
            (part(wrap4(i + 1), 1), left),
        ]
        self.copies = [
            remote(src, src, send.at[base + n], recv.at[base + n], place)
            for n, (src, place) in enumerate(plan)
        ]

    def start(self):
        self.copies[0].start()
        self.copies[1].start()

    def middle(self):
        self.copies[0].wait_recv()
        self.copies[2].start()
        self.copies[1].wait_recv()
        self.copies[3].start()

    def finish(self):
        self.copies[2].wait_recv()
        self.copies[3].wait_recv()

    def drain(self):
        for copy in self.copies:
            copy.wait_send()


def layer_kernel(
    q_in, k_in, v_in, o_in, gain_in, ids_in, weights_in, gate_in, up_in, down_in, grad_in,
    layer_to, hidden_grad_to, gg_out, gu_out, gd_out,
    qs, kv, w, best, tot, acc, att, part_f, part_b, got,
    sel, sel_t, hidden_s, rows_s, grads_s, inv_s, inv_r, xr, cr, wg, wu, wd,
    act_g, act_u, act_b, act, act_back, xt, ct, grad, res, back, res_r, back_r,
    slots1_wide, slots1_slim, slots2_wide, slots2_slim, slot3_wide, slot3_slim,
    lsem, q_send, q_recv, w_send, w_recv, z_send, z_recv, g_send, g_recv, s_send, s_recv,
    a2a_local, a2a_send, a2a_recv, r_local, r_send, r_recv, rs_send, rs_recv,
    layer_out, hidden_grad_out, out_sem,
):
    ctx, e, x, y, z = mesh_place()
    f32, bf = jnp.float32, jnp.bfloat16
    seq, core = e // 2, lax.rem(e, 2)
    group, slot = e // 4, lax.rem(e, 4)
    head_cols = pl.ds(pl.multiple_of(core * HEAD_SIZE, HEAD_SIZE), HEAD_SIZE)
    own_k = pltpu.make_async_copy(k_in.at[seq, :, head_cols], kv.at[x, y, z, 0], lsem.at[0])
    own_v = pltpu.make_async_copy(v_in.at[seq, :, head_cols], kv.at[x, y, z, 1], lsem.at[1])
    own_k.start()
    own_v.start()
    weight_copies = [
        pltpu.make_async_copy(src, dst, lsem.at[2 + n])
        for n, (src, dst) in enumerate(((gate_in, wg), (up_in, wu), (down_in, wd)))
    ]
    greet(all_partners(ctx, e, x, y, z))

    x_right, x_left = {"ctx": ctx_of(wrap4(x + 1), y, z)}, {"ctx": ctx_of(wrap4(x - 1), y, z)}
    y_right, y_left = {"ctx": ctx_of(x, wrap4(y + 1), z)}, {"ctx": ctx_of(x, wrap4(y - 1), z)}

    def ring_x(base, part):
        return RingGather(x, x_right, x_left, part, g_send, g_recv, base)

    def ring_y(base, part):
        return RingGather(y, y_right, y_left, part, g_send, g_recv, base)

    def two(h):
        return slice(None) if h is None else pl.ds(2 * h, 2)

    kv_a1 = ring_x(0, lambda i, h: kv.at[i, y, 0] if h is None else kv.at[i, y, 0, h])
    kv_b1 = ring_y(4, lambda i, h: kv.at[x, i, 1] if h is None else kv.at[x, i, 1, h])
    kv_a2 = ring_y(8, lambda i, h: kv.at[two(h), i, 0])
    kv_b2 = ring_x(12, lambda i, h: kv.at[i, two(h), 1])
    w_rings = []
    for c in range(2):
        cw = w.at[c]
        w_rings.append((
            ring_x(16 + 16 * c, lambda i, h, cw=cw: (
                cw.at[pl.ds(0, 2), i, y] if h is None else cw.at[h, i, y])),
            ring_y(20 + 16 * c, lambda i, h, cw=cw: (
                cw.at[pl.ds(2, 2), x, i] if h is None else cw.at[2 + h, x, i])),
            ring_y(24 + 16 * c, lambda i, h, cw=cw: (
                cw.at[pl.ds(0, 2), :, i] if h is None else cw.at[h, :, i])),
            ring_x(28 + 16 * c, lambda i, h, cw=cw: (
                cw.at[pl.ds(2, 2), i] if h is None else cw.at[2 + h, i])),
        ))
    z_partner = {"ctx": ctx_of(x, y, 1 - z)}
    z_copy = remote(kv.at[x, y, z], kv.at[x, y, z], z_send, z_recv, z_partner)

    own_k.wait()
    own_v.wait()
    z_copy.start()

    @pl.when(z == 0)
    def _():
        kv_a1.start()

    @pl.when(z == 1)
    def _():
        kv_b1.start()

    piece = pl.ds(pl.multiple_of((x * 4 + y) * 16, 16), 16)
    scatters = []
    for d in range(4):
        to = {"exp": 2 * lax.rem(seq + d, 4) + group}
        sends = [
            remote(
                o_in.at[piece, pl.ds(c * 1024, 1024)], w.at[c, slot, x, y],
                w_send.at[c, d], w_recv.at[c, slot], to,
            )
            for c in range(2)
        ]
        sends.append(remote(
            q_in.at[lax.rem(seq + d, 4)], qs.at[slot], q_send.at[d], q_recv.at[slot], to
        ))
        scatters.append(sends)
    mine = core == group
    own_pieces = [
        pltpu.make_async_copy(
            o_in.at[piece, pl.ds(c * 1024, 1024)], w.at[c, slot, x, y], w_recv.at[c, slot]
        )
        for c in range(2)
    ]
    own_pieces.append(pltpu.make_async_copy(q_in.at[seq], qs.at[slot], q_recv.at[slot]))
    for n in (2, 0, 1):
        @pl.when(mine)
        def _():
            own_pieces[n].start()

        @pl.when(jnp.logical_not(mine))
        def _():
            scatters[0][n].start()

        for d in range(1, 4):
            scatters[d][n].start()
    for copy in weight_copies:
        copy.start()

    z_copy.wait_recv()

    @pl.when(z == 0)
    def _():
        kv_b1.start()

    @pl.when(z == 1)
    def _():
        kv_a1.start()

    def exchange(src, dst, number):
        own = pltpu.make_async_copy(src.at[e], dst.at[e], a2a_local.at[number])
        out = []
        for d in range(1, 8):
            to = lax.rem(e + d, 8)
            out.append(remote(
                src.at[to], dst.at[e],
                a2a_send.at[number, d], a2a_recv.at[number, d], {"exp": to},
            ))
        return own, out

    def begin(pair):
        own, out = pair
        for copy in out:
            copy.start()
        own.start()

    def arrive(pair):
        own, out = pair
        own.wait()
        for copy in out:
            copy.wait_recv()

    grads_x = exchange(grads_s, cr, 1)
    res_x = exchange(res, res_r, 2)
    back_x = exchange(back, back_r, 3)

    ids = ids_in[...]
    chosen = (lax.broadcasted_iota(jnp.int32, (16, TOK), 0) == ids).astype(f32)
    rows_at = lax.broadcasted_iota(jnp.int32, (TOK, TOK), 0)
    lanes_at = lax.broadcasted_iota(jnp.int32, (TOK, TOK), 1)
    before = (rows_at < lanes_at).astype(bf)
    earlier = jnp.dot(chosen.astype(bf), before, preferred_element_type=f32)
    place = ids.astype(f32) * CAP + jnp.sum(earlier * chosen, axis=0, keepdims=True)
    slot_at = lax.broadcasted_iota(jnp.int32, (SLOTS, TOK), 0).astype(f32)
    taken = (slot_at == place).astype(f32)
    sel[...] = taken.astype(bf)
    sel_t[...] = taken.T.astype(bf)
    gates = jnp.sum(jnp.where(rows_at == lanes_at, weights_in[...], 0.0), axis=1, keepdims=True)

    def dispatch(dst, value, first):
        width = value.shape[1]
        dst[:, :, first:first + width] = jnp.dot(
            sel[...], value, preferred_element_type=f32
        ).astype(bf).reshape(8, CAP, width)

    kv_a1.middle()
    kv_b1.middle()
    kv_a1.finish()
    kv_a2.start()
    kv_b1.finish()
    kv_b2.start()
    for c in range(2):
        for j in range(4):
            pltpu.make_async_copy(w.at[c, j, x, y], w.at[c, j, x, y], w_recv.at[c, j]).wait()
        for ring in w_rings[c][:2]:
            ring.start()
    for n in range(8):
        cols = slice(n * 256, (n + 1) * 256)
        dispatch(grads_s, (grad_in[:, cols].astype(f32) * gates).astype(bf), n * 256)
    for c in range(2):
        for ring in w_rings[c][:2]:
            ring.middle()
    for ring in w_rings[0][:2]:
        ring.finish()
    for ring in w_rings[0][2:]:
        ring.start()
    for j in range(4):
        pltpu.make_async_copy(qs.at[j], qs.at[j], q_recv.at[j]).wait()
    begin(grads_x)

    scale = math.log2(math.e) / math.sqrt(HEAD_SIZE)
    over_last = (((1,), (1,)), ((), ()))

    def head_scores(h, key):
        t = h % 2
        query = qs[h // 2, :, t * HEAD_SIZE:(t + 1) * HEAD_SIZE]
        return lax.dot_general(query, key, over_last, preferred_element_type=f32) * scale

    def with_ones(value):
        return jnp.concatenate([value, jnp.ones(value.shape, bf)], axis=1)

    key, value = kv[x, y, z, 0], with_ones(kv[x, y, z, 1])
    below = lax.broadcasted_iota(jnp.int32, (256, 256), 1) <= lax.broadcasted_iota(
        jnp.int32, (256, 256), 0
    )
    for h in range(8):
        scores = jnp.where(below, head_scores(h, key), masked_score)
        top = jnp.max(scores, axis=1, keepdims=True)
        blended = jnp.dot(jnp.exp2(scores - top).astype(bf), value, preferred_element_type=f32)
        best[h] = jnp.broadcast_to(top, (256, HEAD_SIZE))
        acc[h] = blended[:, :HEAD_SIZE]
        tot[h] = blended[:, HEAD_SIZE:]

    def fold(places):
        key = jnp.concatenate([kv[bx, by, bz, 0] for bx, by, bz in places], axis=0)
        value = with_ones(jnp.concatenate([kv[bx, by, bz, 1] for bx, by, bz in places], axis=0))
        for h in range(8):
            scores = head_scores(h, key)
            old = best[h]
            new = jnp.maximum(old, jnp.max(scores, axis=1, keepdims=True))
            weights = jnp.exp2(scores - jnp.concatenate([new] * (2 * len(places)), axis=1))
            factor = jnp.exp2(old - new)
            blended = jnp.dot(weights.astype(bf), value, preferred_element_type=f32)
            best[h] = new
            acc[h] = acc[h] * factor + blended[:, :HEAD_SIZE]
            tot[h] = tot[h] * factor + blended[:, HEAD_SIZE:]

    def four(g):
        even = lax.rem(g, 2) == 0
        k = g // 2
        off = jnp.where(k == 2, -1, jnp.where(k == 3, 2, k))
        line = jnp.where(even, wrap4(y + off), wrap4(x + off))

        def at(i):
            return jnp.where(even, i, line), jnp.where(even, line, i), jnp.where(even, 0, 1)

        whole = ctx_of(*at(3)) < ctx

        @pl.when(whole)
        def _():
            fold([at(i) for i in range(4)])

        @pl.when(jnp.logical_not(whole))
        def _():
            def one(i, _):
                bx, by, bz = at(i)

                @pl.when(ctx_of(bx, by, bz) < ctx)
                def _():
                    fold([(bx, by, bz)])

                return 0

            lax.fori_loop(0, 4, one, 0)

    def line(g, _):
        @pl.when(g == 2)
        def _():
            kv_a2.middle()
            kv_b2.middle()

        @pl.when(g == 4)
        def _():
            for ring in w_rings[0][2:]:
                ring.middle()
            for ring in w_rings[1][:2]:
                ring.finish()
            for ring in w_rings[1][2:]:
                ring.start()

        @pl.when(g == 6)
        def _():
            kv_a2.finish()
            kv_b2.finish()

        four(g)
        return 0

    lax.fori_loop(0, 8, line, 0)

    for h in range(8):
        att[:, :, h * HEAD_SIZE:(h + 1) * HEAD_SIZE] = (
            (acc[h] / tot[h]).astype(bf).reshape(2, 128, HEAD_SIZE)
        )

    sibling = {"exp": e + 1 - 2 * core}
    halves, row_copies = [], []
    for n in range(4):
        cols = pl.ds(n * 512, 512)
        halves.append(remote(
            part_b.at[:, cols], got.at[:, cols], s_send.at[n], s_recv.at[n], sibling
        ))
        own_rows = pltpu.make_async_copy(
            rows_s.at[e, :, cols], xr.at[e, :, cols], r_local.at[n]
        )
        out = []
        for d in range(1, 8):
            to = lax.rem(e + d, 8)
            out.append(remote(
                rows_s.at[to, :, cols], xr.at[e, :, cols],
                r_send.at[n, d], r_recv.at[n, d], {"exp": to},
            ))
        row_copies.append((own_rows, out))

    def project(rows, first):
        return jnp.dot(
            rows, w[first // 1024, :, :, :, :, first % 1024:first % 1024 + 256].reshape(1024, 256),
            preferred_element_type=f32,
        )

    squares = jnp.zeros((TOK, 1), f32)
    for c in range(2):
        for ring in w_rings[c][2:]:
            if c == 1:
                ring.middle()
        for ring in w_rings[c][2:]:
            ring.finish()
        for n in (2 * c, 2 * c + 1):
            for first in (n * 512, n * 512 + 256):
                part_b[:, first:first + 256] = project(att[1 - core], first).astype(bf)
            halves[n].start()
        for n in (2 * c, 2 * c + 1):
            cols = slice(n * 512, (n + 1) * 512)
            for first in (n * 512, n * 512 + 256):
                part_f[:, first:first + 256] = project(att[core], first)
            halves[n].wait_recv()
            hidden = (part_f[:, cols] + got[:, cols].astype(f32)).astype(bf)
            hidden_s[:, cols] = hidden
            hidden = hidden.astype(f32)
            squares = squares + jnp.sum(hidden * hidden, axis=1, keepdims=True)
            dispatch(rows_s, (hidden * gain_in[:, cols]).astype(bf), n * 512)
            begin(row_copies[n])
    inv_rms = lax.rsqrt(squares * (1.0 / DM) + epsilon)
    inv_row = jnp.broadcast_to(inv_rms, (TOK, TOK)).T[0:1, :]
    inv_slots = jnp.sum(sel[...].astype(f32) * inv_row, axis=1, keepdims=True)
    inv_s[...] = jnp.broadcast_to(inv_slots, (SLOTS, 128)).reshape(8, CAP, 128)
    inv_x = exchange(inv_s, inv_r, 0)
    begin(inv_x)

    for copy in weight_copies:
        copy.wait()
    arrive(grads_x)
    cot = cr[...].reshape(SLOTS, DM)
    ct[...] = cot.T
    for n in range(3):
        cols = slice(n * 256, (n + 1) * 256)
        act_b[:, cols] = lax.dot_general(cot, wd[cols, :], over_last, preferred_element_type=f32)

    for c in range(2):
        for pair in row_copies[2 * c:2 * c + 2]:
            arrive(pair)
        part = slice(c * 1024, (c + 1) * 1024)
        rows = xr[:, :, part].reshape(SLOTS, 1024)
        for n in range(3):
            cols = slice(n * 256, (n + 1) * 256)
            gate_part = jnp.dot(rows, wg[part, cols], preferred_element_type=f32)
            up_part = jnp.dot(rows, wu[part, cols], preferred_element_type=f32)
            if c == 0:
                act_g[:, cols] = gate_part
                act_u[:, cols] = up_part
            else:
                act_g[:, cols] = act_g[:, cols] + gate_part
                act_u[:, cols] = act_u[:, cols] + up_part
        xt[part, :] = rows.T
    arrive(inv_x)
    inv_in = inv_r[...].reshape(SLOTS, 128)[:, 0:1]
    for n in range(3):
        cols = slice(n * 256, (n + 1) * 256)
        gate_act, up_act = act_g[:, cols] * inv_in, act_u[:, cols] * inv_in
        back_units = act_b[:, cols]
        sigma = jax.nn.sigmoid(gate_act)
        gated = gate_act * sigma
        act[:, 1536 + n * 256:1536 + (n + 1) * 256] = (gated * up_act).astype(bf)
        back_gate = back_units * up_act * sigma * (1.0 + gate_act * (1.0 - sigma))
        back_up = back_units * gated
        act[:, cols] = (back_gate * inv_in).astype(bf)
        act[:, 768 + n * 256:768 + (n + 1) * 256] = (back_up * inv_in).astype(bf)
        act_back[:, cols] = back_gate.astype(bf)
        act_back[:, 768 + n * 256:768 + (n + 1) * 256] = back_up.astype(bf)

    chains = []
    for c, (first, width) in enumerate(CHAINS):
        cols = pl.ds(first, width)
        wide = c < 2
        slots1 = (slots1_wide if wide else slots1_slim).at[c % 2]
        slots2 = (slots2_wide if wide else slots2_slim).at[c % 2]
        slot3 = (slot3_wide if wide else slot3_slim).at[c % 2]
        base = 13 * c
        if c % 2 == 0:
            one = RingSum(
                x, x_right, x_left, lambda i, h, cols=cols: grad.at[i, pl.ds(2 * h, 2), :, :, cols],
                slots1, rs_send, rs_recv, base, add_blocks)
            second = RingSum(
                y, y_right, y_left, lambda i, h, cols=cols: grad.at[x, i, h, :, cols],
                slots2, rs_send, rs_recv, base + 6, add_rows)
        else:
            one = RingSum(
                y, y_right, y_left, lambda i, h, cols=cols: grad.at[pl.ds(2 * h, 2), i, :, :, cols],
                slots1, rs_send, rs_recv, base, add_blocks)
            second = RingSum(
                x, x_right, x_left, lambda i, h, cols=cols: grad.at[i, y, h, :, cols],
                slots2, rs_send, rs_recv, base + 6, add_rows)
        last = remote(
            grad.at[x, y, 1 - z, :, cols], slot3,
            rs_send.at[base + 12], rs_recv.at[base + 12], z_partner,
        )
        chains.append((one, second, last, slot3))

    def weight_grads(step):
        px, py = wrap4(x + step), wrap4(y + step)
        for k in range(2):
            some = pl.ds(pl.multiple_of(px * 512 + k * 256, 256), 256)
            grad[px, 2 * k:2 * k + 2, :, :, 0:1152] = jnp.dot(
                xt[some, :], act[:, 0:1152], preferred_element_type=f32
            ).astype(bf).reshape(2, 2, 64, 1152)
        for k in range(4):
            some = pl.ds(pl.multiple_of(k * 512 + py * 128, 128), 128)
            grad[k, py, :, :, 1152:1536] = jnp.dot(
                xt[some, :], act[:, 1152:1536], preferred_element_type=f32
            ).astype(bf).reshape(2, 64, 384)
            grad[k, py, :, :, 1536:2304] = jnp.dot(
                ct[some, :], act[:, 1536:2304], preferred_element_type=f32
            ).astype(bf).reshape(2, 64, 768)

    def launch(*chosen):
        for chain in chains:
            chain[0].start(*chosen)

    weight_grads(2)
    launch(0, 1)
    for n in range(8):
        cols = slice(n * 256, (n + 1) * 256)
        res[:, :, cols] = jnp.dot(
            act[:, 1536:], wd[:, cols], preferred_element_type=f32
        ).astype(bf).reshape(8, CAP, 256)
    begin(res_x)
    weight_grads(1)
    launch(2)
    weight_grads(-1)
    launch(3)
    weight_grads(0)
    for n in range(8):
        cols = slice(n * 256, (n + 1) * 256)
        back[:, :, cols] = (
            lax.dot_general(act_back[:, 0:768], wg[cols, :], over_last, preferred_element_type=f32)
            + lax.dot_general(act_back[:, 768:1536], wu[cols, :], over_last, preferred_element_type=f32)
        ).astype(bf).reshape(8, CAP, 256)
    begin(back_x)

    for chain in chains:
        chain[0].middle()
    for chain in chains:
        chain[0].finish()
        chain[1].start()

    for chain in chains:
        chain[1].middle()
    for chain in chains:
        chain[1].finish()
        chain[2].start()

    arrive(res_x)
    returned = res_r[...].reshape(SLOTS, DM)
    for n in range(8):
        cols = slice(n * 256, (n + 1) * 256)
        expert_sum = gates * jnp.dot(sel_t[...], returned[:, cols], preferred_element_type=f32)
        layer_out[:, cols] = (hidden_s[:, cols].astype(f32) + expert_sum).astype(bf)

    layer_copy = pltpu.make_async_copy(layer_out, layer_to, out_sem.at[0])
    layer_copy.start()
    arrive(back_x)
    returned = back_r[...].reshape(SLOTS, DM)
    shared = jnp.zeros((TOK, 1), f32)
    for n in range(8):
        cols = slice(n * 256, (n + 1) * 256)
        scaled = gain_in[:, cols] * jnp.dot(
            sel_t[...], returned[:, cols], preferred_element_type=f32
        )
        part_f[:, cols] = scaled
        unit = hidden_s[:, cols].astype(f32) * inv_rms
        shared = shared + jnp.sum(scaled * unit, axis=1, keepdims=True)
    shared = shared * (1.0 / DM)
    for n in range(8):
        cols = slice(n * 256, (n + 1) * 256)
        unit = hidden_s[:, cols].astype(f32) * inv_rms
        hidden_grad_out[:, cols] = (
            grad_in[:, cols].astype(f32) + inv_rms * (part_f[:, cols] - unit * shared)
        ).astype(bf)

    hidden_copy = pltpu.make_async_copy(hidden_grad_out, hidden_grad_to, out_sem.at[1])
    hidden_copy.start()
    for (first, width), (_, _, last, slot3) in zip(CHAINS, chains):
        cols = slice(first, first + width)
        last.wait_recv()
        part_f[0:64, cols.start % 1152:cols.start % 1152 + width] = (
            grad[x, y, z, :, cols].astype(f32) + slot3[...].astype(f32)
        )
        if first == 0:
            gg_out[:, 0:640] = part_f[0:64, 0:640]
        elif first == 640:
            gg_out[:, 640:768] = part_f[0:64, 640:768]
            gu_out[:, 0:384] = part_f[0:64, 768:1152]
        elif first == 1152:
            gu_out[:, 384:768] = part_f[0:64, 0:384]
            gd_out[:, 0:256] = part_f[0:64, 384:640]
        else:
            gd_out[:, 256:768] = part_f[0:64, 640:1152]

    layer_copy.wait()
    hidden_copy.wait()
    for half in halves:
        half.wait_send()
    z_copy.wait_send()
    for ring in [kv_a1, kv_b1, kv_a2, kv_b2] + list(w_rings[0]) + list(w_rings[1]):
        ring.drain()
    for n in range(3):
        @pl.when(jnp.logical_not(mine))
        def _():
            scatters[0][n].wait_send()

        for d in range(1, 4):
            scatters[d][n].wait_send()
    for one, second, last, _ in chains:
        one.drain()
        second.drain()
        last.wait_send()
    for pair in row_copies + [inv_x, grads_x, res_x, back_x]:
        for copy in pair[1]:
            copy.wait_send()


def hand_over(*refs):
    for src, dst in zip(refs[:5], refs[5:]):
        dst[...] = src[...]


def on_device(
    queries, rotated_key_heads, value_head_rows, out_proj, norm_gain, expert_ids,
    gate_weights, expert_gate, expert_up, expert_down, grad_out,
):
    bf, f32 = jnp.bfloat16, jnp.float32
    anywhere = pl.BlockSpec(memory_space=pl.ANY)
    vmem = pl.BlockSpec(memory_space=pltpu.VMEM)
    dma = pltpu.SemaphoreType.DMA
    rows = jax.ShapeDtypeStruct((TOK, DM), bf)
    shard = jax.ShapeDtypeStruct((64, F), f32)
    swapped = pltpu.VMEM((8, CAP, DM), bf)
    units = pltpu.VMEM((SLOTS, F), f32)
    state = pltpu.VMEM((8, 256, HEAD_SIZE), f32)
    layer, hidden_grad, gg, gu, gd = pl.pallas_call(
        layer_kernel,
        out_shape=(rows, rows, shard, shard, shard),
        in_specs=[anywhere] * 4 + [vmem] * 3 + [anywhere] * 3 + [vmem],
        out_specs=(anywhere,) * 2 + (vmem,) * 3,
        scratch_shapes=[
            pltpu.VMEM((4, 256, 256), bf),
            pltpu.VMEM((4, 4, 2, 2, 256, HEAD_SIZE), bf),
            pltpu.VMEM((2, 4, 4, 4, 16, 1024), bf),
            state, state, state,
            pltpu.VMEM((2, 128, 1024), bf),
            pltpu.VMEM((TOK, DM), f32),
            pltpu.VMEM((TOK, DM), bf),
            pltpu.VMEM((TOK, DM), bf),
            pltpu.VMEM((SLOTS, TOK), bf),
            pltpu.VMEM((TOK, SLOTS), bf),
            pltpu.VMEM((TOK, DM), bf),
            swapped, swapped,
            pltpu.VMEM((8, CAP, 128), f32),
            pltpu.VMEM((8, CAP, 128), f32),
            swapped, swapped,
            pltpu.VMEM((DM, F), bf),
            pltpu.VMEM((DM, F), bf),
            pltpu.VMEM((F, DM), bf),
            units, units, units,
            pltpu.VMEM((SLOTS, 3 * F), bf),
            pltpu.VMEM((SLOTS, 2 * F), bf),
            pltpu.VMEM((DM, SLOTS), bf),
            pltpu.VMEM((DM, SLOTS), bf),
            pltpu.VMEM((4, 4, 2, 64, 3 * F), bf),
            swapped, swapped, swapped, swapped,
            pltpu.VMEM((2, 6, 2, 2, 64, 640), bf),
            pltpu.VMEM((2, 6, 2, 2, 64, 512), bf),
            pltpu.VMEM((2, 6, 64, 640), bf),
            pltpu.VMEM((2, 6, 64, 512), bf),
            pltpu.VMEM((2, 64, 640), bf),
            pltpu.VMEM((2, 64, 512), bf),
            dma((5,)), dma((4,)), dma((4,)), dma((2, 4)), dma((2, 4)),
            dma(()), dma(()), dma((48,)), dma((48,)), dma((4,)), dma((4,)),
            dma((4,)), dma((4, 8)), dma((4, 8)), dma((4,)), dma((4, 8)), dma((4, 8)),
            dma((52,)), dma((52,)),
            pltpu.VMEM((TOK, DM), bf), pltpu.VMEM((TOK, DM), bf), dma((2,)),
        ],
        compiler_params=pltpu.CompilerParams(
            collective_id=1, has_side_effects=True, vmem_limit_bytes=62 * 1024 * 1024
        ),
        name="layer",
    )(
        queries, rotated_key_heads, value_head_rows, out_proj, norm_gain[None],
        expert_ids.reshape(1, TOK), gate_weights.reshape(1, TOK), expert_gate[0], expert_up[0], expert_down[0], grad_out,
    )
    shapes = (rows, rows, shard, shard, shard)
    layer, hidden_grad, gg, gu, gd = pl.pallas_call(
        hand_over,
        out_shape=shapes,
        in_specs=[vmem] * 5,
        out_specs=[vmem] * 5,
        compiler_params=pltpu.CompilerParams(vmem_limit_bytes=62 * 1024 * 1024),
        name="hand_over",
    )(layer, hidden_grad, gg, gu, gd)
    return (layer, hidden_grad, gg[None], gu[None], gd.T[None])


def solution(mesh):
    in_specs = (
        P(None, "ctx", "exp"),
        P(None, "ctx", None),
        P(None, "ctx", None),
        P("exp", None),
        P(),
        P(("ctx", "exp"), None),
        P(("ctx", "exp"), None),
        P("exp", None, None),
        P("exp", None, None),
        P("exp", None, None),
        P(("ctx", "exp"), None),
    )
    out_specs = (
        P(("ctx", "exp"), None),
        P(("ctx", "exp"), None),
        P("exp", "ctx", None),
        P("exp", "ctx", None),
        P("exp", None, "ctx"),
    )
    return jax.shard_map(
        on_device, mesh=mesh, in_specs=in_specs, out_specs=out_specs, check_vma=False
    )
```
